512 devices in a mesh: train: 16 (over x_hi, y), target: 32 (over z, x_lo, core).
Axes of the slice: x: 4 (x_hi: 2, x_lo: 2; x = x_hi * 2 + x_lo), y: 8, z: 8, core: 2. Of those that a mesh axis runs over, the one named last changes fastest.
Arguments:
- train_embed: bfloat16 [16384, 256], P('train'), may hold values from -8 to 8
- train_label: int32 [16384], P('train'), may hold values from 0 to 7
- target_embed: bfloat16 [32768, 256], P('target'), may hold values from -8 to 8
- target_label: int32 [32768], P('target'), may hold values from 0 to 7
- label_cost: float32 [8, 8], replicated, may hold values from 0.1 to 1.5
Outputs:
- value: float32 [16384], P('train')
- target_potential: float32 [32768], P('target')
- barycentre: float32 [16384, 256], P(('train', 'target'))
The draws below stay inside these ranges and needn't reach their ends.
All inputs are finite; a program needn't handle non-finite values.
Results may differ from the reference program's by a relative error of at most 0.0033.
Values sent between devices are 32-bit elements; how exact they have to be, the bound alone decides.
No kernel may reach another device: no remote copies, remote signals or barrier semaphores. Data moves between devices by JAX's collectives and lax.ppermute only.
A program may use at most 128 MiB of HBM per device.

```python
import math
import jax
import jax.numpy as jnp
from jax import lax

D = 256
CLASSES = 8
ITERS = 2
TRAIN_ROWS = 16384
TARGET_ROWS = 32768


def shared_pairs(key):
    key = jax.random.fold_in(key, 99)
    first, second, third, fourth = jax.random.split(key, 4)
    signs = (jax.random.randint(first, (4, D), 0, 2) * 2 - 1).astype(jnp.float32)
    levels = jnp.array([6.0, 4.5, 3.2, 2.4], jnp.float32)[:, None]
    factor = jax.random.uniform(second, (4, 1), jnp.float32, 0.95, 1.05)
    vectors = signs * levels * factor
    train_rows = jax.random.permutation(third, TRAIN_ROWS)[:4]
    target_rows = jax.random.permutation(fourth, TARGET_ROWS)[:4]
    return (vectors, train_rows, target_rows)


def draw_train_embed(key, part):
    vectors, train_rows, target_rows = shared_pairs(key)
    key = jax.random.fold_in(key, 7)
    first, second = jax.random.split(key)
    base = jax.random.normal(first, (TRAIN_ROWS, D), jnp.float32)
    scale = jax.random.uniform(second, (TRAIN_ROWS, 1), jnp.float32, 0.8, 1.2)
    base = jnp.clip(base * scale, -8.0, 8.0)
    base = base.at[train_rows].set(vectors)
    return base.astype(jnp.bfloat16)


def draw_target_embed(key, part):
    vectors, train_rows, target_rows = shared_pairs(key)
    key = jax.random.fold_in(key, 11)
    base = jnp.clip(jax.random.normal(key, (TARGET_ROWS, D), jnp.float32), -6.0, 6.0)
    base = base.at[target_rows].set(vectors)
    return base.astype(jnp.bfloat16)


def plant(entries, own_key, least, largest):
    index_at = [jax.random.randint(jax.random.fold_in(own_key, axis), (), 0, length) for axis, length in enumerate(entries.shape)]
    main_axis = entries.shape.index(max(entries.shape))
    beside = index_at[:main_axis] + [(index_at[main_axis] + 1) % entries.shape[main_axis]] + index_at[main_axis + 1:]
    return entries.at[tuple(index_at)].set(least).at[tuple(beside)].set(largest)


def setup_inputs(seed: int = 0) -> dict:
    streams_of = jax.random.split(jax.random.key(seed), 6)
    return {
        "train_embed": draw_train_embed(jax.random.fold_in(streams_of[5], 71), 0),
        "train_label": plant(jax.random.randint(streams_of[1], (TRAIN_ROWS,), 0, CLASSES), jax.random.fold_in(streams_of[1], 1), 0, CLASSES - 1).astype(jnp.int32),
        "target_embed": draw_target_embed(jax.random.fold_in(streams_of[5], 71), 0),
        "target_label": plant(jax.random.randint(streams_of[3], (TARGET_ROWS,), 0, CLASSES), jax.random.fold_in(streams_of[3], 1), 0, CLASSES - 1).astype(jnp.int32),
        "label_cost": jnp.clip(jax.random.uniform(streams_of[4], (CLASSES, CLASSES), jnp.float32, 0.1, 1.5), 0.1, 1.5),
    }


EPS = 0.05


def cost_block(rows, row_label, cols, col_label, label_cost):
    sq_rows = jnp.sum(jnp.square(rows.astype(jnp.float32)), 1)
    sq_cols = jnp.sum(jnp.square(cols.astype(jnp.float32)), 1)
    cross = jnp.dot(rows, cols.T, preferred_element_type=jnp.float32)
    dist = (sq_rows[:, None] + sq_cols[None, :] - 2.0 * cross) / D
    return dist + label_cost[row_label][:, col_label]


def reference(train_embed, train_label, target_embed, target_label, label_cost):
    rblock = math.gcd(TRAIN_ROWS, 1024)
    nblock = TRAIN_ROWS // rblock
    row_blocks = train_embed.reshape(nblock, rblock, D)
    label_blocks = train_label.reshape(nblock, rblock)
    potential = jnp.zeros((TARGET_ROWS,), jnp.float32)
    dual = jnp.zeros((TRAIN_ROWS,), jnp.float32)
    for step in range(ITERS):
        def row_lse(args, potential=potential):
            rows, labels = args
            score = (potential[None, :] - cost_block(rows, labels, target_embed, target_label, label_cost)) / EPS
            peak = jnp.max(score, 1)
            return peak + jnp.log(jnp.sum(jnp.exp(score - peak[:, None]), 1))

        lse = lax.map(row_lse, (row_blocks, label_blocks)).reshape(-1)
        dual = EPS * (-math.log(TRAIN_ROWS) - lse)
        dual_blocks = dual.reshape(nblock, rblock)

        def col_step(carry, args):
            col_max, col_sum = carry
            rows, labels, part = args
            score = (part[:, None] - cost_block(rows, labels, target_embed, target_label, label_cost)) / EPS
            new_max = jnp.maximum(col_max, jnp.max(score, 0))
            col_sum = col_sum * jnp.exp(col_max - new_max) + jnp.sum(jnp.exp(score - new_max[None, :]), 0)
            return (new_max, col_sum), None

        start = (jnp.full((TARGET_ROWS,), -1e30, jnp.float32), jnp.zeros((TARGET_ROWS,), jnp.float32))
        (col_max, col_sum), unused = lax.scan(col_step, start, (row_blocks, label_blocks, dual_blocks))
        potential = EPS * (-math.log(TARGET_ROWS) - (col_max + jnp.log(col_sum)))

    def project(args):
        rows, labels = args
        score = (potential[None, :] - cost_block(rows, labels, target_embed, target_label, label_cost)) / EPS
        peak = jnp.max(score, 1)
        weights = jnp.exp(score - peak[:, None])
        numer = jnp.dot(weights.astype(jnp.bfloat16), target_embed, preferred_element_type=jnp.float32)
        denom = jnp.sum(weights, 1)
        return numer / denom[:, None]

    barycentre = lax.map(project, (row_blocks, label_blocks)).reshape(TRAIN_ROWS, D)
    total = jnp.sum(dual)
    value = dual - (total - dual) / (TRAIN_ROWS - 1)
    return value, potential, barycentre
```

```python
import functools
import math

import jax
import jax.numpy as jnp
from jax import lax
from jax.experimental import pallas as pl
from jax.experimental.pallas import tpu as pltpu
from jax.sharding import PartitionSpec as P

EPS = 0.05
SCALE = 128.0
KAPPA = math.log2(math.e) / EPS / SCALE
LANES = 256
CHUNK = 40


def pieces(v):
    hi = v.astype(jnp.bfloat16).astype(jnp.float32)
    rest = v - hi
    mid = rest.astype(jnp.bfloat16).astype(jnp.float32)
    lo = (rest - mid).astype(jnp.bfloat16).astype(jnp.float32)
    return hi, mid, lo


def tail(first, second):
    n = first[0].shape[1]
    row = lax.broadcasted_iota(jnp.int32, (8, n), 0)
    out = jnp.zeros((8, n), jnp.float32)
    for k, v in enumerate(first + second):
        out = jnp.where(row == k, v, out)
    return out


def ones_like3(v):
    return (jnp.ones_like(v),) * 3


def train_rows(label, phi):
    m = label.shape[1]
    onehot = (lax.broadcasted_iota(jnp.int32, (8, m), 0) == label).astype(jnp.float32)
    last = tail(ones_like3(phi), pieces(phi * SCALE))
    return jnp.concatenate([onehot, onehot, onehot, last], axis=0)


def target_rows(label, gamma, label_cost):
    n = label.shape[1]
    table = jnp.zeros((8, n), jnp.float32)
    for b in range(8):
        table = jnp.where(label == b, label_cost[:, b : b + 1], table)
    last = tail(pieces(gamma * SCALE), ones_like3(gamma))
    return jnp.concatenate(list(pieces(table * -SCALE)) + [last], axis=0)


def as_columns(rows):
    pad = jnp.zeros((96, rows.shape[1]), jnp.float32)
    return jnp.concatenate([rows, pad], axis=0).T.astype(jnp.bfloat16)


def as_rows(rows):
    pad = jnp.zeros((96, rows.shape[1]), jnp.float32)
    return jnp.concatenate([rows, pad], axis=0).astype(jnp.bfloat16)


def dot_nt(a, b):
    return lax.dot_general(a, b, (((1,), (1,)), ((), ())), preferred_element_type=jnp.float32)


def dot_nn(a, b):
    return lax.dot_general(a, b, (((1,), (0,)), ((), ())), preferred_element_type=jnp.float32)


def square_sums(v):
    sq = jnp.square(v.astype(jnp.float32))
    hi = sq.astype(jnp.bfloat16)
    lo = (sq - hi.astype(jnp.float32)).astype(jnp.bfloat16)
    ones = jnp.ones((8, v.shape[1]), jnp.bfloat16)
    return (dot_nt(ones, hi) + dot_nt(ones, lo))[0:1] / v.shape[1]


def reduce_over_sub(sub, sub_columns, lane_ref, lane_rows, out_ref, shifted):
    n = lane_ref.shape[0]
    for k in range(n // LANES):
        at = pl.ds(k * LANES, LANES)
        t = dot_nt(sub, lane_ref[at, :]) + dot_nn(sub_columns, lane_rows[:, k * LANES : (k + 1) * LANES])
        if shifted:
            total = jnp.sum(jnp.exp2(t * KAPPA), axis=0, keepdims=True)
            out_ref[:, at] = total
        else:
            top = jnp.max(t, axis=0, keepdims=True)
            total = jnp.sum(jnp.exp2((t - top) * KAPPA), axis=0, keepdims=True)
            out_ref[:, at] = top * (1.0 / SCALE) + EPS * jnp.log(total)


def rows_first(x_ref, y_ref, lx_ref, ly_ref, lc_ref, out_ref, sqx_ref, sqy_ref):
    y = y_ref[...]
    sq = square_sums(y)
    sqy_ref[...] = sq
    sqx_ref[...] = square_sums(x_ref[...])
    columns = as_columns(target_rows(ly_ref[...], -sq, lc_ref[...]))
    rows = as_rows(train_rows(lx_ref[...], jnp.zeros_like(sq)))
    reduce_over_sub(y, columns, x_ref, rows, out_ref, False)


def columns_first(x_ref, y_ref, lx_ref, ly_ref, lc_ref, phi_ref, out_ref):
    phi = phi_ref[...]
    columns = as_columns(train_rows(lx_ref[...], phi))
    rows = as_rows(target_rows(ly_ref[...], jnp.zeros_like(phi), lc_ref[...]))
    reduce_over_sub(x_ref[...], columns, y_ref, rows, out_ref, False)


def rows_next(x_ref, y_ref, lx_ref, ly_ref, lc_ref, phi_ref, gamma_ref, out_ref):
    columns = as_columns(target_rows(ly_ref[...], gamma_ref[...], lc_ref[...]))
    rows = as_rows(train_rows(lx_ref[...], phi_ref[...]))
    reduce_over_sub(y_ref[...], columns, x_ref, rows, out_ref, True)


def columns_next(x_ref, y_ref, lx_ref, ly_ref, lc_ref, phi_ref, gamma_ref, sqx_ref, out_ref):
    n = y_ref.shape[0]
    phi = phi_ref[...]
    columns = as_columns(train_rows(lx_ref[...], phi))
    rows = as_rows(target_rows(ly_ref[...], gamma_ref[...], lc_ref[...]))
    reduce_over_sub(x_ref[...], columns, y_ref, rows, out_ref, True)
    dual_sum = jnp.sum(phi + sqx_ref[...], axis=1, keepdims=True)
    out_ref[:, n : n + 128] = jnp.broadcast_to(dual_sum, (1, 128))


def project(relative, x_ref, y_ref, lx_ref, ly_ref, lc_ref, phi_ref, gamma_ref, me_ref, out_ref, xs_ref, xa_ref, aug_ref):
    share = 32
    n = y_ref.shape[0]
    me = me_ref[0]
    aug_ref[...] = as_columns(train_rows(lx_ref[...], phi_ref[...])).astype(jnp.float32)
    rows = as_rows(target_rows(ly_ref[...], gamma_ref[...], lc_ref[...]))
    y = y_ref[...]
    for k, rel in enumerate(relative):
        start = pl.multiple_of((me ^ rel) * share, share)
        xs_ref[pl.ds(k * share, share), :] = x_ref[pl.ds(start, share), :]
        xa_ref[pl.ds(k * share, share), :] = aug_ref[pl.ds(start, share), :].astype(jnp.bfloat16)
    diagonal = lax.broadcasted_iota(jnp.int32, (share, 256), 0) == lax.broadcasted_iota(
        jnp.int32, (share, 256), 1
    )
    per = min(8, len(relative))
    block = per * share
    for b in range(len(relative) // per):
        at = pl.ds(b * block, block)
        t = dot_nt(xs_ref[at, :], y) + dot_nn(xa_ref[at, :], rows)
        w = jnp.exp2(t * KAPPA)
        denom = jnp.sum(w, axis=1, keepdims=True)
        numer = dot_nn(w.astype(jnp.bfloat16), y)
        for k in range(per):
            part = slice(k * share, (k + 1) * share)
            out_ref[b * per + k, 0:share, :] = numer[part]
            across = jnp.sum(jnp.where(diagonal, denom[part], 0.0), axis=0, keepdims=True)
            out_ref[b * per + k, share:CHUNK, :] = jnp.broadcast_to(across, (CHUNK - share, 256))


def finish(*refs):
    share = 32
    out_ref = refs[-1]
    total = refs[0][...]
    for ref in refs[1:-1]:
        total = total + ref[...]
    diagonal = lax.broadcasted_iota(jnp.int32, (share, 256), 0) == lax.broadcasted_iota(
        jnp.int32, (share, 256), 1
    )
    denom = jnp.sum(jnp.where(diagonal, total[share : share + 1], 0.0), axis=1, keepdims=True)
    out_ref[...] = total[0:share] / denom


def call(body, outs, scratch=(), smem=(), flops=0, n_in=0):
    vmem = pl.BlockSpec(memory_space=pltpu.VMEM)
    specs = [pl.BlockSpec(memory_space=pltpu.SMEM) if k in smem else vmem for k in range(n_in)]
    return pl.pallas_call(
        body,
        out_shape=[jax.ShapeDtypeStruct(s, jnp.float32) for s in outs],
        in_specs=specs,
        out_specs=[vmem for _ in outs],
        scratch_shapes=list(scratch),
        compiler_params=pltpu.CompilerParams(vmem_limit_bytes=40 * 2**20),
        cost_estimate=pl.CostEstimate(flops=flops, bytes_accessed=2**20, transcendentals=flops // 512),
    )


def swap(x, axis, bits):
    size = lax.axis_size(axis)
    return lax.ppermute(x, axis, [(t, t ^ bits) for t in range(size)])


def tree(parts, combine):
    while len(parts) > 1:
        parts = [combine(parts[k], parts[k + 1]) for k in range(0, len(parts), 2)]
    return parts[0]


def everyone(x, axis, partners):
    return [x if bits == 0 else swap(x, axis, bits) for bits in partners]


def add_all(parts):
    return tree(parts, jnp.add)


def lse_all(parts):
    top = tree(parts, jnp.maximum)
    total = tree([jnp.exp((part - top) * (1.0 / EPS)) for part in parts], jnp.add)
    return top + EPS * jnp.log(total)


def on_device(train_embed, train_label, target_embed, target_label, label_cost):
    m_dev, width = train_embed.shape
    n_dev = target_embed.shape[0]
    trains = lax.axis_size("train")
    targets = lax.axis_size("target")
    log_m = EPS * math.log(m_dev * trains)
    log_n = EPS * math.log(n_dev * targets)
    data = (
        train_embed,
        target_embed,
        train_label.reshape(1, m_dev),
        target_label.reshape(1, n_dev),
        label_cost,
    )
    row_m, row_n = (1, m_dev), (1, n_dev)
    near = list(range(4))
    far = list(range(0, targets, 4))
    flops = 2 * m_dev * n_dev * 512

    local, sqx, sqy = call(rows_first, [row_m, row_m, row_n], n_in=5, flops=flops)(*data)
    lse = lse_all(everyone(local, "target", near))
    lse = lse_all(everyone(lse, "target", far))
    phi = -log_m - lse

    (local,) = call(columns_first, [row_n], n_in=6, flops=flops)(*data, phi)
    lse = lse_all(everyone(local, "train", list(range(trains))))
    gamma = -log_n - lse

    base = phi + log_n
    (local,) = call(rows_next, [row_m], n_in=7, flops=flops)(*data, base, gamma)
    total = add_all(everyone(local, "target", list(range(targets))))
    phi = base - log_m - EPS * jnp.log(total)

    base = gamma + log_m
    (local,) = call(columns_next, [(1, n_dev + 128)], n_in=8, flops=flops)(*data, phi, base, sqx)
    half = trains // 2
    total = add_all(everyone(local, "train", [0, half]))
    total = add_all(everyone(total, "train", list(range(half))))
    gamma = base - log_n - EPS * jnp.log(total[:, :n_dev])
    dual = phi + sqx
    value = dual - (total[:, n_dev : n_dev + 1] - dual) / (m_dev * trains - 1)
    potential = gamma + sqy

    me = lax.axis_index("target").astype(jnp.int32).reshape(1)
    depth = targets // 4

    def part(relative):
        rows = 32 * len(relative)
        (out,) = call(
            functools.partial(project, relative),
            [(len(relative), CHUNK, width)],
            scratch=[
                pltpu.VMEM((rows, width), jnp.bfloat16),
                pltpu.VMEM((rows, 128), jnp.bfloat16),
                pltpu.VMEM((m_dev, 128), jnp.float32),
            ],
            smem=(7,),
            n_in=8,
            flops=flops,
        )(*data, phi + log_n, gamma, me)
        return out

    def order(core):
        return [core + 2 * x + 4 * z for x in (1, 0) for z in range(depth)]

    sent = swap(part(order(1)), "target", 1)
    kept = part(order(0))
    sent_next = swap(kept[:depth] + sent[:depth], "target", 2)
    kept = kept[depth:] + sent[depth:] + sent_next
    chunks = [kept[k] if k == 0 else swap(kept[k], "target", 4 * k) for k in range(depth)]
    (barycentre,) = call(finish, [(32, width)], n_in=depth)(*chunks)
    return (value.reshape(m_dev), potential.reshape(n_dev), barycentre)


def solution(mesh):
    return jax.shard_map(
        on_device,
        mesh=mesh,
        in_specs=(P("train", None), P("train"), P("target", None), P("target"), P()),
        out_specs=(P("train"), P("target"), P(("train", "target"), None)),
        check_vma=False,
    )
```

```python
import functools
import math

import jax
import jax.numpy as jnp
from jax import lax
from jax.experimental import pallas as pl
from jax.experimental.pallas import tpu as pltpu
from jax.sharding import PartitionSpec as P

EPS = 0.05
SCALE = 128.0
KAPPA = math.log2(math.e) / EPS / SCALE
LANES = 256
CHUNK = 40


def pieces(v):
    hi = v.astype(jnp.bfloat16).astype(jnp.float32)
    rest = v - hi
    mid = rest.astype(jnp.bfloat16).astype(jnp.float32)
    lo = (rest - mid).astype(jnp.bfloat16).astype(jnp.float32)
    return hi, mid, lo


def tail(first, second):
    n = first[0].shape[1]
    row = lax.broadcasted_iota(jnp.int32, (8, n), 0)
    out = jnp.zeros((8, n), jnp.float32)
    for k, v in enumerate(first + second):
        out = jnp.where(row == k, v, out)
    return out


def ones_like3(v):
    return (jnp.ones_like(v),) * 3


def train_rows(label, phi):
    m = label.shape[1]
    onehot = (lax.broadcasted_iota(jnp.int32, (8, m), 0) == label).astype(jnp.float32)
    last = tail(ones_like3(phi), pieces(phi * SCALE))
    return jnp.concatenate([onehot, onehot, onehot, last], axis=0)


def target_rows(label, gamma, label_cost):
    n = label.shape[1]
    table = jnp.zeros((8, n), jnp.float32)
    for b in range(8):
        table = jnp.where(label == b, label_cost[:, b : b + 1], table)
    last = tail(pieces(gamma * SCALE), ones_like3(gamma))
    return jnp.concatenate(list(pieces(table * -SCALE)) + [last], axis=0)


def as_columns(rows):
    pad = jnp.zeros((96, rows.shape[1]), jnp.float32)
    return jnp.concatenate([rows, pad], axis=0).T.astype(jnp.bfloat16)


def as_rows(rows):
    pad = jnp.zeros((96, rows.shape[1]), jnp.float32)
    return jnp.concatenate([rows, pad], axis=0).astype(jnp.bfloat16)


def dot_nt(a, b):
    return lax.dot_general(a, b, (((1,), (1,)), ((), ())), preferred_element_type=jnp.float32)


def dot_nn(a, b):
    return lax.dot_general(a, b, (((1,), (0,)), ((), ())), preferred_element_type=jnp.float32)


def square_sums(v):
    sq = jnp.square(v.astype(jnp.float32))
    hi = sq.astype(jnp.bfloat16)
    lo = (sq - hi.astype(jnp.float32)).astype(jnp.bfloat16)
    ones = jnp.ones((8, v.shape[1]), jnp.bfloat16)
    return (dot_nt(ones, hi) + dot_nt(ones, lo))[0:1] / v.shape[1]


def reduce_over_sub(sub, sub_columns, lane_ref, lane_rows, at_ref, shifted):
    n = lane_ref.shape[0]
    for k in range(n // LANES):
        at = pl.ds(k * LANES, LANES)
        t = dot_nt(sub, lane_ref[at, :]) + dot_nn(sub_columns, lane_rows[:, k * LANES : (k + 1) * LANES])
        if shifted:
            out = jnp.sum(jnp.exp2(t * KAPPA), axis=0, keepdims=True)
        else:
            top = jnp.max(t, axis=0, keepdims=True)
            total = jnp.sum(jnp.exp2((t - top) * KAPPA), axis=0, keepdims=True)
            out = top * (1.0 / SCALE) + EPS * jnp.log(total)
        for r in range(LANES // 128):
            row = k * (LANES // 128) + r
            at_ref[row : row + 1, :] = out[:, r * 128 : (r + 1) * 128]


def to_everyone(v, out_ref):
    for k in range(out_ref.shape[0]):
        out_ref[k] = v


def in_lanes(v):
    return jnp.concatenate([v[k : k + 1] for k in range(v.shape[0])], axis=1)


def tree(parts, combine):
    while len(parts) > 1:
        parts = [combine(parts[k], parts[k + 1]) for k in range(0, len(parts), 2)]
    return parts[0]


def lse_received(ref):
    parts = [ref[k] for k in range(ref.shape[0])]
    top = tree(parts, jnp.maximum)
    total = tree([jnp.exp((part - top) * (1.0 / EPS)) for part in parts], jnp.add)
    return in_lanes(top + EPS * jnp.log(total))


def sum_received(ref):
    return tree([ref[k] for k in range(ref.shape[0])], jnp.add)


def rows_first(x_ref, y_ref, lx_ref, ly_ref, lc_ref, out_ref, sqx_ref, sqy_ref, at_ref):
    y = y_ref[...]
    sq = square_sums(y)
    sqy_ref[...] = sq
    sqx_ref[...] = square_sums(x_ref[...])
    columns = as_columns(target_rows(ly_ref[...], -sq, lc_ref[...]))
    rows = as_rows(train_rows(lx_ref[...], jnp.zeros(lx_ref.shape, jnp.float32)))
    reduce_over_sub(y, columns, x_ref, rows, at_ref, False)
    to_everyone(at_ref[...], out_ref)


def columns_first(log_m, x_ref, y_ref, lx_ref, ly_ref, lc_ref, got_ref, out_ref, phi_ref, at_ref):
    phi = -log_m - lse_received(got_ref)
    phi_ref[...] = phi
    columns = as_columns(train_rows(lx_ref[...], phi))
    rows = as_rows(target_rows(ly_ref[...], jnp.zeros(ly_ref.shape, jnp.float32), lc_ref[...]))
    reduce_over_sub(x_ref[...], columns, y_ref, rows, at_ref, False)
    to_everyone(at_ref[...], out_ref)


def rows_next(log_n, x_ref, y_ref, lx_ref, ly_ref, lc_ref, phi_ref, got_ref, out_ref, gamma_ref, at_ref):
    gamma = -log_n - lse_received(got_ref)
    gamma_ref[...] = gamma
    columns = as_columns(target_rows(ly_ref[...], gamma, lc_ref[...]))
    rows = as_rows(train_rows(lx_ref[...], phi_ref[...] + log_n))
    reduce_over_sub(y_ref[...], columns, x_ref, rows, at_ref, True)
    to_everyone(at_ref[...], out_ref)


def columns_next(
    log_m, log_n, x_ref, y_ref, lx_ref, ly_ref, lc_ref, phi_ref, gamma_ref, sqx_ref, got_ref, out_ref, new_ref, at_ref
):
    r = at_ref.shape[0]
    phi = phi_ref[...] + log_n - log_m - EPS * jnp.log(in_lanes(sum_received(got_ref)))
    new_ref[...] = phi
    columns = as_columns(train_rows(lx_ref[...], phi))
    rows = as_rows(target_rows(ly_ref[...], gamma_ref[...] + log_m, lc_ref[...]))
    reduce_over_sub(x_ref[...], columns, y_ref, rows, at_ref, True)
    dual_sum = jnp.sum(phi + sqx_ref[...], axis=1, keepdims=True)
    local = at_ref[...]
    for k in range(out_ref.shape[0]):
        out_ref[k, 0:r, :] = local
        out_ref[k, r : 2 * r, :] = jnp.broadcast_to(dual_sum, (r, 128))


def potentials(log_m, log_n, others, phi_ref, gamma_ref, sqx_ref, sqy_ref, got_ref, new_ref, value_ref, potential_ref):
    total = sum_received(got_ref)
    r = total.shape[0] // 2
    gamma = gamma_ref[...] + log_m - log_n - EPS * jnp.log(in_lanes(total[0:r]))
    new_ref[...] = gamma
    potential_ref[...] = gamma + sqy_ref[...]
    dual = phi_ref[...] + sqx_ref[...]
    value_ref[...] = dual - (in_lanes(total[r : 2 * r]) - dual) / others


def weighted_sums(shift, relative, x_ref, y_ref, lx_ref, ly_ref, lc_ref, phi_ref, gamma_ref, me_ref, out_ref, xs_ref, xa_ref, aug_ref):
    share = 32
    me = me_ref[0]
    aug_ref[...] = as_columns(train_rows(lx_ref[...], phi_ref[...] + shift)).astype(jnp.float32)
    rows = as_rows(target_rows(ly_ref[...], gamma_ref[...], lc_ref[...]))
    y = y_ref[...]
    for k, rel in enumerate(relative):
        start = pl.multiple_of((me ^ rel) * share, share)
        xs_ref[pl.ds(k * share, share), :] = x_ref[pl.ds(start, share), :]
        xa_ref[pl.ds(k * share, share), :] = aug_ref[pl.ds(start, share), :].astype(jnp.bfloat16)
    diagonal = lax.broadcasted_iota(jnp.int32, (share, 256), 0) == lax.broadcasted_iota(
        jnp.int32, (share, 256), 1
    )
    per = min(8, len(relative))
    block = per * share
    for b in range(len(relative) // per):
        at = pl.ds(b * block, block)
        t = dot_nt(xs_ref[at, :], y) + dot_nn(xa_ref[at, :], rows)
        w = jnp.exp2(t * KAPPA).astype(jnp.bfloat16)
        denom = jnp.sum(w.astype(jnp.float32), axis=1, keepdims=True)
        numer = dot_nn(w, y)
        for k in range(per):
            part = slice(k * share, (k + 1) * share)
            out_ref[b * per + k, 0:share, :] = numer[part]
            across = jnp.sum(jnp.where(diagonal, denom[part], 0.0), axis=0, keepdims=True)
            out_ref[b * per + k, share:CHUNK, :] = jnp.broadcast_to(across, (CHUNK - share, 256))


def project_sent(
    log_m, log_n, others, relative,
    x_ref, y_ref, lx_ref, ly_ref, lc_ref, phi_ref, gamma_ref, sqx_ref, sqy_ref, got_ref, me_ref,
    out_ref, new_ref, value_ref, potential_ref, xs_ref, xa_ref, aug_ref,
):
    potentials(log_m, log_n, others, phi_ref, gamma_ref, sqx_ref, sqy_ref, got_ref, new_ref, value_ref, potential_ref)
    weighted_sums(log_n, relative, x_ref, y_ref, lx_ref, ly_ref, lc_ref, phi_ref, new_ref, me_ref, out_ref, xs_ref, xa_ref, aug_ref)


def finish(got_ref, out_ref):
    share = 32
    total = sum_received(got_ref)
    diagonal = lax.broadcasted_iota(jnp.int32, (share, 256), 0) == lax.broadcasted_iota(
        jnp.int32, (share, 256), 1
    )
    denom = jnp.sum(jnp.where(diagonal, total[share : share + 1], 0.0), axis=1, keepdims=True)
    out_ref[...] = total[0:share] / denom


def call(body, outs, scratch=(), smem=(), flops=0, n_in=0):
    vmem = pl.BlockSpec(memory_space=pltpu.VMEM)
    specs = [pl.BlockSpec(memory_space=pltpu.SMEM) if k in smem else vmem for k in range(n_in)]
    return pl.pallas_call(
        body,
        out_shape=[jax.ShapeDtypeStruct(s, jnp.float32) for s in outs],
        in_specs=specs,
        out_specs=[vmem for _ in outs],
        scratch_shapes=list(scratch),
        compiler_params=pltpu.CompilerParams(vmem_limit_bytes=40 * 2**20),
        cost_estimate=pl.CostEstimate(flops=flops, bytes_accessed=2**20, transcendentals=flops // 512),
    )


def exchange(x, axis, groups=None):
    return lax.all_to_all(x, axis, 0, 0, axis_index_groups=groups, tiled=True)


def on_device(train_embed, train_label, target_embed, target_label, label_cost):
    m_dev, width = train_embed.shape
    n_dev = target_embed.shape[0]
    trains = lax.axis_size("train")
    targets = lax.axis_size("target")
    log_m = EPS * math.log(m_dev * trains)
    log_n = EPS * math.log(n_dev * targets)
    data = (
        train_embed,
        target_embed,
        train_label.reshape(1, m_dev),
        target_label.reshape(1, n_dev),
        label_cost,
    )
    row_m, row_n = (1, m_dev), (1, n_dev)
    tile_m, tile_n = (m_dev // 128, 128), (n_dev // 128, 128)
    flops = 2 * m_dev * n_dev * 512

    def run(body, outs, tile, *args):
        return call(body, outs, scratch=[pltpu.VMEM(tile, jnp.float32)], n_in=len(args), flops=flops)(*args)

    local, sqx, sqy = run(rows_first, [(targets,) + tile_m, row_m, row_n], tile_m, *data)
    got = exchange(local, "target")
    local, phi = run(
        functools.partial(columns_first, log_m), [(trains,) + tile_n, row_m], tile_n, *data, got
    )
    got = exchange(local, "train")
    local, gamma = run(
        functools.partial(rows_next, log_n), [(targets,) + tile_m, row_n], tile_m, *data, phi, got
    )
    got = exchange(local, "target")
    local, phi = run(
        functools.partial(columns_next, log_m, log_n),
        [(trains, 2 * tile_n[0], 128), row_m],
        tile_n, *data, phi, gamma, sqx, got,
    )
    got = exchange(local, "train")

    me = lax.axis_index("target").astype(jnp.int32)
    core = (me & 1).reshape(1)
    half = targets // 2
    rows = 32 * half
    scratch = [
        pltpu.VMEM((rows, width), jnp.bfloat16),
        pltpu.VMEM((rows, 128), jnp.bfloat16),
        pltpu.VMEM((m_dev, 128), jnp.float32),
    ]
    chunks = (half, CHUNK, width)
    sent, gamma, value, potential = call(
        functools.partial(project_sent, log_m, log_n, m_dev * trains - 1, [2 * k + 1 for k in range(half)]),
        [chunks, row_n, row_m, row_n],
        scratch=scratch, smem=(10,), n_in=11, flops=flops,
    )(*data, phi, gamma, sqx, sqy, got, core)
    sent = lax.ppermute(sent, "target", [(t, t ^ 1) for t in range(targets)])
    (kept,) = call(
        functools.partial(weighted_sums, log_n, [2 * k for k in range(half)]),
        [chunks],
        scratch=scratch, smem=(7,), n_in=8, flops=flops,
    )(*data, phi, gamma, core)
    groups = [[c + 2 * k for k in range(half)] for c in range(2)]
    got = exchange(kept + sent, "target", groups)
    (barycentre,) = call(finish, [(32, width)], n_in=1)(got)
    return (value.reshape(m_dev), potential.reshape(n_dev), barycentre)


def solution(mesh):
    return jax.shard_map(
        on_device,
        mesh=mesh,
        in_specs=(P("train", None), P("train"), P("target", None), P("target"), P()),
        out_specs=(P("train"), P("target"), P(("train", "target"), None)),
        check_vma=False,
    )
```

```python
import functools
import math

import jax
import jax.numpy as jnp
from jax import lax
from jax.experimental import pallas as pl
from jax.experimental.pallas import tpu as pltpu
from jax.sharding import PartitionSpec as P

EPS = 0.05
SCALE = 128.0
KAPPA = math.log2(math.e) / EPS / SCALE
LANES = 256
SHARE = 32
CHUNK = 2 * SHARE + 8


def pieces(v):
    hi = v.astype(jnp.bfloat16).astype(jnp.float32)
    rest = v - hi
    mid = rest.astype(jnp.bfloat16).astype(jnp.float32)
    lo = (rest - mid).astype(jnp.bfloat16).astype(jnp.float32)
    return hi, mid, lo


def tail(first, second):
    n = first[0].shape[1]
    row = lax.broadcasted_iota(jnp.int32, (8, n), 0)
    out = jnp.zeros((8, n), jnp.float32)
    for k, v in enumerate(first + second):
        out = jnp.where(row == k, v, out)
    return out


def ones_like3(v):
    return (jnp.ones_like(v),) * 3


def train_rows(label, phi):
    m = label.shape[1]
    onehot = (lax.broadcasted_iota(jnp.int32, (8, m), 0) == label).astype(jnp.float32)
    last = tail(ones_like3(phi), pieces(phi * SCALE))
    return jnp.concatenate([onehot, onehot, onehot, last], axis=0)


def target_rows(label, gamma, label_cost):
    n = label.shape[1]
    table = jnp.zeros((8, n), jnp.float32)
    for b in range(8):
        table = jnp.where(label == b, label_cost[:, b : b + 1], table)
    last = tail(pieces(gamma * SCALE), ones_like3(gamma))
    return jnp.concatenate(list(pieces(table * -SCALE)) + [last], axis=0)


def as_columns(rows):
    pad = jnp.zeros((96, rows.shape[1]), jnp.float32)
    return jnp.concatenate([rows, pad], axis=0).T.astype(jnp.bfloat16)


def as_rows(rows):
    pad = jnp.zeros((96, rows.shape[1]), jnp.float32)
    return jnp.concatenate([rows, pad], axis=0).astype(jnp.bfloat16)


def dot_nt(a, b):
    return lax.dot_general(a, b, (((1,), (1,)), ((), ())), preferred_element_type=jnp.float32)


def dot_nn(a, b):
    return lax.dot_general(a, b, (((1,), (0,)), ((), ())), preferred_element_type=jnp.float32)


def square_sums(v):
    sq = jnp.square(v.astype(jnp.float32))
    hi = sq.astype(jnp.bfloat16)
    lo = (sq - hi.astype(jnp.float32)).astype(jnp.bfloat16)
    ones = jnp.ones((8, v.shape[1]), jnp.bfloat16)
    return (dot_nt(ones, hi) + dot_nt(ones, lo))[0:1] / v.shape[1]


def reduce_over_sub(sub, sub_columns, lane_ref, lane_rows, at_ref, shifted):
    n = lane_ref.shape[0]
    for k in range(n // LANES):
        at = pl.ds(k * LANES, LANES)
        t = dot_nt(sub, lane_ref[at, :]) + dot_nn(sub_columns, lane_rows[:, k * LANES : (k + 1) * LANES])
        if shifted:
            out = jnp.sum(jnp.exp2(t * KAPPA), axis=0, keepdims=True)
        else:
            top = jnp.max(t, axis=0, keepdims=True)
            total = jnp.sum(jnp.exp2((t - top) * KAPPA), axis=0, keepdims=True)
            out = top * (1.0 / SCALE) + EPS * jnp.log(total)
        if at_ref.shape[0] == 1:
            at_ref[:, at] = out
            continue
        for r in range(LANES // 128):
            row = k * (LANES // 128) + r
            at_ref[row : row + 1, :] = out[:, r * 128 : (r + 1) * 128]


def to_everyone(v, out_ref):
    for k in range(out_ref.shape[0]):
        out_ref[k] = v


def in_lanes(v):
    return jnp.concatenate([v[k : k + 1] for k in range(v.shape[0])], axis=1)


def tree(parts, combine):
    while len(parts) > 1:
        parts = [combine(parts[k], parts[k + 1]) for k in range(0, len(parts), 2)]
    return parts[0]


def lse_received(ref):
    parts = [ref[k] for k in range(ref.shape[0])]
    top = tree(parts, jnp.maximum)
    total = tree([jnp.exp((part - top) * (1.0 / EPS)) for part in parts], jnp.add)
    return in_lanes(top + EPS * jnp.log(total))


def sum_received(ref):
    return tree([ref[k] for k in range(ref.shape[0])], jnp.add)


def fetch(pairs, sems):
    copies = [pltpu.make_async_copy(src, dst, sems.at[k]) for k, (src, dst) in enumerate(pairs)]
    for copy in copies:
        copy.start()
    return copies


def wait_all(copies):
    for copy in copies:
        copy.wait()


def rows_first(
    x_any, y_any, lx_any, ly_any, lc_any,
    out_ref, sqx_ref, sqy_ref, at_ref, x_ref, y_ref, lx_ref, ly_ref, lc_ref, sems,
):
    pairs = [(ly_any, ly_ref), (lc_any, lc_ref), (lx_any, lx_ref), (y_any, y_ref), (x_any, x_ref)]
    wait_all(fetch(pairs, sems))
    y = y_ref[...]
    sq = square_sums(y)
    sqy_ref[...] = sq
    sqx_ref[...] = square_sums(x_ref[...])
    columns = as_columns(target_rows(ly_ref[...], -sq, lc_ref[...]))
    rows = as_rows(train_rows(lx_ref[...], jnp.zeros(lx_ref.shape, jnp.float32)))
    reduce_over_sub(y, columns, x_ref, rows, at_ref, False)
    to_everyone(at_ref[...], out_ref)


def columns_first(
    log_m, x_ref, y_ref, lx_ref, ly_ref, lc_ref, got_ref, out_ref, phi_ref, at_ref
):
    phi = -log_m - lse_received(got_ref)
    phi_ref[...] = phi
    columns = as_columns(train_rows(lx_ref[...], phi))
    rows = as_rows(target_rows(ly_ref[...], jnp.zeros(ly_ref.shape, jnp.float32), lc_ref[...]))
    reduce_over_sub(x_ref[...], columns, y_ref, rows, at_ref, False)
    to_everyone(at_ref[...], out_ref)


def rows_next(
    log_n, x_ref, y_ref, lx_ref, ly_ref, lc_ref, phi_ref, got_ref, out_ref, gamma_ref, at_ref
):
    gamma = -log_n - lse_received(got_ref)
    gamma_ref[...] = gamma
    columns = as_columns(target_rows(ly_ref[...], gamma, lc_ref[...]))
    rows = as_rows(train_rows(lx_ref[...], phi_ref[...] + log_n))
    reduce_over_sub(y_ref[...], columns, x_ref, rows, at_ref, True)
    to_everyone(at_ref[...], out_ref)


def columns_next(
    log_m, log_n, x_ref, y_ref, lx_ref, ly_ref, lc_ref, phi_ref, gamma_ref, sqx_ref, got_ref,
    out_ref, new_ref, at_ref,
):
    n = y_ref.shape[0]
    phi = phi_ref[...] + log_n - log_m - EPS * jnp.log(in_lanes(sum_received(got_ref)))
    new_ref[...] = phi
    columns = as_columns(train_rows(lx_ref[...], phi))
    rows = as_rows(target_rows(ly_ref[...], gamma_ref[...] + log_m, lc_ref[...]))
    reduce_over_sub(x_ref[...], columns, y_ref, rows, at_ref, True)
    dual_sum = jnp.sum(phi + sqx_ref[...], axis=1, keepdims=True)
    at_ref[:, n : n + 128] = jnp.broadcast_to(dual_sum, (1, 128))
    to_everyone(at_ref[...], out_ref)


def potentials(
    log_m, log_n, others, ly_ref, phi_ref, gamma_ref, sqx_ref, sqy_ref, got_ref, out_ref, value_ref, potential_ref, at_ref
):
    n = gamma_ref.shape[1]
    total = sum_received(got_ref)
    gamma = gamma_ref[...] + log_m - log_n - EPS * jnp.log(total[:, 0:n])
    label = ly_ref[...].astype(jnp.float32)
    for r in range(n // 128):
        at_ref[r : r + 1, :] = gamma[:, r * 128 : (r + 1) * 128]
        at_ref[n // 128 + r : n // 128 + r + 1, :] = label[:, r * 128 : (r + 1) * 128]
    to_everyone(at_ref[...], out_ref)
    potential_ref[...] = gamma + sqy_ref[...]
    dual = phi_ref[...] + sqx_ref[...]
    value_ref[...] = dual - (total[:, n : n + 1] - dual) / others


def on_diagonal(v):
    shape = (SHARE, 128)
    row, column = (lax.broadcasted_iota(jnp.int32, shape, k) for k in range(2))
    axis = 0 if v.shape[0] == SHARE else 1
    return jnp.sum(jnp.where(row == column, v, 0.0), axis=axis, keepdims=True)


def project(
    shift, x_any, lx_ref, lc_ref, phi_ref, got_ref, all_any, quarter_ref, out_ref, xs_ref, xa_ref, aug_ref, here_ref, sems
):
    parts, r = got_ref.shape[0], got_ref.shape[1] // 2
    quarter = quarter_ref[0]
    pairs = []
    for k in range(out_ref.shape[0]):
        start = pl.multiple_of((parts * k + quarter) * SHARE, SHARE)
        pairs.append((x_any.at[pl.ds(start, SHARE), :], xs_ref.at[pl.ds(k * SHARE, SHARE), :]))
    pairs += [(all_any.at[p], here_ref.at[p]) for p in range(parts)]
    copies = fetch(pairs, sems)
    aug_ref[...] = as_columns(train_rows(lx_ref[...], phi_ref[...] + shift)).astype(jnp.float32)
    for k in range(out_ref.shape[0]):
        start = pl.multiple_of((parts * k + quarter) * SHARE, SHARE)
        xa_ref[pl.ds(k * SHARE, SHARE), :] = aug_ref[pl.ds(start, SHARE), :].astype(jnp.bfloat16)
    wait_all(copies[: out_ref.shape[0]])
    numer, denom = 0.0, 0.0
    for p in range(parts):
        copies[out_ref.shape[0] + p].wait()
        y = here_ref[p].astype(jnp.bfloat16)
        got = got_ref[p]
        rows = as_rows(target_rows(in_lanes(got[r:]), in_lanes(got[:r]), lc_ref[...]))
        t = dot_nt(xs_ref[...], y) + dot_nn(xa_ref[...], rows)
        w = jnp.exp2(t * KAPPA).astype(jnp.bfloat16)
        denom = denom + jnp.sum(w.astype(jnp.float32), axis=1, keepdims=True)
        numer = numer + dot_nn(w, y)
    for k in range(out_ref.shape[0]):
        part = slice(k * SHARE, (k + 1) * SHARE)
        out_ref[k, 0:SHARE, :] = numer[part, 0:128]
        out_ref[k, SHARE : 2 * SHARE, :] = numer[part, 128:256]
        out_ref[k, 2 * SHARE : CHUNK, :] = jnp.broadcast_to(on_diagonal(denom[part]), (CHUNK - 2 * SHARE, 128))


def finish(got_ref, out_ref):
    total = sum_received(got_ref)
    denom = on_diagonal(total[2 * SHARE : 2 * SHARE + 1])
    out_ref[:, 0:128] = total[0:SHARE] / denom
    out_ref[:, 128:256] = total[SHARE : 2 * SHARE] / denom


def call(body, outs, args, scratch=(), smem=(), anywhere=(), flops=0, limit=40):
    vmem = pl.BlockSpec(memory_space=pltpu.VMEM)
    specs = [vmem for _ in args]
    for k in smem:
        specs[k] = pl.BlockSpec(memory_space=pltpu.SMEM)
    for k in anywhere:
        specs[k] = pl.BlockSpec(memory_space=pl.ANY)
    outs = [s if hasattr(s, "dtype") else jax.ShapeDtypeStruct(s, jnp.float32) for s in outs]
    return pl.pallas_call(
        body,
        out_shape=outs,
        in_specs=specs,
        out_specs=[vmem for _ in outs],
        scratch_shapes=list(scratch),
        compiler_params=pltpu.CompilerParams(vmem_limit_bytes=limit * 2**20),
        cost_estimate=pl.CostEstimate(flops=flops, bytes_accessed=2**20, transcendentals=flops // 512),
    )(*args)


def exchange(x, axis, groups=None):
    return lax.all_to_all(x, axis, 0, 0, axis_index_groups=groups, tiled=True)


def on_device(train_embed, train_label, target_embed, target_label, label_cost):
    m_dev, width = train_embed.shape
    n_dev = target_embed.shape[0]
    trains = lax.axis_size("train")
    targets = lax.axis_size("target")
    log_m = EPS * math.log(m_dev * trains)
    log_n = EPS * math.log(n_dev * targets)
    near = 4
    depth = targets // near
    near_groups = [[near * z + q for q in range(near)] for z in range(depth)]
    deep_groups = [[near * z + q for z in range(depth)] for q in range(near)]

    near_targets = lax.all_gather(target_embed.astype(jnp.float32), "target", axis_index_groups=near_groups)

    data = (
        train_embed,
        target_embed,
        train_label.reshape(1, m_dev),
        target_label.reshape(1, n_dev),
        label_cost,
    )
    row_m, row_n = (1, m_dev), (1, n_dev)
    tile_m, tile_n = (m_dev // 128, 128), (n_dev // 128, 128)
    flops = 2 * m_dev * n_dev * 512

    def run(body, outs, tile, *args):
        return call(body, outs, args, scratch=[pltpu.VMEM(tile, jnp.float32)], flops=flops)

    local, sqx, sqy = call(
        rows_first,
        [(targets,) + tile_m, row_m, row_n],
        data,
        scratch=[pltpu.VMEM(tile_m, jnp.float32)]
        + [pltpu.VMEM(v.shape, v.dtype) for v in data]
        + [pltpu.SemaphoreType.DMA((len(data),))],
        anywhere=range(len(data)),
        flops=flops,
        limit=54,
    )
    got = exchange(local, "target")
    local, phi = run(
        functools.partial(columns_first, log_m), [(trains,) + tile_n, row_m], tile_n, *data, got
    )
    got = exchange(local, "train")
    local, gamma = run(
        functools.partial(rows_next, log_n), [(targets,) + tile_m, row_n], tile_m, *data, phi, got
    )
    got = exchange(local, "target")
    row_more = (1, n_dev + 128)
    local, phi = run(
        functools.partial(columns_next, log_m, log_n), [(trains,) + row_more, row_m], row_more, *data, phi, gamma, sqx, got
    )
    got = exchange(local, "train")
    local, value, potential = call(
        functools.partial(potentials, log_m, log_n, m_dev * trains - 1),
        [(near, 2 * tile_n[0], 128), row_m, row_n],
        (data[3], phi, gamma, sqx, sqy, got),
        scratch=[pltpu.VMEM((2 * tile_n[0], 128), jnp.float32)],
    )
    got = exchange(local, "target", near_groups)

    quarter = (lax.axis_index("target").astype(jnp.int32) % near).reshape(1)
    rows = SHARE * depth
    (out,) = call(
        functools.partial(project, log_n),
        [(depth, CHUNK, 128)],
        (train_embed, data[2], label_cost, phi, got, near_targets, quarter),
        scratch=[
            pltpu.VMEM((rows, width), jnp.bfloat16),
            pltpu.VMEM((rows, 128), jnp.bfloat16),
            pltpu.VMEM((m_dev, 128), jnp.float32),
            pltpu.VMEM(near_targets.shape, jnp.float32),
            pltpu.SemaphoreType.DMA((depth + near,)),
        ],
        anywhere=(0, 5),
        smem=(6,),
        flops=flops,
        limit=52,
    )
    got = exchange(out, "target", deep_groups)
    (barycentre,) = call(finish, [(SHARE, width)], (got,))
    return (value.reshape(m_dev), potential.reshape(n_dev), barycentre)


def solution(mesh):
    return jax.shard_map(
        on_device,
        mesh=mesh,
        in_specs=(P("train", None), P("train"), P("target", None), P("target"), P()),
        out_specs=(P("train"), P("target"), P(("train", "target"), None)),
        check_vma=False,
    )
```

```python
import functools
import math

import jax
import jax.numpy as jnp
from jax import lax
from jax.experimental import pallas as pl
from jax.experimental.pallas import tpu as pltpu
from jax.sharding import PartitionSpec as P

EPS = 0.05
SCALE = 128.0
KAPPA = math.log2(math.e) / EPS / SCALE
LANES = 256
SHARE = 32
CHUNK = 2 * SHARE + 8


def pieces(v):
    hi = v.astype(jnp.bfloat16).astype(jnp.float32)
    rest = v - hi
    mid = rest.astype(jnp.bfloat16).astype(jnp.float32)
    lo = (rest - mid).astype(jnp.bfloat16).astype(jnp.float32)
    return hi, mid, lo


def tail(first, second):
    n = first[0].shape[1]
    row = lax.broadcasted_iota(jnp.int32, (8, n), 0)
    out = jnp.zeros((8, n), jnp.float32)
    for k, v in enumerate(first + second):
        out = jnp.where(row == k, v, out)
    return out


def ones_like3(v):
    return (jnp.ones_like(v),) * 3


def train_rows(label, phi):
    m = label.shape[1]
    onehot = (lax.broadcasted_iota(jnp.int32, (8, m), 0) == label).astype(jnp.float32)
    last = tail(ones_like3(phi), pieces(phi * SCALE))
    return jnp.concatenate([onehot, onehot, onehot, last], axis=0)


def target_rows(label, gamma, label_cost):
    n = label.shape[1]
    table = jnp.zeros((8, n), jnp.float32)
    for b in range(8):
        table = jnp.where(label == b, label_cost[:, b : b + 1], table)
    last = tail(pieces(gamma * SCALE), ones_like3(gamma))
    return jnp.concatenate(list(pieces(table * -SCALE)) + [last], axis=0)


def as_columns(rows):
    pad = jnp.zeros((96, rows.shape[1]), jnp.float32)
    return jnp.concatenate([rows, pad], axis=0).T.astype(jnp.bfloat16)


def as_rows(rows):
    pad = jnp.zeros((96, rows.shape[1]), jnp.float32)
    return jnp.concatenate([rows, pad], axis=0).astype(jnp.bfloat16)


def dot_nt(a, b):
    return lax.dot_general(a, b, (((1,), (1,)), ((), ())), preferred_element_type=jnp.float32)


def dot_nn(a, b):
    return lax.dot_general(a, b, (((1,), (0,)), ((), ())), preferred_element_type=jnp.float32)


def square_sums(v):
    sq = jnp.square(v.astype(jnp.float32))
    hi = sq.astype(jnp.bfloat16)
    lo = (sq - hi.astype(jnp.float32)).astype(jnp.bfloat16)
    ones = jnp.ones((8, v.shape[1]), jnp.bfloat16)
    return (dot_nt(ones, hi) + dot_nt(ones, lo))[0:1] / v.shape[1]


def reduce_over_sub(sub, sub_columns, lane_ref, lane_rows, at_ref, shifted):
    n = lane_ref.shape[0]
    for k in range(n // LANES):
        at = pl.ds(k * LANES, LANES)
        t = dot_nt(sub, lane_ref[at, :]) + dot_nn(sub_columns, lane_rows[:, k * LANES : (k + 1) * LANES])
        if shifted:
            out = jnp.sum(jnp.exp2(t * KAPPA), axis=0, keepdims=True)
        else:
            top = jnp.max(t, axis=0, keepdims=True)
            total = jnp.sum(jnp.exp2((t - top) * KAPPA), axis=0, keepdims=True)
            out = top * (1.0 / SCALE) + EPS * jnp.log(total)
        if at_ref.shape[0] == 1:
            at_ref[:, at] = out
            continue
        for r in range(LANES // 128):
            row = k * (LANES // 128) + r
            at_ref[row : row + 1, :] = out[:, r * 128 : (r + 1) * 128]


def to_everyone(v, out_ref):
    for k in range(out_ref.shape[0]):
        out_ref[k] = v


def in_lanes(v):
    return jnp.concatenate([v[k : k + 1] for k in range(v.shape[0])], axis=1)


def tree(parts, combine):
    while len(parts) > 1:
        parts = [combine(parts[k], parts[k + 1]) for k in range(0, len(parts), 2)]
    return parts[0]


def lse_received(ref):
    parts = [ref[k] for k in range(ref.shape[0])]
    top = tree(parts, jnp.maximum)
    total = tree([jnp.exp((part - top) * (1.0 / EPS)) for part in parts], jnp.add)
    return in_lanes(top + EPS * jnp.log(total))


def sum_received(ref):
    return tree([ref[k] for k in range(ref.shape[0])], jnp.add)


def fetch(pairs, sems):
    copies = [pltpu.make_async_copy(src, dst, sems.at[k]) for k, (src, dst) in enumerate(pairs)]
    for copy in copies:
        copy.start()
    return copies


def wait_all(copies):
    for copy in copies:
        copy.wait()


def rows_first(
    x_any, y_any, lx_any, ly_any, lc_any,
    out_ref, sqx_ref, sqy_ref, at_ref, x_ref, y_ref, lx_ref, ly_ref, lc_ref, sems,
):
    pairs = [(ly_any, ly_ref), (lc_any, lc_ref), (lx_any, lx_ref), (y_any, y_ref), (x_any, x_ref)]
    copies = fetch(pairs, sems)
    wait_all(copies[:3])
    rows = as_rows(train_rows(lx_ref[...], jnp.zeros(lx_ref.shape, jnp.float32)))
    copies[3].wait()
    y = y_ref[...]
    sq = square_sums(y)
    sqy_ref[...] = sq
    columns = as_columns(target_rows(ly_ref[...], -sq, lc_ref[...]))
    copies[4].wait()
    sqx_ref[...] = square_sums(x_ref[...])
    reduce_over_sub(y, columns, x_ref, rows, at_ref, False)
    to_everyone(at_ref[...], out_ref)


def columns_first(
    log_m, x_ref, y_ref, lx_ref, ly_ref, lc_ref, got_ref, out_ref, phi_ref, at_ref
):
    phi = -log_m - lse_received(got_ref)
    phi_ref[...] = phi
    columns = as_columns(train_rows(lx_ref[...], phi))
    rows = as_rows(target_rows(ly_ref[...], jnp.zeros(ly_ref.shape, jnp.float32), lc_ref[...]))
    reduce_over_sub(x_ref[...], columns, y_ref, rows, at_ref, False)
    to_everyone(at_ref[...], out_ref)


def rows_next(
    log_n, x_ref, y_ref, lx_ref, ly_ref, lc_ref, phi_ref, got_ref, out_ref, gamma_ref, at_ref
):
    gamma = -log_n - lse_received(got_ref)
    gamma_ref[...] = gamma
    columns = as_columns(target_rows(ly_ref[...], gamma, lc_ref[...]))
    rows = as_rows(train_rows(lx_ref[...], phi_ref[...] + log_n))
    reduce_over_sub(y_ref[...], columns, x_ref, rows, at_ref, True)
    to_everyone(at_ref[...], out_ref)


def columns_next(
    log_m, log_n, x_ref, y_ref, lx_ref, ly_ref, lc_ref, phi_ref, gamma_ref, sqx_ref, got_ref,
    out_ref, new_ref, at_ref,
):
    n = y_ref.shape[0]
    phi = phi_ref[...] + log_n - log_m - EPS * jnp.log(in_lanes(sum_received(got_ref)))
    new_ref[...] = phi
    columns = as_columns(train_rows(lx_ref[...], phi))
    rows = as_rows(target_rows(ly_ref[...], gamma_ref[...] + log_m, lc_ref[...]))
    reduce_over_sub(x_ref[...], columns, y_ref, rows, at_ref, True)
    dual_sum = jnp.sum(phi + sqx_ref[...], axis=1, keepdims=True)
    at_ref[:, n : n + 128] = jnp.broadcast_to(dual_sum, (1, 128))
    to_everyone(at_ref[...], out_ref)


def potentials(log_m, log_n, others, phi_ref, gamma_ref, sqx_ref, sqy_ref, got_ref, new_ref, value_ref, potential_ref):
    n = gamma_ref.shape[1]
    total = sum_received(got_ref)
    gamma = gamma_ref[...] + log_m - log_n - EPS * jnp.log(total[:, 0:n])
    new_ref[...] = gamma
    potential_ref[...] = gamma + sqy_ref[...]
    dual = phi_ref[...] + sqx_ref[...]
    value_ref[...] = dual - (total[:, n : n + 1] - dual) / others


def on_diagonal(v):
    shape = (SHARE, 128)
    row, column = (lax.broadcasted_iota(jnp.int32, shape, k) for k in range(2))
    axis = 0 if v.shape[0] == SHARE else 1
    return jnp.sum(jnp.where(row == column, v, 0.0), axis=axis, keepdims=True)


def weighted_sums(shift, relative, x_ref, y_ref, lx_ref, ly_ref, lc_ref, phi_ref, gamma_ref, core_ref, out_ref, xs_ref, xa_ref, aug_ref):
    core = core_ref[0]
    aug_ref[...] = as_columns(train_rows(lx_ref[...], phi_ref[...] + shift)).astype(jnp.float32)
    rows = as_rows(target_rows(ly_ref[...], gamma_ref[...], lc_ref[...]))
    y = y_ref[...]
    for k, rel in enumerate(relative):
        start = pl.multiple_of((core ^ rel) * SHARE, SHARE)
        xs_ref[pl.ds(k * SHARE, SHARE), :] = x_ref[pl.ds(start, SHARE), :]
        xa_ref[pl.ds(k * SHARE, SHARE), :] = aug_ref[pl.ds(start, SHARE), :].astype(jnp.bfloat16)
    per = min(8, len(relative))
    for b in range(len(relative) // per):
        at = pl.ds(b * per * SHARE, per * SHARE)
        t = dot_nt(xs_ref[at, :], y) + dot_nn(xa_ref[at, :], rows)
        w = jnp.exp2(t * KAPPA).astype(jnp.bfloat16)
        denom = jnp.sum(w.astype(jnp.float32), axis=1, keepdims=True)
        numer = dot_nn(w, y)
        for k in range(per):
            part, chunk = slice(k * SHARE, (k + 1) * SHARE), b * per + k
            out_ref[chunk, 0:SHARE, :] = numer[part, 0:128]
            out_ref[chunk, SHARE : 2 * SHARE, :] = numer[part, 128:256]
            out_ref[chunk, 2 * SHARE : CHUNK, :] = jnp.broadcast_to(on_diagonal(denom[part]), (CHUNK - 2 * SHARE, 128))


def project_sent(
    log_m, log_n, others, relative,
    x_ref, y_ref, lx_ref, ly_ref, lc_ref, phi_ref, gamma_ref, sqx_ref, sqy_ref, got_ref, core_ref,
    out_ref, new_ref, value_ref, potential_ref, xs_ref, xa_ref, aug_ref,
):
    potentials(log_m, log_n, others, phi_ref, gamma_ref, sqx_ref, sqy_ref, got_ref, new_ref, value_ref, potential_ref)
    weighted_sums(log_n, relative, x_ref, y_ref, lx_ref, ly_ref, lc_ref, phi_ref, new_ref, core_ref, out_ref, xs_ref, xa_ref, aug_ref)


def finish(got_ref, out_ref):
    total = sum_received(got_ref)
    denom = on_diagonal(total[2 * SHARE : 2 * SHARE + 1])
    out_ref[:, 0:128] = total[0:SHARE] / denom
    out_ref[:, 128:256] = total[SHARE : 2 * SHARE] / denom


def call(body, outs, args, scratch=(), smem=(), anywhere=(), flops=0, limit=40):
    vmem = pl.BlockSpec(memory_space=pltpu.VMEM)
    specs = [vmem for _ in args]
    for k in smem:
        specs[k] = pl.BlockSpec(memory_space=pltpu.SMEM)
    for k in anywhere:
        specs[k] = pl.BlockSpec(memory_space=pl.ANY)
    outs = [s if hasattr(s, "dtype") else jax.ShapeDtypeStruct(s, jnp.float32) for s in outs]
    return pl.pallas_call(
        body,
        out_shape=outs,
        in_specs=specs,
        out_specs=[vmem for _ in outs],
        scratch_shapes=list(scratch),
        compiler_params=pltpu.CompilerParams(vmem_limit_bytes=int(limit * 2**20)),
        cost_estimate=pl.CostEstimate(flops=flops, bytes_accessed=2**20, transcendentals=flops // 512),
    )(*args)


def exchange(x, axis, groups=None):
    return lax.all_to_all(x, axis, 0, 0, axis_index_groups=groups, tiled=True)


def on_device(train_embed, train_label, target_embed, target_label, label_cost):
    m_dev, width = train_embed.shape
    n_dev = target_embed.shape[0]
    trains = lax.axis_size("train")
    targets = lax.axis_size("target")
    log_m = EPS * math.log(m_dev * trains)
    log_n = EPS * math.log(n_dev * targets)
    data = (
        train_embed,
        target_embed,
        train_label.reshape(1, m_dev),
        target_label.reshape(1, n_dev),
        label_cost,
    )
    row_m, row_n = (1, m_dev), (1, n_dev)
    tile_m, tile_n = (m_dev // 128, 128), (n_dev // 128, 128)
    flops = 2 * m_dev * n_dev * 512

    def run(body, outs, tile, *args):
        return call(body, outs, args, scratch=[pltpu.VMEM(tile, jnp.float32)], flops=flops)

    local, sqx, sqy = call(
        rows_first,
        [(targets,) + tile_m, row_m, row_n],
        data,
        scratch=[pltpu.VMEM(tile_m, jnp.float32)]
        + [pltpu.VMEM(v.shape, v.dtype) for v in data]
        + [pltpu.SemaphoreType.DMA((len(data),))],
        anywhere=range(len(data)),
        flops=flops,
        limit=54,
    )
    got = exchange(local, "target")
    local, phi = run(
        functools.partial(columns_first, log_m), [(trains,) + tile_n, row_m], tile_n, *data, got
    )
    got = exchange(local, "train")
    local, gamma = run(
        functools.partial(rows_next, log_n), [(targets,) + tile_m, row_n], tile_m, *data, phi, got
    )
    got = exchange(local, "target")
    row_more = (1, n_dev + 128)
    local, phi = run(
        functools.partial(columns_next, log_m, log_n), [(trains,) + row_more, row_m], row_more, *data, phi, gamma, sqx, got
    )
    got = exchange(local, "train")
    core = (lax.axis_index("target").astype(jnp.int32) & 1).reshape(1)
    half = targets // 2
    rows = SHARE * half
    scratch = [
        pltpu.VMEM((rows, width), jnp.bfloat16),
        pltpu.VMEM((rows, 128), jnp.bfloat16),
        pltpu.VMEM((m_dev, 128), jnp.float32),
    ]
    chunks = (half, CHUNK, 128)
    sent, gamma, value, potential = call(
        functools.partial(project_sent, log_m, log_n, m_dev * trains - 1, [2 * k + 1 for k in range(half)]),
        [chunks, row_n, row_m, row_n],
        (*data, phi, gamma, sqx, sqy, got, core),
        scratch=scratch, smem=(10,), flops=flops,
    )
    sent = lax.ppermute(sent, "target", [(t, t ^ 1) for t in range(targets)])
    (kept,) = call(
        functools.partial(weighted_sums, log_n, [2 * k for k in range(half)]),
        [chunks],
        (*data, phi, gamma, core),
        scratch=scratch, smem=(7,), flops=flops,
    )
    groups = [[c + 2 * k for k in range(half)] for c in range(2)]
    got = exchange(kept + sent, "target", groups)
    (barycentre,) = call(finish, [(SHARE, width)], (got,))
    return (value.reshape(m_dev), potential.reshape(n_dev), barycentre)


def solution(mesh):
    return jax.shard_map(
        on_device,
        mesh=mesh,
        in_specs=(P("train", None), P("train"), P("target", None), P("target"), P()),
        out_specs=(P("train"), P("target"), P(("train", "target"), None)),
        check_vma=False,
    )
```

```python
import functools
import math

import jax
import jax.numpy as jnp
from jax import lax
from jax.experimental import pallas as pl
from jax.experimental.pallas import tpu as pltpu
from jax.sharding import PartitionSpec as P

EPS = 0.05
SCALE = 128.0
KAPPA = math.log2(math.e) / EPS / SCALE
LANES = 256
SHARE = 32
CHUNK = 2 * SHARE + 8


def pieces(v):
    hi = v.astype(jnp.bfloat16).astype(jnp.float32)
    rest = v - hi
    mid = rest.astype(jnp.bfloat16).astype(jnp.float32)
    lo = (rest - mid).astype(jnp.bfloat16).astype(jnp.float32)
    return hi, mid, lo


def tail(first, second):
    n = first[0].shape[1]
    row = lax.broadcasted_iota(jnp.int32, (8, n), 0)
    out = jnp.zeros((8, n), jnp.float32)
    for k, v in enumerate(first + second):
        out = jnp.where(row == k, v, out)
    return out


def ones_like3(v):
    return (jnp.ones_like(v),) * 3


def train_rows(label, phi):
    m = label.shape[1]
    onehot = (lax.broadcasted_iota(jnp.int32, (8, m), 0) == label).astype(jnp.float32)
    last = tail(ones_like3(phi), pieces(phi * SCALE))
    return jnp.concatenate([onehot, onehot, onehot, last], axis=0)


def target_rows(label, gamma, label_cost):
    n = label.shape[1]
    table = jnp.zeros((8, n), jnp.float32)
    for b in range(8):
        table = jnp.where(label == b, label_cost[:, b : b + 1], table)
    last = tail(pieces(gamma * SCALE), ones_like3(gamma))
    return jnp.concatenate(list(pieces(table * -SCALE)) + [last], axis=0)


def as_columns(rows):
    pad = jnp.zeros((96, rows.shape[1]), jnp.float32)
    return jnp.concatenate([rows, pad], axis=0).T.astype(jnp.bfloat16)


def as_rows(rows):
    pad = jnp.zeros((96, rows.shape[1]), jnp.float32)
    return jnp.concatenate([rows, pad], axis=0).astype(jnp.bfloat16)


def dot_nt(a, b):
    return lax.dot_general(a, b, (((1,), (1,)), ((), ())), preferred_element_type=jnp.float32)


def dot_nn(a, b):
    return lax.dot_general(a, b, (((1,), (0,)), ((), ())), preferred_element_type=jnp.float32)


def square_sums(v):
    sq = jnp.square(v.astype(jnp.float32))
    hi = sq.astype(jnp.bfloat16)
    lo = (sq - hi.astype(jnp.float32)).astype(jnp.bfloat16)
    ones = jnp.ones((8, v.shape[1]), jnp.bfloat16)
    return (dot_nt(ones, hi) + dot_nt(ones, lo))[0:1] / v.shape[1]


def reduce_over_sub(sub, sub_columns, lane_ref, lane_rows, at_ref, shifted):
    n = lane_ref.shape[0]
    for k in range(n // LANES):
        at = pl.ds(k * LANES, LANES)
        t = dot_nt(sub, lane_ref[at, :]) + dot_nn(sub_columns, lane_rows[:, k * LANES : (k + 1) * LANES])
        if shifted:
            out = jnp.sum(jnp.exp2(t * KAPPA), axis=0, keepdims=True)
        else:
            top = jnp.max(t, axis=0, keepdims=True)
            total = jnp.sum(jnp.exp2((t - top) * KAPPA), axis=0, keepdims=True)
            out = top * (1.0 / SCALE) + EPS * jnp.log(total)
        if at_ref.shape[0] == 1:
            at_ref[:, at] = out
            continue
        for r in range(LANES // 128):
            row = k * (LANES // 128) + r
            at_ref[row : row + 1, :] = out[:, r * 128 : (r + 1) * 128]


def to_everyone(v, out_ref):
    for k in range(out_ref.shape[0]):
        out_ref[k] = v


def in_lanes(v):
    return jnp.concatenate([v[k : k + 1] for k in range(v.shape[0])], axis=1)


def tree(parts, combine):
    while len(parts) > 1:
        parts = [combine(parts[k], parts[k + 1]) for k in range(0, len(parts), 2)]
    return parts[0]


def lse_received(ref):
    parts = [ref[k] for k in range(ref.shape[0])]
    top = tree(parts, jnp.maximum)
    total = tree([jnp.exp((part - top) * (1.0 / EPS)) for part in parts], jnp.add)
    return in_lanes(top + EPS * jnp.log(total))


def sum_received(ref):
    return tree([ref[k] for k in range(ref.shape[0])], jnp.add)


def fetch(pairs, sems):
    copies = [pltpu.make_async_copy(src, dst, sems.at[k]) for k, (src, dst) in enumerate(pairs)]
    for copy in copies:
        copy.start()
    return copies


def wait_all(copies):
    for copy in copies:
        copy.wait()


def rows_first(
    x_any, y_any, lx_any, ly_any, lc_any, core_ref,
    out_ref, sqx_ref, sqy_ref, at_ref, x_ref, y_ref, lx_ref, ly_ref, lc_ref, sems,
):
    pairs = [(ly_any, ly_ref), (lc_any, lc_ref), (lx_any, lx_ref), (y_any, y_ref), (x_any, x_ref)]
    copies = fetch(pairs, sems)
    wait_all(copies[:3])
    rows = as_rows(train_rows(lx_ref[...], jnp.zeros(lx_ref.shape, jnp.float32)))
    copies[3].wait()
    y = y_ref[...]
    sq = square_sums(y)
    sqy_ref[...] = sq
    columns = as_columns(target_rows(ly_ref[...], -sq, lc_ref[...]))
    copies[4].wait()
    sqx_ref[...] = square_sums(x_ref[...])
    reduce_over_sub(y, columns, x_ref, rows, at_ref, False)
    to_everyone(at_ref[...], out_ref)


def columns_first(
    log_m, x_ref, y_ref, lx_ref, ly_ref, lc_ref, got_ref, out_ref, phi_ref, at_ref
):
    phi = -log_m - lse_received(got_ref)
    phi_ref[...] = phi
    columns = as_columns(train_rows(lx_ref[...], phi))
    rows = as_rows(target_rows(ly_ref[...], jnp.zeros(ly_ref.shape, jnp.float32), lc_ref[...]))
    reduce_over_sub(x_ref[...], columns, y_ref, rows, at_ref, False)
    to_everyone(at_ref[...], out_ref)


def rows_next(
    log_n, x_ref, y_ref, lx_ref, ly_ref, lc_ref, phi_ref, got_ref, out_ref, gamma_ref, at_ref
):
    gamma = -log_n - lse_received(got_ref)
    gamma_ref[...] = gamma
    columns = as_columns(target_rows(ly_ref[...], gamma, lc_ref[...]))
    rows = as_rows(train_rows(lx_ref[...], phi_ref[...] + log_n))
    reduce_over_sub(y_ref[...], columns, x_ref, rows, at_ref, True)
    to_everyone(at_ref[...], out_ref)


def columns_next(
    log_m, log_n, x_ref, y_ref, lx_ref, ly_ref, lc_ref, phi_ref, gamma_ref, sqx_ref, got_ref,
    out_ref, new_ref, at_ref,
):
    n = y_ref.shape[0]
    phi = phi_ref[...] + log_n - log_m - EPS * jnp.log(in_lanes(sum_received(got_ref)))
    new_ref[...] = phi
    columns = as_columns(train_rows(lx_ref[...], phi))
    rows = as_rows(target_rows(ly_ref[...], gamma_ref[...] + log_m, lc_ref[...]))
    reduce_over_sub(x_ref[...], columns, y_ref, rows, at_ref, True)
    dual_sum = jnp.sum(phi + sqx_ref[...], axis=1, keepdims=True)
    at_ref[:, n : n + 128] = jnp.broadcast_to(dual_sum, (1, 128))
    to_everyone(at_ref[...], out_ref)


def on_diagonal(v):
    shape = (SHARE, 128)
    row, column = (lax.broadcasted_iota(jnp.int32, shape, k) for k in range(2))
    axis = 0 if v.shape[0] == SHARE else 1
    return jnp.sum(jnp.where(row == column, v, 0.0), axis=axis, keepdims=True)


def weighted_sums(shift, relative, x_ref, y_ref, lx_ref, ly_ref, lc_ref, phi_ref, gamma_ref, core_ref, out_ref, xs_ref, xa_ref, aug_ref):
    core = core_ref[0]
    aug_ref[...] = as_columns(train_rows(lx_ref[...], phi_ref[...] + shift)).astype(jnp.float32)
    rows = as_rows(target_rows(ly_ref[...], gamma_ref[...], lc_ref[...]))
    y = y_ref[...]
    for k, rel in enumerate(relative):
        start = pl.multiple_of((core ^ rel) * SHARE, SHARE)
        xs_ref[pl.ds(k * SHARE, SHARE), :] = x_ref[pl.ds(start, SHARE), :]
        xa_ref[pl.ds(k * SHARE, SHARE), :] = aug_ref[pl.ds(start, SHARE), :].astype(jnp.bfloat16)
    per = min(8, len(relative))
    for b in range(len(relative) // per):
        at = pl.ds(b * per * SHARE, per * SHARE)
        t = dot_nt(xs_ref[at, :], y) + dot_nn(xa_ref[at, :], rows)
        w = jnp.exp2(t * KAPPA).astype(jnp.bfloat16)
        denom = jnp.sum(w.astype(jnp.float32), axis=1, keepdims=True)
        numer = dot_nn(w, y)
        for k in range(per):
            part, chunk = slice(k * SHARE, (k + 1) * SHARE), b * per + k
            out_ref[chunk, 0:SHARE, :] = numer[part, 0:128]
            out_ref[chunk, SHARE : 2 * SHARE, :] = numer[part, 128:256]
            out_ref[chunk, 2 * SHARE : CHUNK, :] = jnp.broadcast_to(on_diagonal(denom[part]), (CHUNK - 2 * SHARE, 128))


def project_sent(
    log_m, log_n, relative,
    x_ref, y_ref, lx_ref, ly_ref, lc_ref, phi_ref, gamma_ref, got_ref, core_ref,
    out_ref, new_ref, xs_ref, xa_ref, aug_ref,
):
    total = sum_received(got_ref)
    new_ref[...] = gamma_ref[...] + log_m - log_n - EPS * jnp.log(total[:, 0 : new_ref.shape[1]])
    weighted_sums(log_n, relative, x_ref, y_ref, lx_ref, ly_ref, lc_ref, phi_ref, new_ref, core_ref, out_ref, xs_ref, xa_ref, aug_ref)


def project_kept(
    log_n, others, relative,
    x_ref, y_ref, lx_ref, ly_ref, lc_ref, phi_ref, gamma_ref, sqx_ref, sqy_ref, got_ref, core_ref,
    out_ref, value_ref, potential_ref, xs_ref, xa_ref, aug_ref,
):
    n = gamma_ref.shape[1]
    potential_ref[...] = gamma_ref[...] + sqy_ref[...]
    dual = phi_ref[...] + sqx_ref[...]
    dual_sum = tree([got_ref[k, :, n : n + 1] for k in range(got_ref.shape[0])], jnp.add)
    value_ref[...] = dual - (dual_sum - dual) / others
    weighted_sums(log_n, relative, x_ref, y_ref, lx_ref, ly_ref, lc_ref, phi_ref, gamma_ref, core_ref, out_ref, xs_ref, xa_ref, aug_ref)


def finish(got_ref, out_ref):
    total = sum_received(got_ref)
    denom = on_diagonal(total[2 * SHARE : 2 * SHARE + 1])
    out_ref[:, 0:128] = total[0:SHARE] / denom
    out_ref[:, 128:256] = total[SHARE : 2 * SHARE] / denom


def call(body, outs, args, scratch=(), smem=(), anywhere=(), flops=0, limit=40):
    vmem = pl.BlockSpec(memory_space=pltpu.VMEM)
    specs = [vmem for _ in args]
    for k in smem:
        specs[k] = pl.BlockSpec(memory_space=pltpu.SMEM)
    for k in anywhere:
        specs[k] = pl.BlockSpec(memory_space=pl.ANY)
    outs = [s if hasattr(s, "dtype") else jax.ShapeDtypeStruct(s, jnp.float32) for s in outs]
    return pl.pallas_call(
        body,
        out_shape=outs,
        in_specs=specs,
        out_specs=[vmem for _ in outs],
        scratch_shapes=list(scratch),
        compiler_params=pltpu.CompilerParams(vmem_limit_bytes=int(limit * 2**20)),
        cost_estimate=pl.CostEstimate(flops=flops, bytes_accessed=2**20, transcendentals=flops // 512),
    )(*args)


def exchange(x, axis, groups=None):
    return lax.all_to_all(x, axis, 0, 0, axis_index_groups=groups, tiled=True)


def on_device(train_embed, train_label, target_embed, target_label, label_cost):
    m_dev, width = train_embed.shape
    n_dev = target_embed.shape[0]
    trains = lax.axis_size("train")
    targets = lax.axis_size("target")
    log_m = EPS * math.log(m_dev * trains)
    log_n = EPS * math.log(n_dev * targets)
    data = (
        train_embed,
        target_embed,
        train_label.reshape(1, m_dev),
        target_label.reshape(1, n_dev),
        label_cost,
    )
    row_m, row_n = (1, m_dev), (1, n_dev)
    tile_m, tile_n = (m_dev // 128, 128), (n_dev // 128, 128)
    flops = 2 * m_dev * n_dev * 512

    def run(body, outs, tile, *args):
        return call(body, outs, args, scratch=[pltpu.VMEM(tile, jnp.float32)], flops=flops)

    core = (lax.axis_index("target").astype(jnp.int32) & 1).reshape(1)
    local, sqx, sqy = call(
        rows_first,
        [(targets,) + tile_m, row_m, row_n],
        (*data, core),
        scratch=[pltpu.VMEM(tile_m, jnp.float32)]
        + [pltpu.VMEM(v.shape, v.dtype) for v in data]
        + [pltpu.SemaphoreType.DMA((len(data),))],
        anywhere=range(len(data)),
        smem=(len(data),),
        flops=flops,
        limit=54,
    )
    got = exchange(local, "target")
    local, phi = run(
        functools.partial(columns_first, log_m), [(trains,) + tile_n, row_m], tile_n, *data, got
    )
    got = exchange(local, "train")
    local, gamma = run(
        functools.partial(rows_next, log_n), [(targets,) + tile_m, row_n], tile_m, *data, phi, got
    )
    got = exchange(local, "target")
    row_more = (1, n_dev + 128)
    local, phi = run(
        functools.partial(columns_next, log_m, log_n), [(trains,) + row_more, row_m], row_more, *data, phi, gamma, sqx, got
    )
    got = exchange(local, "train")
    half = targets // 2
    rows = SHARE * half
    scratch = [
        pltpu.VMEM((rows, width), jnp.bfloat16),
        pltpu.VMEM((rows, 128), jnp.bfloat16),
        pltpu.VMEM((m_dev, 128), jnp.float32),
    ]
    chunks = (half, CHUNK, 128)
    sent, gamma = call(
        functools.partial(project_sent, log_m, log_n, [2 * k + 1 for k in range(half)]),
        [chunks, row_n],
        (*data, phi, gamma, got, core),
        scratch=scratch, smem=(8,), flops=flops,
    )
    sent = lax.ppermute(sent, "target", [(t, t ^ 1) for t in range(targets)])
    kept, value, potential = call(
        functools.partial(project_kept, log_n, m_dev * trains - 1, [2 * k for k in range(half)]),
        [chunks, row_m, row_n],
        (*data, phi, gamma, sqx, sqy, got, core),
        scratch=scratch, smem=(10,), flops=flops,
    )
    groups = [[c + 2 * k for k in range(half)] for c in range(2)]
    got = exchange(kept + sent, "target", groups)
    (barycentre,) = call(finish, [(SHARE, width)], (got,))
    return (value.reshape(m_dev), potential.reshape(n_dev), barycentre)


def solution(mesh):
    return jax.shard_map(
        on_device,
        mesh=mesh,
        in_specs=(P("train", None), P("train"), P("target", None), P("target"), P()),
        out_specs=(P("train"), P("target"), P(("train", "target"), None)),
        check_vma=False,
    )
```

```python
import functools
import math

import jax
import jax.numpy as jnp
from jax import lax
from jax.experimental import pallas as pl
from jax.experimental.pallas import tpu as pltpu
from jax.sharding import PartitionSpec as P

EPS = 0.05
SCALE = 128.0
KAPPA = math.log2(math.e) / EPS / SCALE
LANES = 256
SHARE = 32
NEAR = 4
CHUNK = 2 * SHARE + 8


def pieces(v):
    hi = v.astype(jnp.bfloat16).astype(jnp.float32)
    rest = v - hi
    mid = rest.astype(jnp.bfloat16).astype(jnp.float32)
    lo = (rest - mid).astype(jnp.bfloat16).astype(jnp.float32)
    return hi, mid, lo


def tail(first, second):
    n = first[0].shape[1]
    row = lax.broadcasted_iota(jnp.int32, (8, n), 0)
    out = jnp.zeros((8, n), jnp.float32)
    for k, v in enumerate(first + second):
        out = jnp.where(row == k, v, out)
    return out


def ones_like3(v):
    return (jnp.ones_like(v),) * 3


def train_rows(label, phi):
    m = label.shape[1]
    onehot = (lax.broadcasted_iota(jnp.int32, (8, m), 0) == label).astype(jnp.float32)
    last = tail(ones_like3(phi), pieces(phi * SCALE))
    return jnp.concatenate([onehot, onehot, onehot, last], axis=0)


def target_rows(label, gamma, label_cost):
    n = label.shape[1]
    table = jnp.zeros((8, n), jnp.float32)
    for b in range(8):
        table = jnp.where(label == b, label_cost[:, b : b + 1], table)
    last = tail(pieces(gamma * SCALE), ones_like3(gamma))
    return jnp.concatenate(list(pieces(table * -SCALE)) + [last], axis=0)


def as_columns(rows):
    pad = jnp.zeros((96, rows.shape[1]), jnp.float32)
    return jnp.concatenate([rows, pad], axis=0).T.astype(jnp.bfloat16)


def as_rows(rows):
    pad = jnp.zeros((96, rows.shape[1]), jnp.float32)
    return jnp.concatenate([rows, pad], axis=0).astype(jnp.bfloat16)


def dot_nt(a, b):
    return lax.dot_general(a, b, (((1,), (1,)), ((), ())), preferred_element_type=jnp.float32)


def dot_nn(a, b):
    return lax.dot_general(a, b, (((1,), (0,)), ((), ())), preferred_element_type=jnp.float32)


def square_sums(v):
    sq = jnp.square(v.astype(jnp.float32))
    hi = sq.astype(jnp.bfloat16)
    lo = (sq - hi.astype(jnp.float32)).astype(jnp.bfloat16)
    ones = jnp.ones((8, v.shape[1]), jnp.bfloat16)
    return (dot_nt(ones, hi) + dot_nt(ones, lo))[0:1] / v.shape[1]


def reduce_over_sub(sub, sub_columns, lane_ref, lane_rows, at_ref, shifted):
    n = lane_ref.shape[0]
    for k in range(n // LANES):
        at = pl.ds(k * LANES, LANES)
        t = dot_nt(sub, lane_ref[at, :]) + dot_nn(sub_columns, lane_rows[:, k * LANES : (k + 1) * LANES])
        if shifted:
            out = jnp.sum(jnp.exp2(t * KAPPA), axis=0, keepdims=True)
        else:
            top = jnp.max(t, axis=0, keepdims=True)
            total = jnp.sum(jnp.exp2((t - top) * KAPPA), axis=0, keepdims=True)
            out = top * (1.0 / SCALE) + EPS * jnp.log(total)
        if at_ref.shape[0] == 1:
            at_ref[:, at] = out
            continue
        for r in range(LANES // 128):
            row = k * (LANES // 128) + r
            at_ref[row : row + 1, :] = out[:, r * 128 : (r + 1) * 128]


def to_everyone(v, out_ref):
    for k in range(out_ref.shape[0]):
        out_ref[k] = v


def in_lanes(v):
    return jnp.concatenate([v[k : k + 1] for k in range(v.shape[0])], axis=1)


def tree(parts, combine):
    while len(parts) > 1:
        parts = [combine(parts[k], parts[k + 1]) for k in range(0, len(parts), 2)]
    return parts[0]


def lse(parts):
    top = tree(parts, jnp.maximum)
    total = tree([jnp.exp((part - top) * (1.0 / EPS)) for part in parts], jnp.add)
    return top + EPS * jnp.log(total)


def lse_received(ref):
    return in_lanes(lse([ref[k] for k in range(ref.shape[0])]))


def sum_received(ref):
    return tree([ref[k] for k in range(ref.shape[0])], jnp.add)


def fetch(pairs, sems):
    copies = [pltpu.make_async_copy(src, dst, sems.at[k]) for k, (src, dst) in enumerate(pairs)]
    for copy in copies:
        copy.start()
    return copies


def wait_all(copies):
    for copy in copies:
        copy.wait()


def rows_first(
    x_any, y_any, lx_any, ly_any, lc_any, near_ref,
    wide_any, out_ref, sqx_ref, sqy_ref, at_ref, x_ref, y_ref, lx_ref, ly_ref, lc_ref, wide_ref, sems,
):
    pairs = [(ly_any, ly_ref), (lc_any, lc_ref), (lx_any, lx_ref), (y_any, y_ref), (x_any, x_ref)]
    copies = fetch(pairs, sems)
    wait_all(copies[:3])
    rows = as_rows(train_rows(lx_ref[...], jnp.zeros(lx_ref.shape, jnp.float32)))
    copies[3].wait()
    y = y_ref[...]
    n, width = y.shape
    wide_ref[0:n, :] = y.astype(jnp.float32)
    wide_ref[n : n + 8, :] = jnp.zeros((8, width), jnp.float32)
    label = ly_ref[...].astype(jnp.float32)
    for k in range(n // width):
        wide_ref[n + k : n + k + 1, :] = label[:, k * width : (k + 1) * width]
    wide = pltpu.make_async_copy(wide_ref, wide_any, sems.at[len(pairs)])
    wide.start()
    sq = square_sums(y)
    sqy_ref[...] = sq
    columns = as_columns(target_rows(ly_ref[...], -sq, lc_ref[...]))
    copies[4].wait()
    sqx_ref[...] = square_sums(x_ref[...])
    reduce_over_sub(y, columns, x_ref, rows, at_ref, False)
    to_everyone(at_ref[...], out_ref)
    wide.wait()


def columns_first(
    log_m, x_ref, y_ref, lx_ref, ly_ref, lc_ref, got_ref, out_ref, phi_ref, at_ref
):
    phi = -log_m - lse_received(got_ref)
    phi_ref[...] = phi
    columns = as_columns(train_rows(lx_ref[...], phi))
    rows = as_rows(target_rows(ly_ref[...], jnp.zeros(ly_ref.shape, jnp.float32), lc_ref[...]))
    reduce_over_sub(x_ref[...], columns, y_ref, rows, at_ref, False)
    to_everyone(at_ref[...], out_ref)


def rows_next(
    log_n, x_ref, y_ref, lx_ref, ly_ref, lc_ref, phi_ref, got_ref, out_ref, gamma_ref, at_ref
):
    gamma = -log_n - lse_received(got_ref)
    gamma_ref[...] = gamma
    columns = as_columns(target_rows(ly_ref[...], gamma, lc_ref[...]))
    rows = as_rows(train_rows(lx_ref[...], phi_ref[...] + log_n))
    reduce_over_sub(y_ref[...], columns, x_ref, rows, at_ref, True)
    to_everyone(at_ref[...], out_ref)


def columns_next(
    log_m, log_n, x_ref, y_ref, lx_ref, ly_ref, lc_ref, phi_ref, gamma_ref, sqx_ref, got_ref,
    out_ref, new_ref, at_ref,
):
    n = y_ref.shape[0]
    phi = phi_ref[...] + log_n - log_m - EPS * jnp.log(in_lanes(sum_received(got_ref)))
    new_ref[...] = phi
    columns = as_columns(train_rows(lx_ref[...], phi))
    rows = as_rows(target_rows(ly_ref[...], gamma_ref[...] + log_m, lc_ref[...]))
    reduce_over_sub(x_ref[...], columns, y_ref, rows, at_ref, True)
    at_ref[:, 0:n] = EPS * jnp.log(at_ref[:, 0:n]) - (gamma_ref[...] + log_m)
    dual_sum = jnp.sum(phi + sqx_ref[...], axis=1, keepdims=True)
    at_ref[:, n : n + 128] = jnp.broadcast_to(dual_sum, (1, 128))
    to_everyone(at_ref[...], out_ref)


def on_diagonal(v):
    shape = (SHARE, 128)
    row, column = (lax.broadcasted_iota(jnp.int32, shape, k) for k in range(2))
    axis = 0 if v.shape[0] == SHARE else 1
    return jnp.sum(jnp.where(row == column, v, 0.0), axis=axis, keepdims=True)


def weighted_sums(
    shift, other, x_ref, y_ref, lx_ref, ly_ref, lc_ref, wide_ref, phi_ref, gamma_ref, near_ref, out_ref, xs_ref, xa_ref, aug_ref
):
    n, width = y_ref.shape
    mine = near_ref[0] ^ other
    aug_ref[...] = as_columns(train_rows(lx_ref[...], phi_ref[...] + shift)).astype(jnp.float32)
    for k in range(out_ref.shape[0]):
        start = pl.multiple_of((NEAR * k + mine) * SHARE, SHARE)
        xs_ref[pl.ds(k * SHARE, SHARE), :] = x_ref[pl.ds(start, SHARE), :]
        xa_ref[pl.ds(k * SHARE, SHARE), :] = aug_ref[pl.ds(start, SHARE), :].astype(jnp.bfloat16)
    parts = [
        (y_ref[...], ly_ref[...]),
        (wide_ref[0:n, :].astype(jnp.bfloat16), in_lanes(wide_ref[n : n + n // width, :])),
    ]
    numer, denom = 0.0, 0.0
    for p, (y, label) in enumerate(parts):
        rows = as_rows(target_rows(label, gamma_ref[p : p + 1, :], lc_ref[...]))
        t = dot_nt(xs_ref[...], y) + dot_nn(xa_ref[...], rows)
        w = jnp.exp2(t * KAPPA).astype(jnp.bfloat16)
        denom = denom + jnp.sum(w.astype(jnp.float32), axis=1, keepdims=True)
        numer = numer + dot_nn(w, y)
    for k in range(out_ref.shape[0]):
        part = slice(k * SHARE, (k + 1) * SHARE)
        out_ref[k, 0:SHARE, :] = numer[part, 0:128]
        out_ref[k, SHARE : 2 * SHARE, :] = numer[part, 128:256]
        out_ref[k, 2 * SHARE : CHUNK, :] = jnp.broadcast_to(on_diagonal(denom[part]), (CHUNK - 2 * SHARE, 128))


def project_sent(
    log_n, x_ref, y_ref, lx_ref, ly_ref, lc_ref, wide_ref, phi_ref, got_ref, near_ref,
    out_ref, gamma_ref, xs_ref, xa_ref, aug_ref,
):
    n = gamma_ref.shape[1]
    half = got_ref.shape[0] // 2
    side = near_ref[0] >> 1
    first, second = (
        -log_n - lse([got_ref[half * p + k, :, 0:n] for k in range(half)]) for p in range(2)
    )
    gamma_ref[0:1, :] = jnp.where(side == 0, first, second)
    gamma_ref[1:2, :] = jnp.where(side == 0, second, first)
    weighted_sums(
        log_n, 1, x_ref, y_ref, lx_ref, ly_ref, lc_ref, wide_ref, phi_ref, gamma_ref, near_ref, out_ref, xs_ref, xa_ref, aug_ref
    )


def project_kept(
    log_n, others, x_ref, y_ref, lx_ref, ly_ref, lc_ref, wide_ref, phi_ref, gamma_ref, sqx_ref, sqy_ref, got_ref, near_ref,
    out_ref, value_ref, potential_ref, xs_ref, xa_ref, aug_ref,
):
    n = gamma_ref.shape[1]
    potential_ref[...] = gamma_ref[0:1, :] + sqy_ref[...]
    dual = phi_ref[...] + sqx_ref[...]
    dual_sum = tree([got_ref[k, :, n : n + 1] for k in range(got_ref.shape[0] // 2)], jnp.add)
    value_ref[...] = dual - (dual_sum - dual) / others
    weighted_sums(
        log_n, 0, x_ref, y_ref, lx_ref, ly_ref, lc_ref, wide_ref, phi_ref, gamma_ref, near_ref, out_ref, xs_ref, xa_ref, aug_ref
    )


def finish(got_ref, out_ref):
    total = sum_received(got_ref)
    denom = on_diagonal(total[2 * SHARE : 2 * SHARE + 1])
    out_ref[:, 0:128] = total[0:SHARE] / denom
    out_ref[:, 128:256] = total[SHARE : 2 * SHARE] / denom


def call(body, outs, args, scratch=(), smem=(), anywhere=(), anywhere_out=(), flops=0, limit=40):
    vmem = pl.BlockSpec(memory_space=pltpu.VMEM)
    specs = [vmem for _ in args]
    for k in smem:
        specs[k] = pl.BlockSpec(memory_space=pltpu.SMEM)
    for k in anywhere:
        specs[k] = pl.BlockSpec(memory_space=pl.ANY)
    out_specs = [pl.BlockSpec(memory_space=pl.ANY) if k in anywhere_out else vmem for k in range(len(outs))]
    outs = [s if hasattr(s, "dtype") else jax.ShapeDtypeStruct(s, jnp.float32) for s in outs]
    return pl.pallas_call(
        body,
        out_shape=outs,
        in_specs=specs,
        out_specs=out_specs,
        scratch_shapes=list(scratch),
        compiler_params=pltpu.CompilerParams(vmem_limit_bytes=int(limit * 2**20)),
        cost_estimate=pl.CostEstimate(flops=flops, bytes_accessed=2**20, transcendentals=flops // 512),
    )(*args)


def exchange(x, axis, groups=None):
    return lax.all_to_all(x, axis, 0, 0, axis_index_groups=groups, tiled=True)


def on_device(train_embed, train_label, target_embed, target_label, label_cost):
    m_dev, width = train_embed.shape
    n_dev = target_embed.shape[0]
    trains = lax.axis_size("train")
    targets = lax.axis_size("target")
    log_m = EPS * math.log(m_dev * trains)
    log_n = EPS * math.log(n_dev * targets)
    data = (
        train_embed,
        target_embed,
        train_label.reshape(1, m_dev),
        target_label.reshape(1, n_dev),
        label_cost,
    )
    row_m, row_n = (1, m_dev), (1, n_dev)
    tile_m, tile_n = (m_dev // 128, 128), (n_dev // 128, 128)
    flops = 2 * m_dev * n_dev * 512

    def run(body, outs, tile, *args):
        return call(body, outs, args, scratch=[pltpu.VMEM(tile, jnp.float32)], flops=flops)

    near = (lax.axis_index("target").astype(jnp.int32) % NEAR).reshape(1)
    wide_shape = (n_dev + 8, width)
    wide, local, sqx, sqy = call(
        rows_first,
        [wide_shape, (targets,) + tile_m, row_m, row_n],
        (*data, near),
        scratch=[pltpu.VMEM(tile_m, jnp.float32)]
        + [pltpu.VMEM(v.shape, v.dtype) for v in data]
        + [pltpu.VMEM(wide_shape, jnp.float32), pltpu.SemaphoreType.DMA((len(data) + 1,))],
        anywhere=range(len(data)),
        anywhere_out=(0,),
        smem=(len(data),),
        flops=flops,
        limit=54,
    )
    wide = lax.ppermute(wide, "target", [(t, t ^ 2) for t in range(targets)])
    got = exchange(local, "target")
    local, phi = run(
        functools.partial(columns_first, log_m), [(trains,) + tile_n, row_m], tile_n, *data, got
    )
    got = exchange(local, "train")
    local, gamma = run(
        functools.partial(rows_next, log_n), [(targets,) + tile_m, row_n], tile_m, *data, phi, got
    )
    got = exchange(local, "target")
    row_more = (1, n_dev + 128)
    local, phi = run(
        functools.partial(columns_next, log_m, log_n),
        [(2 * trains,) + row_more, row_m],
        row_more, *data, phi, gamma, sqx, got,
    )
    sides = [
        [a * targets + NEAR * z + 2 * side + core for side in range(2) for a in range(trains)]
        for z in range(targets // NEAR)
        for core in range(2)
    ]
    got = exchange(local, ("train", "target"), sides)

    depth = targets // NEAR
    scratch = [
        pltpu.VMEM((SHARE * depth, width), jnp.bfloat16),
        pltpu.VMEM((SHARE * depth, 128), jnp.bfloat16),
        pltpu.VMEM((m_dev, 128), jnp.float32),
    ]
    chunks = (depth, CHUNK, 128)
    sent, gamma = call(
        functools.partial(project_sent, log_n),
        [chunks, (2, n_dev)],
        (*data, wide, phi, got, near),
        scratch=scratch, smem=(8,), flops=flops,
    )
    sent = lax.ppermute(sent, "target", [(t, t ^ 1) for t in range(targets)])
    kept, value, potential = call(
        functools.partial(project_kept, log_n, m_dev * trains - 1),
        [chunks, row_m, row_n],
        (*data, wide, phi, gamma, sqx, sqy, got, near),
        scratch=scratch, smem=(11,), flops=flops,
    )
    groups = [[NEAR * z + q for z in range(depth)] for q in range(NEAR)]
    got = exchange(kept + sent, "target", groups)
    (barycentre,) = call(finish, [(SHARE, width)], (got,))
    return (value.reshape(m_dev), potential.reshape(n_dev), barycentre)


def solution(mesh):
    return jax.shard_map(
        on_device,
        mesh=mesh,
        in_specs=(P("train", None), P("train"), P("target", None), P("target"), P()),
        out_specs=(P("train"), P("target"), P(("train", "target"), None)),
        check_vma=False,
    )
```

```python
import functools
import math

import jax
import jax.numpy as jnp
from jax import lax
from jax.experimental import pallas as pl
from jax.experimental.pallas import tpu as pltpu
from jax.sharding import PartitionSpec as P

EPS = 0.05
SCALE = 128.0
KAPPA = math.log2(math.e) / EPS / SCALE
LOG2 = math.log2(math.e) / EPS
LANES = 256
SHARE = 32
CHUNK = 2 * SHARE + 8


def pieces(v):
    hi = v.astype(jnp.bfloat16).astype(jnp.float32)
    rest = v - hi
    mid = rest.astype(jnp.bfloat16).astype(jnp.float32)
    lo = (rest - mid).astype(jnp.bfloat16).astype(jnp.float32)
    return hi, mid, lo


def tail(first, second):
    n = first[0].shape[1]
    row = lax.broadcasted_iota(jnp.int32, (8, n), 0)
    out = jnp.zeros((8, n), jnp.float32)
    for k, v in enumerate(first + second):
        out = jnp.where(row == k, v, out)
    return out


def ones_like3(v):
    return (jnp.ones_like(v),) * 3


def train_rows(label, phi):
    m = label.shape[1]
    onehot = (lax.broadcasted_iota(jnp.int32, (8, m), 0) == label).astype(jnp.float32)
    last = tail(ones_like3(phi), pieces(phi * SCALE))
    return jnp.concatenate([onehot, onehot, onehot, last], axis=0)


def target_rows(label, gamma, label_cost):
    n = label.shape[1]
    table = jnp.zeros((8, n), jnp.float32)
    for b in range(8):
        table = jnp.where(label == b, label_cost[:, b : b + 1], table)
    last = tail(pieces(gamma * SCALE), ones_like3(gamma))
    return jnp.concatenate(list(pieces(table * -SCALE)) + [last], axis=0)


def as_columns(rows):
    pad = jnp.zeros((96, rows.shape[1]), jnp.float32)
    return jnp.concatenate([rows, pad], axis=0).T.astype(jnp.bfloat16)


def as_rows(rows):
    pad = jnp.zeros((96, rows.shape[1]), jnp.float32)
    return jnp.concatenate([rows, pad], axis=0).astype(jnp.bfloat16)


def dot_nt(a, b):
    return lax.dot_general(a, b, (((1,), (1,)), ((), ())), preferred_element_type=jnp.float32)


def dot_nn(a, b):
    return lax.dot_general(a, b, (((1,), (0,)), ((), ())), preferred_element_type=jnp.float32)


def square_sums(v):
    sq = jnp.square(v.astype(jnp.float32))
    hi = sq.astype(jnp.bfloat16)
    lo = (sq - hi.astype(jnp.float32)).astype(jnp.bfloat16)
    ones = jnp.ones((8, v.shape[1]), jnp.bfloat16)
    return (dot_nt(ones, hi) + dot_nt(ones, lo))[0:1] / v.shape[1]


def reduce_over_sub(sub, sub_columns, lane_ref, lane_rows, at_ref):
    n = lane_ref.shape[0]
    for k in range(n // LANES):
        at = slice(k * LANES, (k + 1) * LANES)
        t = dot_nt(sub, lane_ref[at, :]) + dot_nn(sub_columns, lane_rows[:, at])
        top = jnp.max(t, axis=0, keepdims=True)
        total = jnp.sum(jnp.exp2((t - top) * KAPPA), axis=0, keepdims=True)
        out = top * (1.0 / SCALE) + EPS * jnp.log(total)
        for r in range(LANES // 128):
            row = k * (LANES // 128) + r
            at_ref[row : row + 1, :] = out[:, r * 128 : (r + 1) * 128]


def to_everyone(v, out_ref):
    for k in range(out_ref.shape[0]):
        out_ref[k] = v


def in_lanes(v):
    return jnp.concatenate([v[k : k + 1] for k in range(v.shape[0])], axis=1)


def tree(parts, combine):
    while len(parts) > 1:
        parts = [combine(parts[k], parts[k + 1]) for k in range(0, len(parts), 2)]
    return parts[0]


def lse_received(ref):
    parts = [ref[k] for k in range(ref.shape[0])]
    top = tree(parts, jnp.maximum)
    total = tree([jnp.exp((part - top) * (1.0 / EPS)) for part in parts], jnp.add)
    return in_lanes(top + EPS * jnp.log(total))


def sum_received(ref):
    return tree([ref[k] for k in range(ref.shape[0])], jnp.add)


def fetch(pairs, sems):
    copies = [pltpu.make_async_copy(src, dst, sems.at[k]) for k, (src, dst) in enumerate(pairs)]
    for copy in copies:
        copy.start()
    return copies


def wait_all(copies):
    for copy in copies:
        copy.wait()


def rows_first(
    x_any, y_any, lx_any, ly_any, lc_any, core_ref,
    out_ref, sqx_ref, sqy_ref, at_ref, x_ref, y_ref, lx_ref, ly_ref, lc_ref, sems,
):
    pairs = [(ly_any, ly_ref), (lc_any, lc_ref), (lx_any, lx_ref), (y_any, y_ref), (x_any, x_ref)]
    copies = fetch(pairs, sems)
    wait_all(copies[:3])
    rows = as_rows(train_rows(lx_ref[...], jnp.zeros(lx_ref.shape, jnp.float32)))
    copies[3].wait()
    y = y_ref[...]
    sq = square_sums(y)
    sqy_ref[...] = sq
    columns = as_columns(target_rows(ly_ref[...], -sq, lc_ref[...]))
    copies[4].wait()
    sqx_ref[...] = square_sums(x_ref[...])
    reduce_over_sub(y, columns, x_ref, rows, at_ref)
    to_everyone(at_ref[...], out_ref)


def scores(x_ref, y_ref, lx_ref, ly_ref, lc_ref, after_any, out_ref):
    zero_m, zero_n = (jnp.zeros(ref.shape, jnp.float32) for ref in (lx_ref, ly_ref))
    x = x_ref[...]
    columns = as_columns(train_rows(lx_ref[...], zero_m))
    rows = as_rows(target_rows(ly_ref[...], zero_n, lc_ref[...]))
    for k in range(y_ref.shape[0] // LANES):
        at = slice(k * LANES, (k + 1) * LANES)
        out_ref[:, at] = (dot_nt(x, y_ref[at, :]) + dot_nn(columns, rows[:, at])) * KAPPA


def in_rows(v):
    return jnp.broadcast_to(v, (128, v.shape[1])).T


def columns_first(log_m, t_ref, got_ref, out_ref, phi_ref, at_ref):
    phi = -log_m - lse_received(got_ref)
    phi_ref[...] = phi
    down = in_rows(phi * LOG2)
    for k in range(t_ref.shape[1] // 128):
        t = t_ref[:, k * 128 : (k + 1) * 128] + down
        top = jnp.max(t, axis=0, keepdims=True)
        total = jnp.sum(jnp.exp2(t - top), axis=0, keepdims=True)
        at_ref[k : k + 1, :] = top * (1.0 / LOG2) + EPS * jnp.log(total)
    to_everyone(at_ref[...], out_ref)


def rows_next(log_n, t_ref, phi_ref, got_ref, out_ref, gamma_ref, at_ref):
    gamma = -log_n - lse_received(got_ref)
    gamma_ref[...] = gamma
    down = in_rows((phi_ref[...] + log_n) * LOG2)
    across = gamma * LOG2
    for k in range(t_ref.shape[0] // 128):
        rows = slice(k * 128, (k + 1) * 128)
        total = 0.0
        for j in range(t_ref.shape[1] // 128):
            at = slice(j * 128, (j + 1) * 128)
            total = total + jnp.exp2(t_ref[rows, at] + down[rows] + across[:, at])
        at_ref[k : k + 1, :] = jnp.sum(total.T, axis=0, keepdims=True)
    to_everyone(at_ref[...], out_ref)


def columns_next(log_m, log_n, t_ref, phi_ref, gamma_ref, sqx_ref, got_ref, out_ref, new_ref, at_ref):
    n = t_ref.shape[1]
    phi = phi_ref[...] + log_n - log_m - EPS * jnp.log(in_lanes(sum_received(got_ref)))
    new_ref[...] = phi
    down = in_rows(phi * LOG2)
    across = (gamma_ref[...] + log_m) * LOG2
    for k in range(n // 128):
        at = slice(k * 128, (k + 1) * 128)
        at_ref[:, at] = jnp.sum(jnp.exp2(t_ref[:, at] + down + across[:, at]), axis=0, keepdims=True)
    dual_sum = jnp.sum(phi + sqx_ref[...], axis=1, keepdims=True)
    at_ref[:, n : n + 128] = jnp.broadcast_to(dual_sum, (1, 128))
    to_everyone(at_ref[...], out_ref)


def on_diagonal(v):
    shape = (SHARE, 128)
    row, column = (lax.broadcasted_iota(jnp.int32, shape, k) for k in range(2))
    axis = 0 if v.shape[0] == SHARE else 1
    return jnp.sum(jnp.where(row == column, v, 0.0), axis=axis, keepdims=True)


def weighted_sums(shift, relative, t_ref, y_ref, phi_ref, gamma_ref, core_ref, out_ref, down_ref):
    core = core_ref[0]
    n = t_ref.shape[1]
    down_ref[...] = in_rows((phi_ref[...] + shift) * LOG2)
    across = gamma_ref[...] * LOG2
    y = y_ref[...]
    per = min(8, len(relative))
    for b in range(len(relative) // per):
        weights = []
        for k in range(per):
            start = pl.multiple_of((core ^ relative[b * per + k]) * SHARE, SHARE)
            at = pl.ds(start, SHARE)
            down = jnp.concatenate([down_ref[at, :]] * (n // 128), axis=1)
            weights.append(jnp.exp2(t_ref[at, :] + down + across).astype(jnp.bfloat16))
        w = jnp.concatenate(weights, axis=0)
        denom = jnp.sum(w.astype(jnp.float32), axis=1, keepdims=True)
        numer = dot_nn(w, y)
        for k in range(per):
            part, chunk = slice(k * SHARE, (k + 1) * SHARE), b * per + k
            out_ref[chunk, 0:SHARE, :] = numer[part, 0:128]
            out_ref[chunk, SHARE : 2 * SHARE, :] = numer[part, 128:256]
            out_ref[chunk, 2 * SHARE : CHUNK, :] = jnp.broadcast_to(on_diagonal(denom[part]), (CHUNK - 2 * SHARE, 128))


def project_sent(
    log_m, log_n, relative, t_ref, y_ref, phi_ref, gamma_ref, got_ref, core_ref, out_ref, new_ref, down_ref
):
    total = sum_received(got_ref)
    new_ref[...] = gamma_ref[...] + log_m - log_n - EPS * jnp.log(total[:, 0 : new_ref.shape[1]])
    weighted_sums(log_n, relative, t_ref, y_ref, phi_ref, new_ref, core_ref, out_ref, down_ref)


def project_kept(
    log_n, others, relative, t_ref, y_ref, phi_ref, gamma_ref, sqx_ref, sqy_ref, got_ref, core_ref,
    out_ref, value_ref, potential_ref, down_ref,
):
    n = gamma_ref.shape[1]
    potential_ref[...] = gamma_ref[...] + sqy_ref[...]
    dual = phi_ref[...] + sqx_ref[...]
    dual_sum = tree([got_ref[k, :, n : n + 1] for k in range(got_ref.shape[0])], jnp.add)
    value_ref[...] = dual - (dual_sum - dual) / others
    weighted_sums(log_n, relative, t_ref, y_ref, phi_ref, gamma_ref, core_ref, out_ref, down_ref)


def finish(got_ref, out_ref):
    total = sum_received(got_ref)
    denom = on_diagonal(total[2 * SHARE : 2 * SHARE + 1])
    out_ref[:, 0:128] = total[0:SHARE] / denom
    out_ref[:, 128:256] = total[SHARE : 2 * SHARE] / denom


def call(body, outs, args, scratch=(), smem=(), anywhere=(), flops=0, limit=40):
    vmem = pl.BlockSpec(memory_space=pltpu.VMEM)
    specs = [vmem for _ in args]
    for k in smem:
        specs[k] = pl.BlockSpec(memory_space=pltpu.SMEM)
    for k in anywhere:
        specs[k] = pl.BlockSpec(memory_space=pl.ANY)
    outs = [s if hasattr(s, "dtype") else jax.ShapeDtypeStruct(s, jnp.float32) for s in outs]
    return pl.pallas_call(
        body,
        out_shape=outs,
        in_specs=specs,
        out_specs=[vmem for _ in outs],
        scratch_shapes=list(scratch),
        compiler_params=pltpu.CompilerParams(vmem_limit_bytes=int(limit * 2**20)),
        cost_estimate=pl.CostEstimate(flops=flops, bytes_accessed=2**20, transcendentals=flops // 512),
    )(*args)


def exchange(x, axis, groups=None):
    return lax.all_to_all(x, axis, 0, 0, axis_index_groups=groups, tiled=True)


def on_device(train_embed, train_label, target_embed, target_label, label_cost):
    m_dev, width = train_embed.shape
    n_dev = target_embed.shape[0]
    trains = lax.axis_size("train")
    targets = lax.axis_size("target")
    log_m = EPS * math.log(m_dev * trains)
    log_n = EPS * math.log(n_dev * targets)
    data = (
        train_embed,
        target_embed,
        train_label.reshape(1, m_dev),
        target_label.reshape(1, n_dev),
        label_cost,
    )
    row_m, row_n = (1, m_dev), (1, n_dev)
    tile_m, tile_n = (m_dev // 128, 128), (n_dev // 128, 128)
    flops = 2 * m_dev * n_dev * 512

    def run(body, outs, tile, *args):
        return call(body, outs, args, scratch=[pltpu.VMEM(tile, jnp.float32)], flops=flops)

    core = (lax.axis_index("target").astype(jnp.int32) & 1).reshape(1)
    local, sqx, sqy = call(
        rows_first,
        [(targets,) + tile_m, row_m, row_n],
        (*data, core),
        scratch=[pltpu.VMEM(tile_m, jnp.float32)]
        + [pltpu.VMEM(v.shape, v.dtype) for v in data]
        + [pltpu.SemaphoreType.DMA((len(data),))],
        anywhere=range(len(data)),
        smem=(len(data),),
        flops=flops,
        limit=54,
    )
    got = exchange(local, "target")
    (t,) = call(scores, [(m_dev, n_dev)], (*data, sqx), anywhere=(len(data),), flops=flops)
    local, phi = run(functools.partial(columns_first, log_m), [(trains,) + tile_n, row_m], tile_n, t, got)
    got = exchange(local, "train")
    local, gamma = run(functools.partial(rows_next, log_n), [(targets,) + tile_m, row_n], tile_m, t, phi, got)
    got = exchange(local, "target")
    row_more = (1, n_dev + 128)
    local, phi = run(
        functools.partial(columns_next, log_m, log_n), [(trains,) + row_more, row_m], row_more, t, phi, gamma, sqx, got
    )
    got = exchange(local, "train")

    half = targets // 2
    scratch = [pltpu.VMEM((m_dev, 128), jnp.float32)]
    chunks = (half, CHUNK, 128)
    sent, gamma = call(
        functools.partial(project_sent, log_m, log_n, [2 * k + 1 for k in range(half)]),
        [chunks, row_n],
        (t, target_embed, phi, gamma, got, core),
        scratch=scratch, smem=(5,), flops=flops,
    )
    sent = lax.ppermute(sent, "target", [(t, t ^ 1) for t in range(targets)])
    kept, value, potential = call(
        functools.partial(project_kept, log_n, m_dev * trains - 1, [2 * k for k in range(half)]),
        [chunks, row_m, row_n],
        (t, target_embed, phi, gamma, sqx, sqy, got, core),
        scratch=scratch, smem=(7,), flops=flops,
    )
    groups = [[c + 2 * k for k in range(half)] for c in range(2)]
    got = exchange(kept + sent, "target", groups)
    (barycentre,) = call(finish, [(SHARE, width)], (got,))
    return (value.reshape(m_dev), potential.reshape(n_dev), barycentre)


def solution(mesh):
    return jax.shard_map(
        on_device,
        mesh=mesh,
        in_specs=(P("train", None), P("train"), P("target", None), P("target"), P()),
        out_specs=(P("train"), P("target"), P(("train", "target"), None)),
        check_vma=False,
    )
```

```python
import functools
import math

import jax
import jax.numpy as jnp
from jax import lax
from jax.experimental import pallas as pl
from jax.experimental.pallas import tpu as pltpu
from jax.sharding import PartitionSpec as P

EPS = 0.05
SCALE = 128.0
KAPPA = math.log2(math.e) / EPS / SCALE
LOG2 = math.log2(math.e) / EPS
LANES = 256
SHARE = 32
CHUNK = 2 * SHARE + 8


def pieces(v):
    hi = v.astype(jnp.bfloat16).astype(jnp.float32)
    rest = v - hi
    mid = rest.astype(jnp.bfloat16).astype(jnp.float32)
    lo = (rest - mid).astype(jnp.bfloat16).astype(jnp.float32)
    return hi, mid, lo


def tail(first, second):
    n = first[0].shape[1]
    row = lax.broadcasted_iota(jnp.int32, (8, n), 0)
    out = jnp.zeros((8, n), jnp.float32)
    for k, v in enumerate(first + second):
        out = jnp.where(row == k, v, out)
    return out


def ones_like3(v):
    return (jnp.ones_like(v),) * 3


def train_rows(label, phi):
    m = label.shape[1]
    onehot = (lax.broadcasted_iota(jnp.int32, (8, m), 0) == label).astype(jnp.float32)
    last = tail(ones_like3(phi), pieces(phi * SCALE))
    return jnp.concatenate([onehot, onehot, onehot, last], axis=0)


def target_rows(label, gamma, label_cost):
    n = label.shape[1]
    table = jnp.zeros((8, n), jnp.float32)
    for b in range(8):
        table = jnp.where(label == b, label_cost[:, b : b + 1], table)
    last = tail(pieces(gamma * SCALE), ones_like3(gamma))
    return jnp.concatenate(list(pieces(table * -SCALE)) + [last], axis=0)


def as_columns(rows):
    pad = jnp.zeros((96, rows.shape[1]), jnp.float32)
    return jnp.concatenate([rows, pad], axis=0).T.astype(jnp.bfloat16)


def as_rows(rows):
    pad = jnp.zeros((96, rows.shape[1]), jnp.float32)
    return jnp.concatenate([rows, pad], axis=0).astype(jnp.bfloat16)


def dot_nt(a, b):
    return lax.dot_general(a, b, (((1,), (1,)), ((), ())), preferred_element_type=jnp.float32)


def dot_nn(a, b):
    return lax.dot_general(a, b, (((1,), (0,)), ((), ())), preferred_element_type=jnp.float32)


def square_sums(v):
    sq = jnp.square(v.astype(jnp.float32))
    hi = sq.astype(jnp.bfloat16)
    lo = (sq - hi.astype(jnp.float32)).astype(jnp.bfloat16)
    ones = jnp.ones((8, v.shape[1]), jnp.bfloat16)
    return (dot_nt(ones, hi) + dot_nt(ones, lo))[0:1] / v.shape[1]


def reduce_over_sub(sub, sub_columns, lane_ref, lane_rows, at_ref):
    n = lane_ref.shape[0]
    for k in range(n // LANES):
        at = slice(k * LANES, (k + 1) * LANES)
        t = dot_nt(sub, lane_ref[at, :]) + dot_nn(sub_columns, lane_rows[:, at])
        top = jnp.max(t, axis=0, keepdims=True)
        total = jnp.sum(jnp.exp2((t - top) * KAPPA), axis=0, keepdims=True)
        out = top * (1.0 / SCALE) + EPS * jnp.log(total)
        for r in range(LANES // 128):
            row = k * (LANES // 128) + r
            at_ref[row : row + 1, :] = out[:, r * 128 : (r + 1) * 128]


def to_everyone(v, out_ref):
    for k in range(out_ref.shape[0]):
        out_ref[k] = v


def in_lanes(v):
    return jnp.concatenate([v[k : k + 1] for k in range(v.shape[0])], axis=1)


def tree(parts, combine):
    while len(parts) > 1:
        parts = [combine(parts[k], parts[k + 1]) for k in range(0, len(parts), 2)]
    return parts[0]


def lse_received(ref):
    parts = [ref[k] for k in range(ref.shape[0])]
    top = tree(parts, jnp.maximum)
    total = tree([jnp.exp((part - top) * (1.0 / EPS)) for part in parts], jnp.add)
    return in_lanes(top + EPS * jnp.log(total))


def sum_received(ref):
    return tree([ref[k] for k in range(ref.shape[0])], jnp.add)


def fetch(pairs, sems):
    copies = [pltpu.make_async_copy(src, dst, sems.at[k]) for k, (src, dst) in enumerate(pairs)]
    for copy in copies:
        copy.start()
    return copies


def wait_all(copies):
    for copy in copies:
        copy.wait()


def rows_first(
    x_any, y_any, lx_any, ly_any, lc_any, core_ref,
    out_ref, sqx_ref, sqy_ref, at_ref, x_ref, y_ref, lx_ref, ly_ref, lc_ref, sems,
):
    pairs = [(ly_any, ly_ref), (lc_any, lc_ref), (lx_any, lx_ref), (y_any, y_ref), (x_any, x_ref)]
    copies = fetch(pairs, sems)
    wait_all(copies[:3])
    rows = as_rows(train_rows(lx_ref[...], jnp.zeros(lx_ref.shape, jnp.float32)))
    copies[3].wait()
    y = y_ref[...]
    sq = square_sums(y)
    sqy_ref[...] = sq
    columns = as_columns(target_rows(ly_ref[...], -sq, lc_ref[...]))
    copies[4].wait()
    sqx_ref[...] = square_sums(x_ref[...])
    reduce_over_sub(y, columns, x_ref, rows, at_ref)
    to_everyone(at_ref[...], out_ref)


def scores(x_ref, y_ref, lx_ref, ly_ref, lc_ref, after_any, out_ref):
    zero_m, zero_n = (jnp.zeros(ref.shape, jnp.float32) for ref in (lx_ref, ly_ref))
    x = x_ref[...]
    columns = as_columns(train_rows(lx_ref[...], zero_m))
    rows = as_rows(target_rows(ly_ref[...], zero_n, lc_ref[...]))
    for k in range(y_ref.shape[0] // LANES):
        at = slice(k * LANES, (k + 1) * LANES)
        out_ref[:, at] = (dot_nt(x, y_ref[at, :]) + dot_nn(columns, rows[:, at])) * KAPPA


def in_rows(v):
    return jnp.broadcast_to(v, (128, v.shape[1])).T


def columns_first(log_m, t_any, got_ref, t_ref, out_ref, phi_ref, at_ref, sems):
    blocks = [slice(k * 128, (k + 1) * 128) for k in range(t_ref.shape[1] // 128)]
    copies = fetch([(t_any.at[:, at], t_ref.at[:, at]) for at in blocks], sems)
    phi = -log_m - lse_received(got_ref)
    phi_ref[...] = phi
    down = in_rows(phi * LOG2)
    for k, at in enumerate(blocks):
        copies[k].wait()
        t = t_ref[:, at] + down
        top = jnp.max(t, axis=0, keepdims=True)
        total = jnp.sum(jnp.exp2(t - top), axis=0, keepdims=True)
        at_ref[k : k + 1, :] = top * (1.0 / LOG2) + EPS * jnp.log(total)
    to_everyone(at_ref[...], out_ref)


def rows_next(log_n, t_ref, phi_ref, got_ref, out_ref, gamma_ref, at_ref):
    gamma = -log_n - lse_received(got_ref)
    gamma_ref[...] = gamma
    down = in_rows((phi_ref[...] + log_n) * LOG2)
    across = gamma * LOG2
    for k in range(t_ref.shape[0] // 128):
        rows = slice(k * 128, (k + 1) * 128)
        total = 0.0
        for j in range(t_ref.shape[1] // 128):
            at = slice(j * 128, (j + 1) * 128)
            total = total + jnp.exp2(t_ref[rows, at] + down[rows] + across[:, at])
        at_ref[k : k + 1, :] = jnp.sum(total.T, axis=0, keepdims=True)
    to_everyone(at_ref[...], out_ref)


def columns_next(log_m, log_n, t_ref, phi_ref, gamma_ref, sqx_ref, got_ref, out_ref, new_ref, at_ref):
    n = t_ref.shape[1]
    phi = phi_ref[...] + log_n - log_m - EPS * jnp.log(in_lanes(sum_received(got_ref)))
    new_ref[...] = phi
    down = in_rows(phi * LOG2)
    across = (gamma_ref[...] + log_m) * LOG2
    for k in range(n // 128):
        at = slice(k * 128, (k + 1) * 128)
        at_ref[:, at] = jnp.sum(jnp.exp2(t_ref[:, at] + down + across[:, at]), axis=0, keepdims=True)
    dual_sum = jnp.sum(phi + sqx_ref[...], axis=1, keepdims=True)
    at_ref[:, n : n + 128] = jnp.broadcast_to(dual_sum, (1, 128))
    to_everyone(at_ref[...], out_ref)


def on_diagonal(v):
    shape = (SHARE, 128)
    row, column = (lax.broadcasted_iota(jnp.int32, shape, k) for k in range(2))
    axis = 0 if v.shape[0] == SHARE else 1
    return jnp.sum(jnp.where(row == column, v, 0.0), axis=axis, keepdims=True)


def weighted_sums(shift, relative, t_ref, y_ref, phi_ref, gamma_ref, core_ref, out_ref, down_ref):
    core = core_ref[0]
    n = t_ref.shape[1]
    down_ref[...] = in_rows((phi_ref[...] + shift) * LOG2)
    across = gamma_ref[...] * LOG2
    y = y_ref[...]
    per = min(8, len(relative))
    for b in range(len(relative) // per):
        weights = []
        for k in range(per):
            start = pl.multiple_of((core ^ relative[b * per + k]) * SHARE, SHARE)
            at = pl.ds(start, SHARE)
            down = jnp.concatenate([down_ref[at, :]] * (n // 128), axis=1)
            weights.append(jnp.exp2(t_ref[at, :] + down + across).astype(jnp.bfloat16))
        w = jnp.concatenate(weights, axis=0)
        denom = jnp.sum(w.astype(jnp.float32), axis=1, keepdims=True)
        numer = dot_nn(w, y)
        for k in range(per):
            part, chunk = slice(k * SHARE, (k + 1) * SHARE), b * per + k
            out_ref[chunk, 0:SHARE, :] = numer[part, 0:128]
            out_ref[chunk, SHARE : 2 * SHARE, :] = numer[part, 128:256]
            out_ref[chunk, 2 * SHARE : CHUNK, :] = jnp.broadcast_to(on_diagonal(denom[part]), (CHUNK - 2 * SHARE, 128))


def project_sent(
    log_m, log_n, relative, t_ref, y_ref, phi_ref, gamma_ref, got_ref, core_ref, out_ref, new_ref, down_ref
):
    total = sum_received(got_ref)
    new_ref[...] = gamma_ref[...] + log_m - log_n - EPS * jnp.log(total[:, 0 : new_ref.shape[1]])
    weighted_sums(log_n, relative, t_ref, y_ref, phi_ref, new_ref, core_ref, out_ref, down_ref)


def project_kept(
    log_n, others, relative, t_ref, y_ref, phi_ref, gamma_ref, sqx_ref, sqy_ref, got_ref, core_ref,
    out_ref, value_ref, potential_ref, down_ref,
):
    n = gamma_ref.shape[1]
    potential_ref[...] = gamma_ref[...] + sqy_ref[...]
    dual = phi_ref[...] + sqx_ref[...]
    dual_sum = tree([got_ref[k, :, n : n + 1] for k in range(got_ref.shape[0])], jnp.add)
    value_ref[...] = dual - (dual_sum - dual) / others
    weighted_sums(log_n, relative, t_ref, y_ref, phi_ref, gamma_ref, core_ref, out_ref, down_ref)


def finish(got_ref, out_ref):
    total = sum_received(got_ref)
    denom = on_diagonal(total[2 * SHARE : 2 * SHARE + 1])
    out_ref[:, 0:128] = total[0:SHARE] / denom
    out_ref[:, 128:256] = total[SHARE : 2 * SHARE] / denom


def call(body, outs, args, scratch=(), smem=(), anywhere=(), flops=0, limit=40):
    vmem = pl.BlockSpec(memory_space=pltpu.VMEM)
    specs = [vmem for _ in args]
    for k in smem:
        specs[k] = pl.BlockSpec(memory_space=pltpu.SMEM)
    for k in anywhere:
        specs[k] = pl.BlockSpec(memory_space=pl.ANY)
    outs = [s if hasattr(s, "dtype") else jax.ShapeDtypeStruct(s, jnp.float32) for s in outs]
    return pl.pallas_call(
        body,
        out_shape=outs,
        in_specs=specs,
        out_specs=[vmem for _ in outs],
        scratch_shapes=list(scratch),
        compiler_params=pltpu.CompilerParams(vmem_limit_bytes=int(limit * 2**20)),
        cost_estimate=pl.CostEstimate(flops=flops, bytes_accessed=2**20, transcendentals=flops // 512),
    )(*args)


def exchange(x, axis, groups=None):
    return lax.all_to_all(x, axis, 0, 0, axis_index_groups=groups, tiled=True)


def on_device(train_embed, train_label, target_embed, target_label, label_cost):
    m_dev, width = train_embed.shape
    n_dev = target_embed.shape[0]
    trains = lax.axis_size("train")
    targets = lax.axis_size("target")
    log_m = EPS * math.log(m_dev * trains)
    log_n = EPS * math.log(n_dev * targets)
    data = (
        train_embed,
        target_embed,
        train_label.reshape(1, m_dev),
        target_label.reshape(1, n_dev),
        label_cost,
    )
    row_m, row_n = (1, m_dev), (1, n_dev)
    tile_m, tile_n = (m_dev // 128, 128), (n_dev // 128, 128)
    flops = 2 * m_dev * n_dev * 512

    def run(body, outs, tile, *args):
        return call(body, outs, args, scratch=[pltpu.VMEM(tile, jnp.float32)], flops=flops)

    core = (lax.axis_index("target").astype(jnp.int32) & 1).reshape(1)
    local, sqx, sqy = call(
        rows_first,
        [(targets,) + tile_m, row_m, row_n],
        (*data, core),
        scratch=[pltpu.VMEM(tile_m, jnp.float32)]
        + [pltpu.VMEM(v.shape, v.dtype) for v in data]
        + [pltpu.SemaphoreType.DMA((len(data),))],
        anywhere=range(len(data)),
        smem=(len(data),),
        flops=flops,
        limit=54,
    )
    got = exchange(local, "target")
    (t,) = call(scores, [(m_dev, n_dev)], (*data, sqx), anywhere=(len(data),), flops=flops, limit=54)
    t, local, phi = call(
        functools.partial(columns_first, log_m),
        [(m_dev, n_dev), (trains,) + tile_n, row_m],
        (t, got),
        scratch=[pltpu.VMEM(tile_n, jnp.float32), pltpu.SemaphoreType.DMA((n_dev // 128,))],
        anywhere=(0,),
        limit=48,
    )
    got = exchange(local, "train")
    local, gamma = run(functools.partial(rows_next, log_n), [(targets,) + tile_m, row_n], tile_m, t, phi, got)
    got = exchange(local, "target")
    row_more = (1, n_dev + 128)
    local, phi = run(
        functools.partial(columns_next, log_m, log_n), [(trains,) + row_more, row_m], row_more, t, phi, gamma, sqx, got
    )
    got = exchange(local, "train")

    half = targets // 2
    scratch = [pltpu.VMEM((m_dev, 128), jnp.float32)]
    chunks = (half, CHUNK, 128)
    sent, gamma = call(
        functools.partial(project_sent, log_m, log_n, [2 * k + 1 for k in range(half)]),
        [chunks, row_n],
        (t, target_embed, phi, gamma, got, core),
        scratch=scratch, smem=(5,), flops=flops,
    )
    sent = lax.ppermute(sent, "target", [(t, t ^ 1) for t in range(targets)])
    kept, value, potential = call(
        functools.partial(project_kept, log_n, m_dev * trains - 1, [2 * k for k in range(half)]),
        [chunks, row_m, row_n],
        (t, target_embed, phi, gamma, sqx, sqy, got, core),
        scratch=scratch, smem=(7,), flops=flops,
    )
    groups = [[c + 2 * k for k in range(half)] for c in range(2)]
    got = exchange(kept + sent, "target", groups)
    (barycentre,) = call(finish, [(SHARE, width)], (got,))
    return (value.reshape(m_dev), potential.reshape(n_dev), barycentre)


def solution(mesh):
    return jax.shard_map(
        on_device,
        mesh=mesh,
        in_specs=(P("train", None), P("train"), P("target", None), P("target"), P()),
        out_specs=(P("train"), P("target"), P(("train", "target"), None)),
        check_vma=False,
    )
```

```python
import functools
import math

import jax
import jax.numpy as jnp
from jax import lax
from jax.experimental import pallas as pl
from jax.experimental.pallas import tpu as pltpu
from jax.sharding import PartitionSpec as P

EPS = 0.05
SCALE = 128.0
KAPPA = math.log2(math.e) / EPS / SCALE
LOG2 = math.log2(math.e) / EPS
LANES = 256
SHARE = 32
CHUNK = 2 * SHARE + 8


def pieces(v):
    hi = v.astype(jnp.bfloat16).astype(jnp.float32)
    rest = v - hi
    mid = rest.astype(jnp.bfloat16).astype(jnp.float32)
    lo = (rest - mid).astype(jnp.bfloat16).astype(jnp.float32)
    return hi, mid, lo


def tail(first, second):
    n = first[0].shape[1]
    row = lax.broadcasted_iota(jnp.int32, (8, n), 0)
    out = jnp.zeros((8, n), jnp.float32)
    for k, v in enumerate(first + second):
        out = jnp.where(row == k, v, out)
    return out


def ones_like3(v):
    return (jnp.ones_like(v),) * 3


def train_rows(label, phi):
    m = label.shape[1]
    onehot = (lax.broadcasted_iota(jnp.int32, (8, m), 0) == label).astype(jnp.float32)
    last = tail(ones_like3(phi), pieces(phi * SCALE))
    return jnp.concatenate([onehot, onehot, onehot, last], axis=0)


def target_rows(label, gamma, label_cost):
    n = label.shape[1]
    table = jnp.zeros((8, n), jnp.float32)
    for b in range(8):
        table = jnp.where(label == b, label_cost[:, b : b + 1], table)
    last = tail(pieces(gamma * SCALE), ones_like3(gamma))
    return jnp.concatenate(list(pieces(table * -SCALE)) + [last], axis=0)


def as_columns(rows):
    pad = jnp.zeros((96, rows.shape[1]), jnp.float32)
    return jnp.concatenate([rows, pad], axis=0).T.astype(jnp.bfloat16)


def as_rows(rows):
    pad = jnp.zeros((96, rows.shape[1]), jnp.float32)
    return jnp.concatenate([rows, pad], axis=0).astype(jnp.bfloat16)


def dot_nt(a, b):
    return lax.dot_general(a, b, (((1,), (1,)), ((), ())), preferred_element_type=jnp.float32)


def dot_nn(a, b):
    return lax.dot_general(a, b, (((1,), (0,)), ((), ())), preferred_element_type=jnp.float32)


def square_sums(v):
    sq = jnp.square(v.astype(jnp.float32))
    hi = sq.astype(jnp.bfloat16)
    lo = (sq - hi.astype(jnp.float32)).astype(jnp.bfloat16)
    ones = jnp.ones((8, v.shape[1]), jnp.bfloat16)
    return (dot_nt(ones, hi) + dot_nt(ones, lo))[0:1] / v.shape[1]


def to_everyone(v, out_ref):
    for k in range(out_ref.shape[0]):
        out_ref[k] = v


def in_lanes(v):
    return jnp.concatenate([v[k : k + 1] for k in range(v.shape[0])], axis=1)


def tree(parts, combine):
    while len(parts) > 1:
        parts = [combine(parts[k], parts[k + 1]) for k in range(0, len(parts), 2)]
    return parts[0]


def lse_received(ref):
    parts = [ref[k] for k in range(ref.shape[0])]
    top = tree(parts, jnp.maximum)
    total = tree([jnp.exp((part - top) * (1.0 / EPS)) for part in parts], jnp.add)
    return in_lanes(top + EPS * jnp.log(total))


def sum_received(ref):
    return tree([ref[k] for k in range(ref.shape[0])], jnp.add)


def fetch(pairs, sems):
    copies = [pltpu.make_async_copy(src, dst, sems.at[k]) for k, (src, dst) in enumerate(pairs)]
    for copy in copies:
        copy.start()
    return copies


def wait_all(copies):
    for copy in copies:
        copy.wait()


def rows_first(
    x_any, y_any, lx_any, ly_any, lc_any, core_ref,
    out_ref, sqx_ref, sqy_ref, at_ref, x_ref, y_ref, lx_ref, ly_ref, lc_ref, sems,
):
    pairs = [(ly_any, ly_ref), (lc_any, lc_ref), (lx_any, lx_ref), (y_any, y_ref), (x_any, x_ref)]
    copies = fetch(pairs, sems)
    wait_all(copies[:3])
    rows = as_rows(train_rows(lx_ref[...], jnp.zeros(lx_ref.shape, jnp.float32)))
    columns = as_columns(target_rows(ly_ref[...], jnp.zeros(ly_ref.shape, jnp.float32), lc_ref[...]))
    copies[3].wait()
    y = y_ref[...]
    width = y.shape[1]
    norms = jnp.sum(jnp.square(y.astype(jnp.float32)), axis=1, keepdims=True) * (SCALE / width)
    norms = jnp.broadcast_to(norms, (y.shape[0], LANES))
    copies[4].wait()
    for k in range(x_ref.shape[0] // LANES):
        at = slice(k * LANES, (k + 1) * LANES)
        t = dot_nt(y, x_ref[at, :]) + dot_nn(columns, rows[:, at]) - norms
        top = jnp.max(t, axis=0, keepdims=True)
        total = jnp.sum(jnp.exp2((t - top) * KAPPA), axis=0, keepdims=True)
        out = top * (1.0 / SCALE) + EPS * jnp.log(total)
        for r in range(LANES // 128):
            row = k * (LANES // 128) + r
            at_ref[row : row + 1, :] = out[:, r * 128 : (r + 1) * 128]
    sqx_ref[...] = square_sums(x_ref[...])
    sqy_ref[...] = square_sums(y)
    to_everyone(at_ref[...], out_ref)


def in_rows(v):
    return jnp.broadcast_to(v, (128, v.shape[1])).T


def columns_first(log_m, x_ref, y_ref, lx_ref, ly_ref, lc_ref, got_ref, t_ref, out_ref, phi_ref, at_ref):
    zero_m, zero_n = (jnp.zeros(ref.shape, jnp.float32) for ref in (lx_ref, ly_ref))
    phi = -log_m - lse_received(got_ref)
    phi_ref[...] = phi
    down = in_rows(phi * LOG2)
    down = jnp.concatenate([down] * (LANES // 128), axis=1)
    x = x_ref[...]
    columns = as_columns(train_rows(lx_ref[...], zero_m))
    rows = as_rows(target_rows(ly_ref[...], zero_n, lc_ref[...]))
    for k in range(y_ref.shape[0] // LANES):
        at = slice(k * LANES, (k + 1) * LANES)
        t = (dot_nt(x, y_ref[at, :]) + dot_nn(columns, rows[:, at])) * KAPPA
        t_ref[:, at] = t
        t = t + down
        top = jnp.max(t, axis=0, keepdims=True)
        total = jnp.sum(jnp.exp2(t - top), axis=0, keepdims=True)
        out = top * (1.0 / LOG2) + EPS * jnp.log(total)
        for r in range(LANES // 128):
            row = k * (LANES // 128) + r
            at_ref[row : row + 1, :] = out[:, r * 128 : (r + 1) * 128]
    to_everyone(at_ref[...], out_ref)


def rows_next(log_n, t_ref, phi_ref, got_ref, out_ref, gamma_ref, at_ref):
    gamma = -log_n - lse_received(got_ref)
    gamma_ref[...] = gamma
    down = in_rows((phi_ref[...] + log_n) * LOG2)
    across = gamma * LOG2
    for k in range(t_ref.shape[0] // 128):
        rows = slice(k * 128, (k + 1) * 128)
        total = 0.0
        for j in range(t_ref.shape[1] // 128):
            at = slice(j * 128, (j + 1) * 128)
            total = total + jnp.exp2(t_ref[rows, at] + down[rows] + across[:, at])
        at_ref[k : k + 1, :] = jnp.sum(total.T, axis=0, keepdims=True)
    to_everyone(at_ref[...], out_ref)


def columns_next(log_m, log_n, t_ref, phi_ref, gamma_ref, sqx_ref, got_ref, out_ref, new_ref, at_ref):
    n = t_ref.shape[1]
    phi = phi_ref[...] + log_n - log_m - EPS * jnp.log(in_lanes(sum_received(got_ref)))
    new_ref[...] = phi
    down = in_rows(phi * LOG2)
    across = (gamma_ref[...] + log_m) * LOG2
    for k in range(n // 128):
        at = slice(k * 128, (k + 1) * 128)
        at_ref[:, at] = jnp.sum(jnp.exp2(t_ref[:, at] + down + across[:, at]), axis=0, keepdims=True)
    dual_sum = jnp.sum(phi + sqx_ref[...], axis=1, keepdims=True)
    at_ref[:, n : n + 128] = jnp.broadcast_to(dual_sum, (1, 128))
    to_everyone(at_ref[...], out_ref)


def on_diagonal(v):
    shape = (SHARE, 128)
    row, column = (lax.broadcasted_iota(jnp.int32, shape, k) for k in range(2))
    axis = 0 if v.shape[0] == SHARE else 1
    return jnp.sum(jnp.where(row == column, v, 0.0), axis=axis, keepdims=True)


def weighted_sums(shift, relative, t_ref, y_ref, phi_ref, gamma_ref, core_ref, out_ref, down_ref):
    core = core_ref[0]
    n = t_ref.shape[1]
    down_ref[...] = in_rows((phi_ref[...] + shift) * LOG2)
    across = gamma_ref[...] * LOG2
    y = y_ref[...]
    per = min(8, len(relative))
    for b in range(len(relative) // per):
        weights = []
        for k in range(per):
            start = pl.multiple_of((core ^ relative[b * per + k]) * SHARE, SHARE)
            at = pl.ds(start, SHARE)
            down = jnp.concatenate([down_ref[at, :]] * (n // 128), axis=1)
            weights.append(jnp.exp2(t_ref[at, :] + down + across).astype(jnp.bfloat16))
        w = jnp.concatenate(weights, axis=0)
        denom = jnp.sum(w.astype(jnp.float32), axis=1, keepdims=True)
        numer = dot_nn(w, y)
        for k in range(per):
            part, chunk = slice(k * SHARE, (k + 1) * SHARE), b * per + k
            out_ref[chunk, 0:SHARE, :] = numer[part, 0:128]
            out_ref[chunk, SHARE : 2 * SHARE, :] = numer[part, 128:256]
            out_ref[chunk, 2 * SHARE : CHUNK, :] = jnp.broadcast_to(on_diagonal(denom[part]), (CHUNK - 2 * SHARE, 128))


def project_sent(
    log_m, log_n, relative, t_ref, y_ref, phi_ref, gamma_ref, got_ref, core_ref, out_ref, new_ref, down_ref
):
    total = sum_received(got_ref)
    new_ref[...] = gamma_ref[...] + log_m - log_n - EPS * jnp.log(total[:, 0 : new_ref.shape[1]])
    weighted_sums(log_n, relative, t_ref, y_ref, phi_ref, new_ref, core_ref, out_ref, down_ref)


def project_kept(
    log_n, others, relative, t_ref, y_ref, phi_ref, gamma_ref, sqx_ref, sqy_ref, got_ref, core_ref,
    out_ref, value_ref, potential_ref, down_ref,
):
    n = gamma_ref.shape[1]
    potential_ref[...] = gamma_ref[...] + sqy_ref[...]
    dual = phi_ref[...] + sqx_ref[...]
    dual_sum = tree([got_ref[k, :, n : n + 1] for k in range(got_ref.shape[0])], jnp.add)
    value_ref[...] = dual - (dual_sum - dual) / others
    weighted_sums(log_n, relative, t_ref, y_ref, phi_ref, gamma_ref, core_ref, out_ref, down_ref)


def finish(got_ref, out_ref):
    total = sum_received(got_ref)
    denom = on_diagonal(total[2 * SHARE : 2 * SHARE + 1])
    out_ref[:, 0:128] = total[0:SHARE] / denom
    out_ref[:, 128:256] = total[SHARE : 2 * SHARE] / denom


def call(body, outs, args, scratch=(), smem=(), anywhere=(), flops=0, limit=40):
    vmem = pl.BlockSpec(memory_space=pltpu.VMEM)
    specs = [vmem for _ in args]
    for k in smem:
        specs[k] = pl.BlockSpec(memory_space=pltpu.SMEM)
    for k in anywhere:
        specs[k] = pl.BlockSpec(memory_space=pl.ANY)
    outs = [s if hasattr(s, "dtype") else jax.ShapeDtypeStruct(s, jnp.float32) for s in outs]
    return pl.pallas_call(
        body,
        out_shape=outs,
        in_specs=specs,
        out_specs=[vmem for _ in outs],
        scratch_shapes=list(scratch),
        compiler_params=pltpu.CompilerParams(vmem_limit_bytes=int(limit * 2**20)),
        cost_estimate=pl.CostEstimate(flops=flops, bytes_accessed=2**20, transcendentals=flops // 512),
    )(*args)


def exchange(x, axis, groups=None):
    return lax.all_to_all(x, axis, 0, 0, axis_index_groups=groups, tiled=True)


def on_device(train_embed, train_label, target_embed, target_label, label_cost):
    m_dev, width = train_embed.shape
    n_dev = target_embed.shape[0]
    trains = lax.axis_size("train")
    targets = lax.axis_size("target")
    log_m = EPS * math.log(m_dev * trains)
    log_n = EPS * math.log(n_dev * targets)
    data = (
        train_embed,
        target_embed,
        train_label.reshape(1, m_dev),
        target_label.reshape(1, n_dev),
        label_cost,
    )
    row_m, row_n = (1, m_dev), (1, n_dev)
    tile_m, tile_n = (m_dev // 128, 128), (n_dev // 128, 128)
    flops = 2 * m_dev * n_dev * 512

    def run(body, outs, tile, *args):
        return call(body, outs, args, scratch=[pltpu.VMEM(tile, jnp.float32)], flops=flops)

    core = (lax.axis_index("target").astype(jnp.int32) & 1).reshape(1)
    local, sqx, sqy = call(
        rows_first,
        [(targets,) + tile_m, row_m, row_n],
        (*data, core),
        scratch=[pltpu.VMEM(tile_m, jnp.float32)]
        + [pltpu.VMEM(v.shape, v.dtype) for v in data]
        + [pltpu.SemaphoreType.DMA((len(data),))],
        anywhere=range(len(data)),
        smem=(len(data),),
        flops=flops,
        limit=54,
    )
    got = exchange(local, "target")
    t, local, phi = run(
        functools.partial(columns_first, log_m), [(m_dev, n_dev), (trains,) + tile_n, row_m], tile_n, *data, got
    )
    got = exchange(local, "train")
    local, gamma = run(functools.partial(rows_next, log_n), [(targets,) + tile_m, row_n], tile_m, t, phi, got)
    got = exchange(local, "target")
    row_more = (1, n_dev + 128)
    local, phi = run(
        functools.partial(columns_next, log_m, log_n), [(trains,) + row_more, row_m], row_more, t, phi, gamma, sqx, got
    )
    got = exchange(local, "train")

    half = targets // 2
    scratch = [pltpu.VMEM((m_dev, 128), jnp.float32)]
    chunks = (half, CHUNK, 128)
    sent, gamma = call(
        functools.partial(project_sent, log_m, log_n, [2 * k + 1 for k in range(half)]),
        [chunks, row_n],
        (t, target_embed, phi, gamma, got, core),
        scratch=scratch, smem=(5,), flops=flops,
    )
    sent = lax.ppermute(sent, "target", [(t, t ^ 1) for t in range(targets)])
    kept, value, potential = call(
        functools.partial(project_kept, log_n, m_dev * trains - 1, [2 * k for k in range(half)]),
        [chunks, row_m, row_n],
        (t, target_embed, phi, gamma, sqx, sqy, got, core),
        scratch=scratch, smem=(7,), flops=flops,
    )
    groups = [[c + 2 * k for k in range(half)] for c in range(2)]
    got = exchange(kept + sent, "target", groups)
    (barycentre,) = call(finish, [(SHARE, width)], (got,))
    return (value.reshape(m_dev), potential.reshape(n_dev), barycentre)


def solution(mesh):
    return jax.shard_map(
        on_device,
        mesh=mesh,
        in_specs=(P("train", None), P("train"), P("target", None), P("target"), P()),
        out_specs=(P("train"), P("target"), P(("train", "target"), None)),
        check_vma=False,
    )
```

```python
import functools
import math

import jax
import jax.numpy as jnp
from jax import lax
from jax.experimental import pallas as pl
from jax.experimental.pallas import tpu as pltpu
from jax.sharding import PartitionSpec as P

EPS = 0.05
SCALE = 128.0
KAPPA = math.log2(math.e) / EPS / SCALE
LOG2 = math.log2(math.e) / EPS
LANES = 256
SHARE = 32
CHUNK = 2 * SHARE + 8


def pieces(v):
    hi = v.astype(jnp.bfloat16).astype(jnp.float32)
    rest = v - hi
    mid = rest.astype(jnp.bfloat16).astype(jnp.float32)
    lo = (rest - mid).astype(jnp.bfloat16).astype(jnp.float32)
    return hi, mid, lo


def tail(first, second):
    n = first[0].shape[1]
    row = lax.broadcasted_iota(jnp.int32, (8, n), 0)
    out = jnp.zeros((8, n), jnp.float32)
    for k, v in enumerate(first + second):
        out = jnp.where(row == k, v, out)
    return out


def ones_like3(v):
    return (jnp.ones_like(v),) * 3


def train_rows(label, phi):
    m = label.shape[1]
    onehot = (lax.broadcasted_iota(jnp.int32, (8, m), 0) == label).astype(jnp.float32)
    last = tail(ones_like3(phi), pieces(phi * SCALE))
    return jnp.concatenate([onehot, onehot, onehot, last], axis=0)


def target_rows(label, gamma, label_cost):
    n = label.shape[1]
    table = jnp.zeros((8, n), jnp.float32)
    for b in range(8):
        table = jnp.where(label == b, label_cost[:, b : b + 1], table)
    last = tail(pieces(gamma * SCALE), ones_like3(gamma))
    return jnp.concatenate(list(pieces(table * -SCALE)) + [last], axis=0)


def as_columns(rows):
    pad = jnp.zeros((96, rows.shape[1]), jnp.float32)
    return jnp.concatenate([rows, pad], axis=0).T.astype(jnp.bfloat16)


def as_rows(rows):
    pad = jnp.zeros((96, rows.shape[1]), jnp.float32)
    return jnp.concatenate([rows, pad], axis=0).astype(jnp.bfloat16)


def dot_nt(a, b):
    return lax.dot_general(a, b, (((1,), (1,)), ((), ())), preferred_element_type=jnp.float32)


def dot_nn(a, b):
    return lax.dot_general(a, b, (((1,), (0,)), ((), ())), preferred_element_type=jnp.float32)


def square_means(v):
    sums = jnp.sum(jnp.square(v.astype(jnp.float32)), axis=1, keepdims=True)
    return jnp.broadcast_to(sums * (1.0 / v.shape[1]), (v.shape[0], 128))


def to_everyone(v, out_ref):
    for k in range(out_ref.shape[0]):
        out_ref[k] = v


def in_lanes(v):
    return jnp.concatenate([v[k : k + 1] for k in range(v.shape[0])], axis=1)


def tree(parts, combine):
    while len(parts) > 1:
        parts = [combine(parts[k], parts[k + 1]) for k in range(0, len(parts), 2)]
    return parts[0]


def lse_received(ref):
    parts = [ref[k] for k in range(ref.shape[0])]
    top = tree(parts, jnp.maximum)
    total = tree([jnp.exp((part - top) * (1.0 / EPS)) for part in parts], jnp.add)
    return in_lanes(top + EPS * jnp.log(total))


def sum_received(ref):
    return tree([ref[k] for k in range(ref.shape[0])], jnp.add)


def fetch(pairs, sems):
    copies = [pltpu.make_async_copy(src, dst, sems.at[k]) for k, (src, dst) in enumerate(pairs)]
    for copy in copies:
        copy.start()
    return copies


def wait_all(copies):
    for copy in copies:
        copy.wait()


def rows_first(
    x_any, y_any, lx_any, ly_any, lc_any, core_ref,
    out_ref, sqx_ref, sqy_ref, at_ref, x_ref, y_ref, lx_ref, ly_ref, lc_ref, sems,
):
    pairs = [(ly_any, ly_ref), (lc_any, lc_ref), (lx_any, lx_ref), (y_any, y_ref), (x_any, x_ref)]
    copies = fetch(pairs, sems)
    wait_all(copies[:3])
    rows = as_rows(train_rows(lx_ref[...], jnp.zeros(lx_ref.shape, jnp.float32)))
    columns = as_columns(target_rows(ly_ref[...], jnp.zeros(ly_ref.shape, jnp.float32), lc_ref[...]))
    copies[3].wait()
    y = y_ref[...]
    means = square_means(y)
    norms = jnp.concatenate([means * SCALE] * (LANES // 128), axis=1)
    copies[4].wait()
    for k in range(x_ref.shape[0] // LANES):
        at = slice(k * LANES, (k + 1) * LANES)
        t = dot_nt(y, x_ref[at, :]) + dot_nn(columns, rows[:, at]) - norms
        top = jnp.max(t, axis=0, keepdims=True)
        total = jnp.sum(jnp.exp2((t - top) * KAPPA), axis=0, keepdims=True)
        out = top * (1.0 / SCALE) + EPS * jnp.log(total)
        for r in range(LANES // 128):
            row = k * (LANES // 128) + r
            at_ref[row : row + 1, :] = out[:, r * 128 : (r + 1) * 128]
    sqx_ref[...] = square_means(x_ref[...]).T[0:1]
    sqy_ref[...] = means.T[0:1]
    to_everyone(at_ref[...], out_ref)


def in_rows(v):
    return jnp.broadcast_to(v, (128, v.shape[1])).T


def columns_first(log_m, x_ref, y_ref, lx_ref, ly_ref, lc_ref, got_ref, t_ref, out_ref, phi_ref, at_ref):
    zero_m, zero_n = (jnp.zeros(ref.shape, jnp.float32) for ref in (lx_ref, ly_ref))
    phi = -log_m - lse_received(got_ref)
    phi_ref[...] = phi
    down = in_rows(phi * LOG2)
    down = jnp.concatenate([down] * (LANES // 128), axis=1)
    x = x_ref[...]
    columns = as_columns(train_rows(lx_ref[...], zero_m))
    rows = as_rows(target_rows(ly_ref[...], zero_n, lc_ref[...]))
    for k in range(y_ref.shape[0] // LANES):
        at = slice(k * LANES, (k + 1) * LANES)
        t = (dot_nt(x, y_ref[at, :]) + dot_nn(columns, rows[:, at])) * KAPPA
        t_ref[:, at] = t
        t = t + down
        top = jnp.max(t, axis=0, keepdims=True)
        total = jnp.sum(jnp.exp2(t - top), axis=0, keepdims=True)
        out = top * (1.0 / LOG2) + EPS * jnp.log(total)
        for r in range(LANES // 128):
            row = k * (LANES // 128) + r
            at_ref[row : row + 1, :] = out[:, r * 128 : (r + 1) * 128]
    to_everyone(at_ref[...], out_ref)


def rows_next(log_n, t_ref, phi_ref, got_ref, out_ref, gamma_ref, at_ref):
    gamma = -log_n - lse_received(got_ref)
    gamma_ref[...] = gamma
    down = in_rows((phi_ref[...] + log_n) * LOG2)
    across = gamma * LOG2
    for k in range(t_ref.shape[0] // 128):
        rows = slice(k * 128, (k + 1) * 128)
        total = 0.0
        for j in range(t_ref.shape[1] // 128):
            at = slice(j * 128, (j + 1) * 128)
            total = total + jnp.exp2(t_ref[rows, at] + down[rows] + across[:, at])
        at_ref[k : k + 1, :] = jnp.sum(total.T, axis=0, keepdims=True)
    to_everyone(at_ref[...], out_ref)


def columns_next(log_m, log_n, t_ref, phi_ref, gamma_ref, sqx_ref, got_ref, out_ref, new_ref, at_ref):
    n = t_ref.shape[1]
    phi = phi_ref[...] + log_n - log_m - EPS * jnp.log(in_lanes(sum_received(got_ref)))
    new_ref[...] = phi
    down = in_rows(phi * LOG2)
    across = (gamma_ref[...] + log_m) * LOG2
    for k in range(n // 128):
        at = slice(k * 128, (k + 1) * 128)
        at_ref[:, at] = jnp.sum(jnp.exp2(t_ref[:, at] + down + across[:, at]), axis=0, keepdims=True)
    dual_sum = jnp.sum(phi + sqx_ref[...], axis=1, keepdims=True)
    at_ref[:, n : n + 128] = jnp.broadcast_to(dual_sum, (1, 128))
    to_everyone(at_ref[...], out_ref)


def on_diagonal(v):
    shape = (SHARE, 128)
    row, column = (lax.broadcasted_iota(jnp.int32, shape, k) for k in range(2))
    axis = 0 if v.shape[0] == SHARE else 1
    return jnp.sum(jnp.where(row == column, v, 0.0), axis=axis, keepdims=True)


def weighted_sums(shift, relative, t_ref, y_ref, phi_ref, gamma_ref, core_ref, out_ref, down_ref):
    core = core_ref[0]
    n = t_ref.shape[1]
    down_ref[...] = in_rows((phi_ref[...] + shift) * LOG2)
    across = gamma_ref[...] * LOG2
    y = y_ref[...]
    per = min(8, len(relative))
    for b in range(len(relative) // per):
        weights = []
        for k in range(per):
            start = pl.multiple_of((core ^ relative[b * per + k]) * SHARE, SHARE)
            at = pl.ds(start, SHARE)
            down = jnp.concatenate([down_ref[at, :]] * (n // 128), axis=1)
            weights.append(jnp.exp2(t_ref[at, :] + down + across).astype(jnp.bfloat16))
        w = jnp.concatenate(weights, axis=0)
        denom = jnp.sum(w.astype(jnp.float32), axis=1, keepdims=True)
        numer = dot_nn(w, y)
        for k in range(per):
            part, chunk = slice(k * SHARE, (k + 1) * SHARE), b * per + k
            out_ref[chunk, 0:SHARE, :] = numer[part, 0:128]
            out_ref[chunk, SHARE : 2 * SHARE, :] = numer[part, 128:256]
            out_ref[chunk, 2 * SHARE : CHUNK, :] = jnp.broadcast_to(on_diagonal(denom[part]), (CHUNK - 2 * SHARE, 128))


def project_sent(
    log_m, log_n, relative, t_ref, y_ref, phi_ref, gamma_ref, got_ref, core_ref, out_ref, new_ref, down_ref
):
    total = sum_received(got_ref)
    new_ref[...] = gamma_ref[...] + log_m - log_n - EPS * jnp.log(total[:, 0 : new_ref.shape[1]])
    weighted_sums(log_n, relative, t_ref, y_ref, phi_ref, new_ref, core_ref, out_ref, down_ref)


def project_kept(log_n, relative, t_ref, y_ref, phi_ref, gamma_ref, core_ref, out_ref, down_ref):
    weighted_sums(log_n, relative, t_ref, y_ref, phi_ref, gamma_ref, core_ref, out_ref, down_ref)


def finish(others, got_ref, phi_ref, gamma_ref, sqx_ref, sqy_ref, columns_ref, out_ref, value_ref, potential_ref):
    total = sum_received(got_ref)
    denom = on_diagonal(total[2 * SHARE : 2 * SHARE + 1])
    out_ref[:, 0:128] = total[0:SHARE] / denom
    out_ref[:, 128:256] = total[SHARE : 2 * SHARE] / denom
    n = gamma_ref.shape[1]
    potential_ref[...] = gamma_ref[...] + sqy_ref[...]
    dual = phi_ref[...] + sqx_ref[...]
    dual_sum = tree([columns_ref[k, :, n : n + 1] for k in range(columns_ref.shape[0])], jnp.add)
    value_ref[...] = dual - (dual_sum - dual) / others


def call(body, outs, args, scratch=(), smem=(), anywhere=(), flops=0, limit=40):
    vmem = pl.BlockSpec(memory_space=pltpu.VMEM)
    specs = [vmem for _ in args]
    for k in smem:
        specs[k] = pl.BlockSpec(memory_space=pltpu.SMEM)
    for k in anywhere:
        specs[k] = pl.BlockSpec(memory_space=pl.ANY)
    outs = [s if hasattr(s, "dtype") else jax.ShapeDtypeStruct(s, jnp.float32) for s in outs]
    return pl.pallas_call(
        body,
        out_shape=outs,
        in_specs=specs,
        out_specs=[vmem for _ in outs],
        scratch_shapes=list(scratch),
        compiler_params=pltpu.CompilerParams(vmem_limit_bytes=int(limit * 2**20)),
        cost_estimate=pl.CostEstimate(flops=flops, bytes_accessed=2**20, transcendentals=flops // 512),
    )(*args)


def exchange(x, axis, groups=None):
    return lax.all_to_all(x, axis, 0, 0, axis_index_groups=groups, tiled=True)


def on_device(train_embed, train_label, target_embed, target_label, label_cost):
    m_dev, width = train_embed.shape
    n_dev = target_embed.shape[0]
    trains = lax.axis_size("train")
    targets = lax.axis_size("target")
    log_m = EPS * math.log(m_dev * trains)
    log_n = EPS * math.log(n_dev * targets)
    data = (
        train_embed,
        target_embed,
        train_label.reshape(1, m_dev),
        target_label.reshape(1, n_dev),
        label_cost,
    )
    row_m, row_n = (1, m_dev), (1, n_dev)
    tile_m, tile_n = (m_dev // 128, 128), (n_dev // 128, 128)
    flops = 2 * m_dev * n_dev * 512

    def run(body, outs, tile, *args):
        return call(body, outs, args, scratch=[pltpu.VMEM(tile, jnp.float32)], flops=flops)

    core = (lax.axis_index("target").astype(jnp.int32) & 1).reshape(1)
    local, sqx, sqy = call(
        rows_first,
        [(targets,) + tile_m, row_m, row_n],
        (*data, core),
        scratch=[pltpu.VMEM(tile_m, jnp.float32)]
        + [pltpu.VMEM(v.shape, v.dtype) for v in data]
        + [pltpu.SemaphoreType.DMA((len(data),))],
        anywhere=range(len(data)),
        smem=(len(data),),
        flops=flops,
        limit=54,
    )
    got = exchange(local, "target")
    t, local, phi = run(
        functools.partial(columns_first, log_m), [(m_dev, n_dev), (trains,) + tile_n, row_m], tile_n, *data, got
    )
    got = exchange(local, "train")
    local, gamma = run(functools.partial(rows_next, log_n), [(targets,) + tile_m, row_n], tile_m, t, phi, got)
    got = exchange(local, "target")
    row_more = (1, n_dev + 128)
    local, phi = run(
        functools.partial(columns_next, log_m, log_n), [(trains,) + row_more, row_m], row_more, t, phi, gamma, sqx, got
    )
    columns = exchange(local, "train")

    half = targets // 2
    scratch = [pltpu.VMEM((m_dev, 128), jnp.float32)]
    chunks = (half, CHUNK, 128)
    sent, gamma = call(
        functools.partial(project_sent, log_m, log_n, [2 * k + 1 for k in range(half)]),
        [chunks, row_n],
        (t, target_embed, phi, gamma, columns, core),
        scratch=scratch, smem=(5,), flops=flops,
    )
    sent = lax.ppermute(sent, "target", [(t, t ^ 1) for t in range(targets)])
    (kept,) = call(
        functools.partial(project_kept, log_n, [2 * k for k in range(half)]),
        [chunks],
        (t, target_embed, phi, gamma, core),
        scratch=scratch, smem=(4,), flops=flops,
    )
    groups = [[c + 2 * k for k in range(half)] for c in range(2)]
    got = exchange(kept + sent, "target", groups)
    barycentre, value, potential = call(
        functools.partial(finish, m_dev * trains - 1),
        [(SHARE, width), row_m, row_n],
        (got, phi, gamma, sqx, sqy, columns),
    )
    return (value.reshape(m_dev), potential.reshape(n_dev), barycentre)


def solution(mesh):
    return jax.shard_map(
        on_device,
        mesh=mesh,
        in_specs=(P("train", None), P("train"), P("target", None), P("target"), P()),
        out_specs=(P("train"), P("target"), P(("train", "target"), None)),
        check_vma=False,
    )
```

```python
import functools
import math

import jax
import jax.numpy as jnp
from jax import lax
from jax.experimental import pallas as pl
from jax.experimental.pallas import tpu as pltpu
from jax.sharding import PartitionSpec as P

EPS = 0.05
SCALE = 128.0
KAPPA = math.log2(math.e) / EPS / SCALE
LOG2 = math.log2(math.e) / EPS
LANES = 256
SHARE = 32
CHUNK = 2 * SHARE + 8


def pieces(v):
    hi = v.astype(jnp.bfloat16).astype(jnp.float32)
    rest = v - hi
    mid = rest.astype(jnp.bfloat16).astype(jnp.float32)
    lo = (rest - mid).astype(jnp.bfloat16).astype(jnp.float32)
    return hi, mid, lo


def tail(first, second):
    n = first[0].shape[1]
    row = lax.broadcasted_iota(jnp.int32, (8, n), 0)
    out = jnp.zeros((8, n), jnp.float32)
    for k, v in enumerate(first + second):
        out = jnp.where(row == k, v, out)
    return out


def ones_like3(v):
    return (jnp.ones_like(v),) * 3


def train_rows(label, phi):
    m = label.shape[1]
    onehot = (lax.broadcasted_iota(jnp.int32, (8, m), 0) == label).astype(jnp.float32)
    last = tail(ones_like3(phi), pieces(phi * SCALE))
    return jnp.concatenate([onehot, onehot, onehot, last], axis=0)


def target_rows(label, gamma, label_cost):
    n = label.shape[1]
    table = jnp.zeros((8, n), jnp.float32)
    for b in range(8):
        table = jnp.where(label == b, label_cost[:, b : b + 1], table)
    last = tail(pieces(gamma * SCALE), ones_like3(gamma))
    return jnp.concatenate(list(pieces(table * -SCALE)) + [last], axis=0)


def as_columns(rows):
    pad = jnp.zeros((96, rows.shape[1]), jnp.float32)
    return jnp.concatenate([rows, pad], axis=0).T.astype(jnp.bfloat16)


def as_rows(rows):
    pad = jnp.zeros((96, rows.shape[1]), jnp.float32)
    return jnp.concatenate([rows, pad], axis=0).astype(jnp.bfloat16)


def dot_nt(a, b):
    return lax.dot_general(a, b, (((1,), (1,)), ((), ())), preferred_element_type=jnp.float32)


def dot_nn(a, b):
    return lax.dot_general(a, b, (((1,), (0,)), ((), ())), preferred_element_type=jnp.float32)


def square_means(v):
    sums = jnp.sum(jnp.square(v.astype(jnp.float32)), axis=1, keepdims=True)
    return jnp.broadcast_to(sums * (1.0 / v.shape[1]), (v.shape[0], 128))


def to_everyone(v, out_ref):
    for k in range(out_ref.shape[0]):
        out_ref[k] = v


def in_lanes(v):
    return jnp.concatenate([v[k : k + 1] for k in range(v.shape[0])], axis=1)


def tree(parts, combine):
    while len(parts) > 1:
        parts = [combine(parts[k], parts[k + 1]) for k in range(0, len(parts), 2)]
    return parts[0]


def lse(parts):
    top = tree(parts, jnp.maximum)
    total = tree([jnp.exp((part - top) * (1.0 / EPS)) for part in parts], jnp.add)
    return top + EPS * jnp.log(total)


def lse_received(ref):
    return in_lanes(lse([ref[k] for k in range(ref.shape[0])]))


def sum_received(ref):
    return tree([ref[k] for k in range(ref.shape[0])], jnp.add)


def fetch(pairs, sems):
    copies = [pltpu.make_async_copy(src, dst, sems.at[k]) for k, (src, dst) in enumerate(pairs)]
    for copy in copies:
        copy.start()
    return copies


def wait_all(copies):
    for copy in copies:
        copy.wait()


def rows_first(
    x_any, y_any, lx_any, ly_any, lc_any, core_ref,
    wide_any, out_ref, sqx_ref, sqy_ref, at_ref, x_ref, y_ref, lx_ref, ly_ref, lc_ref, wide_ref, sems,
):
    pairs = [(ly_any, ly_ref), (lc_any, lc_ref), (lx_any, lx_ref), (y_any, y_ref), (x_any, x_ref)]
    copies = fetch(pairs, sems)
    wait_all(copies[:3])
    rows = as_rows(train_rows(lx_ref[...], jnp.zeros(lx_ref.shape, jnp.float32)))
    columns = as_columns(target_rows(ly_ref[...], jnp.zeros(ly_ref.shape, jnp.float32), lc_ref[...]))
    copies[3].wait()
    y = y_ref[...]
    n, width = y.shape
    wide_ref[0:n, :] = y.astype(jnp.float32)
    wide_ref[n : n + 8, :] = jnp.zeros((8, width), jnp.float32)
    label = ly_ref[...].astype(jnp.float32)
    for k in range(n // width):
        wide_ref[n + k : n + k + 1, :] = label[:, k * width : (k + 1) * width]
    wide = pltpu.make_async_copy(wide_ref, wide_any, sems.at[len(pairs)])
    wide.start()
    means = square_means(y)
    norms = jnp.concatenate([means * SCALE] * (LANES // 128), axis=1)
    copies[4].wait()
    for k in range(x_ref.shape[0] // LANES):
        at = slice(k * LANES, (k + 1) * LANES)
        t = dot_nt(y, x_ref[at, :]) + dot_nn(columns, rows[:, at]) - norms
        top = jnp.max(t, axis=0, keepdims=True)
        total = jnp.sum(jnp.exp2((t - top) * KAPPA), axis=0, keepdims=True)
        out = top * (1.0 / SCALE) + EPS * jnp.log(total)
        for r in range(LANES // 128):
            row = k * (LANES // 128) + r
            at_ref[row : row + 1, :] = out[:, r * 128 : (r + 1) * 128]
    sqx_ref[...] = square_means(x_ref[...]).T[0:1]
    sqy_ref[...] = means.T[0:1]
    to_everyone(at_ref[...], out_ref)
    wide.wait()


def in_rows(v):
    return jnp.broadcast_to(v, (128, v.shape[1])).T


def columns_first(log_m, x_ref, y_ref, lx_ref, ly_ref, lc_ref, got_ref, t_ref, out_ref, phi_ref, at_ref):
    zero_m, zero_n = (jnp.zeros(ref.shape, jnp.float32) for ref in (lx_ref, ly_ref))
    phi = -log_m - lse_received(got_ref)
    phi_ref[...] = phi
    down = in_rows(phi * LOG2)
    down = jnp.concatenate([down] * (LANES // 128), axis=1)
    x = x_ref[...]
    columns = as_columns(train_rows(lx_ref[...], zero_m))
    rows = as_rows(target_rows(ly_ref[...], zero_n, lc_ref[...]))
    for k in range(y_ref.shape[0] // LANES):
        at = slice(k * LANES, (k + 1) * LANES)
        t = (dot_nt(x, y_ref[at, :]) + dot_nn(columns, rows[:, at])) * KAPPA
        t_ref[:, at] = t
        t = t + down
        top = jnp.max(t, axis=0, keepdims=True)
        total = jnp.sum(jnp.exp2(t - top), axis=0, keepdims=True)
        out = top * (1.0 / LOG2) + EPS * jnp.log(total)
        for r in range(LANES // 128):
            row = k * (LANES // 128) + r
            at_ref[row : row + 1, :] = out[:, r * 128 : (r + 1) * 128]
    to_everyone(at_ref[...], out_ref)


def rows_next(log_n, t_ref, phi_ref, got_ref, out_ref, gamma_ref, at_ref):
    gamma = -log_n - lse_received(got_ref)
    gamma_ref[...] = gamma
    down = in_rows((phi_ref[...] + log_n) * LOG2)
    across = gamma * LOG2
    for k in range(t_ref.shape[0] // 128):
        rows = slice(k * 128, (k + 1) * 128)
        total = 0.0
        for j in range(t_ref.shape[1] // 128):
            at = slice(j * 128, (j + 1) * 128)
            total = total + jnp.exp2(t_ref[rows, at] + down[rows] + across[:, at])
        at_ref[k : k + 1, :] = jnp.sum(total.T, axis=0, keepdims=True)
    to_everyone(at_ref[...], out_ref)


def columns_next(log_m, log_n, t_ref, phi_ref, gamma_ref, sqx_ref, got_ref, out_ref, new_ref, at_ref):
    n = t_ref.shape[1]
    phi = phi_ref[...] + log_n - log_m - EPS * jnp.log(in_lanes(sum_received(got_ref)))
    new_ref[...] = phi
    down = in_rows(phi * LOG2)
    across = (gamma_ref[...] + log_m) * LOG2
    for k in range(n // 128):
        at = slice(k * 128, (k + 1) * 128)
        at_ref[:, at] = jnp.sum(jnp.exp2(t_ref[:, at] + down + across[:, at]), axis=0, keepdims=True)
    at_ref[:, 0:n] = EPS * jnp.log(at_ref[:, 0:n]) - (gamma_ref[...] + log_m)
    dual_sum = jnp.sum(phi + sqx_ref[...], axis=1, keepdims=True)
    at_ref[:, n : n + 128] = jnp.broadcast_to(dual_sum, (1, 128))
    to_everyone(at_ref[...], out_ref)


def on_diagonal(v):
    shape = (SHARE, 128)
    row, column = (lax.broadcasted_iota(jnp.int32, shape, k) for k in range(2))
    axis = 0 if v.shape[0] == SHARE else 1
    return jnp.sum(jnp.where(row == column, v, 0.0), axis=axis, keepdims=True)


def project(
    log_n, t_ref, x_ref, y_ref, lx_ref, lc_ref, wide_ref, phi_ref, got_ref, core_ref,
    out_ref, gamma_ref, down_ref, aug_ref, xs_ref, xa_ref,
):
    core = core_ref[0]
    n, width = y_ref.shape
    half = got_ref.shape[0] // 2
    first, second = (-log_n - lse([got_ref[half * p + k, :, 0:n] for k in range(half)]) for p in range(2))
    mine = jnp.where(core == 0, first, second)
    other = jnp.where(core == 0, second, first)
    gamma_ref[...] = mine
    across = mine * LOG2
    down_ref[...] = in_rows((phi_ref[...] + log_n) * LOG2)
    aug_ref[...] = as_columns(train_rows(lx_ref[...], jnp.zeros(lx_ref.shape, jnp.float32))).astype(jnp.float32)
    y = y_ref[...]
    y_other = wide_ref[0:n, :].astype(jnp.bfloat16)
    rows = as_rows(target_rows(in_lanes(wide_ref[n : n + n // width, :]), other, lc_ref[...]))
    chunks = out_ref.shape[0]
    per = min(8, chunks)
    for b in range(chunks // per):
        weights, downs = [], []
        for k in range(per):
            start = pl.multiple_of((2 * (b * per + k) + core) * SHARE, SHARE)
            at, to = pl.ds(start, SHARE), pl.ds((b * per + k) * SHARE, SHARE)
            xs_ref[to, :] = x_ref[at, :]
            xa_ref[to, :] = aug_ref[at, :].astype(jnp.bfloat16)
            downs.append(jnp.concatenate([down_ref[at, :]] * (n // 128), axis=1))
            weights.append(jnp.exp2(t_ref[at, :] + downs[k] + across).astype(jnp.bfloat16))
        w = jnp.concatenate(weights, axis=0)
        block = pl.ds(b * per * SHARE, per * SHARE)
        t = dot_nt(xs_ref[block, :], y_other) + dot_nn(xa_ref[block, :], rows)
        v = jnp.exp2(t * KAPPA + jnp.concatenate(downs, axis=0)).astype(jnp.bfloat16)
        denom = jnp.sum(w.astype(jnp.float32) + v.astype(jnp.float32), axis=1, keepdims=True)
        numer = dot_nn(w, y) + dot_nn(v, y_other)
        for k in range(per):
            part, chunk = slice(k * SHARE, (k + 1) * SHARE), b * per + k
            out_ref[chunk, 0:SHARE, :] = numer[part, 0:128]
            out_ref[chunk, SHARE : 2 * SHARE, :] = numer[part, 128:256]
            out_ref[chunk, 2 * SHARE : CHUNK, :] = jnp.broadcast_to(on_diagonal(denom[part]), (CHUNK - 2 * SHARE, 128))


def finish(others, got_ref, phi_ref, gamma_ref, sqx_ref, sqy_ref, columns_ref, out_ref, value_ref, potential_ref):
    total = sum_received(got_ref)
    denom = on_diagonal(total[2 * SHARE : 2 * SHARE + 1])
    out_ref[:, 0:128] = total[0:SHARE] / denom
    out_ref[:, 128:256] = total[SHARE : 2 * SHARE] / denom
    n = gamma_ref.shape[1]
    potential_ref[...] = gamma_ref[...] + sqy_ref[...]
    dual = phi_ref[...] + sqx_ref[...]
    dual_sum = tree([columns_ref[k, :, n : n + 1] for k in range(columns_ref.shape[0] // 2)], jnp.add)
    value_ref[...] = dual - (dual_sum - dual) / others


def call(body, outs, args, scratch=(), smem=(), anywhere=(), anywhere_out=(), flops=0, limit=40):
    vmem = pl.BlockSpec(memory_space=pltpu.VMEM)
    specs = [vmem for _ in args]
    for k in smem:
        specs[k] = pl.BlockSpec(memory_space=pltpu.SMEM)
    for k in anywhere:
        specs[k] = pl.BlockSpec(memory_space=pl.ANY)
    out_specs = [pl.BlockSpec(memory_space=pl.ANY) if k in anywhere_out else vmem for k in range(len(outs))]
    outs = [s if hasattr(s, "dtype") else jax.ShapeDtypeStruct(s, jnp.float32) for s in outs]
    return pl.pallas_call(
        body,
        out_shape=outs,
        in_specs=specs,
        out_specs=out_specs,
        scratch_shapes=list(scratch),
        compiler_params=pltpu.CompilerParams(vmem_limit_bytes=int(limit * 2**20)),
        cost_estimate=pl.CostEstimate(flops=flops, bytes_accessed=2**20, transcendentals=flops // 512),
    )(*args)


def exchange(x, axis, groups=None):
    return lax.all_to_all(x, axis, 0, 0, axis_index_groups=groups, tiled=True)


def on_device(train_embed, train_label, target_embed, target_label, label_cost):
    m_dev, width = train_embed.shape
    n_dev = target_embed.shape[0]
    trains = lax.axis_size("train")
    targets = lax.axis_size("target")
    log_m = EPS * math.log(m_dev * trains)
    log_n = EPS * math.log(n_dev * targets)
    data = (
        train_embed,
        target_embed,
        train_label.reshape(1, m_dev),
        target_label.reshape(1, n_dev),
        label_cost,
    )
    row_m, row_n = (1, m_dev), (1, n_dev)
    tile_m, tile_n = (m_dev // 128, 128), (n_dev // 128, 128)
    flops = 2 * m_dev * n_dev * 512

    def run(body, outs, tile, *args):
        return call(body, outs, args, scratch=[pltpu.VMEM(tile, jnp.float32)], flops=flops)

    core = (lax.axis_index("target").astype(jnp.int32) & 1).reshape(1)
    wide_shape = (n_dev + 8, width)
    wide, local, sqx, sqy = call(
        rows_first,
        [wide_shape, (targets,) + tile_m, row_m, row_n],
        (*data, core),
        scratch=[pltpu.VMEM(tile_m, jnp.float32)]
        + [pltpu.VMEM(v.shape, v.dtype) for v in data]
        + [pltpu.VMEM(wide_shape, jnp.float32), pltpu.SemaphoreType.DMA((len(data) + 1,))],
        anywhere=range(len(data)),
        anywhere_out=(0,),
        smem=(len(data),),
        flops=flops,
        limit=54,
    )
    wide = lax.ppermute(wide, "target", [(k, k ^ 1) for k in range(targets)])
    got = exchange(local, "target")
    t, local, phi = run(
        functools.partial(columns_first, log_m), [(m_dev, n_dev), (trains,) + tile_n, row_m], tile_n, *data, got
    )
    got = exchange(local, "train")
    local, gamma = run(functools.partial(rows_next, log_n), [(targets,) + tile_m, row_n], tile_m, t, phi, got)
    got = exchange(local, "target")
    row_more = (1, n_dev + 128)
    local, phi = run(
        functools.partial(columns_next, log_m, log_n), [(2 * trains,) + row_more, row_m], row_more, t, phi, gamma, sqx, got
    )
    chips = [
        [a * targets + 2 * k + c for c in range(2) for a in range(trains)] for k in range(targets // 2)
    ]
    columns = exchange(local, ("train", "target"), chips)

    half = targets // 2
    got, gamma = call(
        functools.partial(project, log_n),
        [(half, CHUNK, 128), row_n],
        (t, train_embed, target_embed, data[2], label_cost, wide, phi, columns, core),
        scratch=[
            pltpu.VMEM((m_dev, 128), jnp.float32),
            pltpu.VMEM((m_dev, 128), jnp.float32),
            pltpu.VMEM((SHARE * half, width), jnp.bfloat16),
            pltpu.VMEM((SHARE * half, 128), jnp.bfloat16),
        ],
        smem=(8,),
        flops=flops,
    )
    got = exchange(got, "target", [[c + 2 * k for k in range(half)] for c in range(2)])
    barycentre, value, potential = call(
        functools.partial(finish, m_dev * trains - 1),
        [(SHARE, width), row_m, row_n],
        (got, phi, gamma, sqx, sqy, columns),
    )
    return (value.reshape(m_dev), potential.reshape(n_dev), barycentre)


def solution(mesh):
    return jax.shard_map(
        on_device,
        mesh=mesh,
        in_specs=(P("train", None), P("train"), P("target", None), P("target"), P()),
        out_specs=(P("train"), P("target"), P(("train", "target"), None)),
        check_vma=False,
    )
```

```python
import functools
import math

import jax
import jax.numpy as jnp
from jax import lax
from jax.experimental import pallas as pl
from jax.experimental.pallas import tpu as pltpu
from jax.sharding import PartitionSpec as P

EPS = 0.05
SCALE = 128.0
KAPPA = math.log2(math.e) / EPS / SCALE
LOG2 = math.log2(math.e) / EPS
LANES = 256
SHARE = 32
CHUNK = 2 * SHARE + 8


def pieces(v):
    hi = v.astype(jnp.bfloat16).astype(jnp.float32)
    rest = v - hi
    mid = rest.astype(jnp.bfloat16).astype(jnp.float32)
    lo = (rest - mid).astype(jnp.bfloat16).astype(jnp.float32)
    return hi, mid, lo


def tail(first, second):
    n = first[0].shape[1]
    row = lax.broadcasted_iota(jnp.int32, (8, n), 0)
    out = jnp.zeros((8, n), jnp.float32)
    for k, v in enumerate(first + second):
        out = jnp.where(row == k, v, out)
    return out


def ones_like3(v):
    return (jnp.ones_like(v),) * 3


def train_rows(label, phi):
    m = label.shape[1]
    onehot = (lax.broadcasted_iota(jnp.int32, (8, m), 0) == label).astype(jnp.float32)
    last = tail(ones_like3(phi), pieces(phi * SCALE))
    return jnp.concatenate([onehot, onehot, onehot, last], axis=0)


def target_rows(label, gamma, label_cost):
    n = label.shape[1]
    table = jnp.zeros((8, n), jnp.float32)
    for b in range(8):
        table = jnp.where(label == b, label_cost[:, b : b + 1], table)
    last = tail(pieces(gamma * SCALE), ones_like3(gamma))
    return jnp.concatenate(list(pieces(table * -SCALE)) + [last], axis=0)


def as_columns(rows):
    pad = jnp.zeros((96, rows.shape[1]), jnp.float32)
    return jnp.concatenate([rows, pad], axis=0).T.astype(jnp.bfloat16)


def as_rows(rows):
    pad = jnp.zeros((96, rows.shape[1]), jnp.float32)
    return jnp.concatenate([rows, pad], axis=0).astype(jnp.bfloat16)


def dot_nt(a, b):
    return lax.dot_general(a, b, (((1,), (1,)), ((), ())), preferred_element_type=jnp.float32)


def dot_nn(a, b):
    return lax.dot_general(a, b, (((1,), (0,)), ((), ())), preferred_element_type=jnp.float32)


def square_means(v):
    sums = jnp.sum(jnp.square(v.astype(jnp.float32)), axis=1, keepdims=True)
    return jnp.broadcast_to(sums * (1.0 / v.shape[1]), (v.shape[0], 128))


def to_everyone(v, out_ref):
    for k in range(out_ref.shape[0]):
        out_ref[k] = v


def in_lanes(v):
    return jnp.concatenate([v[k : k + 1] for k in range(v.shape[0])], axis=1)


def tree(parts, combine):
    while len(parts) > 1:
        parts = [combine(parts[k], parts[k + 1]) for k in range(0, len(parts), 2)]
    return parts[0]


def lse(parts):
    top = tree(parts, jnp.maximum)
    total = tree([jnp.exp((part - top) * (1.0 / EPS)) for part in parts], jnp.add)
    return top + EPS * jnp.log(total)


def lse_received(ref):
    return in_lanes(lse([ref[k] for k in range(ref.shape[0])]))


def sum_received(ref):
    return tree([ref[k] for k in range(ref.shape[0])], jnp.add)


def fetch(pairs, sems):
    copies = [pltpu.make_async_copy(src, dst, sems.at[k]) for k, (src, dst) in enumerate(pairs)]
    for copy in copies:
        copy.start()
    return copies


def wait_all(copies):
    for copy in copies:
        copy.wait()


def rows_first(
    x_any, y_any, lx_any, ly_any, lc_any, core_ref,
    wide_any, out_ref, sqx_ref, sqy_ref, at_ref, x_ref, y_ref, lx_ref, ly_ref, lc_ref, wide_ref, sems,
):
    pairs = [(ly_any, ly_ref), (lc_any, lc_ref), (lx_any, lx_ref), (y_any, y_ref)]
    steps = [slice(k * LANES, (k + 1) * LANES) for k in range(x_ref.shape[0] // LANES)]
    copies = fetch(pairs + [(x_any.at[at, :], x_ref.at[at, :]) for at in steps], sems)
    wait_all(copies[:3])
    rows = as_rows(train_rows(lx_ref[...], jnp.zeros(lx_ref.shape, jnp.float32)))
    columns = as_columns(target_rows(ly_ref[...], jnp.zeros(ly_ref.shape, jnp.float32), lc_ref[...]))
    copies[3].wait()
    y = y_ref[...]
    n, width = y.shape
    wide_ref[0:n, :] = y.astype(jnp.float32)
    wide_ref[n : n + 8, :] = jnp.zeros((8, width), jnp.float32)
    label = ly_ref[...].astype(jnp.float32)
    for k in range(n // width):
        wide_ref[n + k : n + k + 1, :] = label[:, k * width : (k + 1) * width]
    wide = pltpu.make_async_copy(wide_ref, wide_any, sems.at[len(copies)])
    wide.start()
    means = square_means(y)
    norms = jnp.concatenate([means * SCALE] * (LANES // 128), axis=1)
    for k, at in enumerate(steps):
        copies[len(pairs) + k].wait()
        t = dot_nt(y, x_ref[at, :]) + dot_nn(columns, rows[:, at]) - norms
        top = jnp.max(t, axis=0, keepdims=True)
        total = jnp.sum(jnp.exp2((t - top) * KAPPA), axis=0, keepdims=True)
        out = top * (1.0 / SCALE) + EPS * jnp.log(total)
        for r in range(LANES // 128):
            row = k * (LANES // 128) + r
            at_ref[row : row + 1, :] = out[:, r * 128 : (r + 1) * 128]
    sqx_ref[...] = square_means(x_ref[...]).T[0:1]
    sqy_ref[...] = means.T[0:1]
    to_everyone(at_ref[...], out_ref)
    wide.wait()


def in_rows(v):
    return jnp.broadcast_to(v, (128, v.shape[1])).T


def columns_first(log_m, x_ref, y_ref, lx_ref, ly_ref, lc_ref, got_ref, t_ref, out_ref, phi_ref, at_ref):
    zero_m, zero_n = (jnp.zeros(ref.shape, jnp.float32) for ref in (lx_ref, ly_ref))
    phi = -log_m - lse_received(got_ref)
    phi_ref[...] = phi
    down = in_rows(phi * LOG2)
    down = jnp.concatenate([down] * (LANES // 128), axis=1)
    x = x_ref[...]
    columns = as_columns(train_rows(lx_ref[...], zero_m))
    rows = as_rows(target_rows(ly_ref[...], zero_n, lc_ref[...]))
    for k in range(y_ref.shape[0] // LANES):
        at = slice(k * LANES, (k + 1) * LANES)
        t = (dot_nt(x, y_ref[at, :]) + dot_nn(columns, rows[:, at])) * KAPPA
        t_ref[:, at] = t
        t = t + down
        top = jnp.max(t, axis=0, keepdims=True)
        total = jnp.sum(jnp.exp2(t - top), axis=0, keepdims=True)
        out = top * (1.0 / LOG2) + EPS * jnp.log(total)
        for r in range(LANES // 128):
            row = k * (LANES // 128) + r
            at_ref[row : row + 1, :] = out[:, r * 128 : (r + 1) * 128]
    to_everyone(at_ref[...], out_ref)


def rows_next(log_n, t_ref, phi_ref, got_ref, out_ref, gamma_ref, at_ref):
    gamma = -log_n - lse_received(got_ref)
    gamma_ref[...] = gamma
    down = in_rows((phi_ref[...] + log_n) * LOG2)
    across = gamma * LOG2
    for k in range(t_ref.shape[0] // 128):
        rows = slice(k * 128, (k + 1) * 128)
        total = 0.0
        for j in range(t_ref.shape[1] // 128):
            at = slice(j * 128, (j + 1) * 128)
            total = total + jnp.exp2(t_ref[rows, at] + down[rows] + across[:, at])
        at_ref[k : k + 1, :] = jnp.sum(total.T, axis=0, keepdims=True)
    to_everyone(at_ref[...], out_ref)


def columns_next(log_m, log_n, t_ref, phi_ref, gamma_ref, sqx_ref, got_ref, out_ref, new_ref, at_ref):
    n = t_ref.shape[1]
    phi = phi_ref[...] + log_n - log_m - EPS * jnp.log(in_lanes(sum_received(got_ref)))
    new_ref[...] = phi
    down = in_rows(phi * LOG2)
    across = (gamma_ref[...] + log_m) * LOG2
    for k in range(n // 128):
        at = slice(k * 128, (k + 1) * 128)
        at_ref[:, at] = jnp.sum(jnp.exp2(t_ref[:, at] + down + across[:, at]), axis=0, keepdims=True)
    at_ref[:, 0:n] = EPS * jnp.log(at_ref[:, 0:n]) - (gamma_ref[...] + log_m)
    dual_sum = jnp.sum(phi + sqx_ref[...], axis=1, keepdims=True)
    at_ref[:, n : n + 128] = jnp.broadcast_to(dual_sum, (1, 128))
    to_everyone(at_ref[...], out_ref)


def on_diagonal(v):
    shape = (SHARE, 128)
    row, column = (lax.broadcasted_iota(jnp.int32, shape, k) for k in range(2))
    axis = 0 if v.shape[0] == SHARE else 1
    return jnp.sum(jnp.where(row == column, v, 0.0), axis=axis, keepdims=True)


def project(
    log_n, t_ref, x_ref, y_ref, lx_ref, lc_ref, wide_ref, phi_ref, got_ref, core_ref,
    out_ref, gamma_ref, down_ref, aug_ref, xs_ref, xa_ref,
):
    core = core_ref[0]
    n, width = y_ref.shape
    half = got_ref.shape[0] // 2
    first, second = (-log_n - lse([got_ref[2 * k + p, :, 0:n] for k in range(half)]) for p in range(2))
    mine = jnp.where(core == 0, first, second)
    other = jnp.where(core == 0, second, first)
    gamma_ref[...] = mine
    across = mine * LOG2
    down_ref[...] = in_rows((phi_ref[...] + log_n) * LOG2)
    aug_ref[...] = as_columns(train_rows(lx_ref[...], jnp.zeros(lx_ref.shape, jnp.float32))).astype(jnp.float32)
    y = y_ref[...]
    y_other = wide_ref[0:n, :].astype(jnp.bfloat16)
    rows = as_rows(target_rows(in_lanes(wide_ref[n : n + n // width, :]), other, lc_ref[...]))
    chunks = out_ref.shape[0]
    per = min(8, chunks)
    for b in range(chunks // per):
        weights, downs = [], []
        for k in range(per):
            start = pl.multiple_of((2 * (b * per + k) + core) * SHARE, SHARE)
            at, to = pl.ds(start, SHARE), pl.ds((b * per + k) * SHARE, SHARE)
            xs_ref[to, :] = x_ref[at, :]
            xa_ref[to, :] = aug_ref[at, :].astype(jnp.bfloat16)
            downs.append(jnp.concatenate([down_ref[at, :]] * (n // 128), axis=1))
            weights.append(jnp.exp2(t_ref[at, :] + downs[k] + across).astype(jnp.bfloat16))
        w = jnp.concatenate(weights, axis=0)
        block = pl.ds(b * per * SHARE, per * SHARE)
        t = dot_nt(xs_ref[block, :], y_other) + dot_nn(xa_ref[block, :], rows)
        v = jnp.exp2(t * KAPPA + jnp.concatenate(downs, axis=0)).astype(jnp.bfloat16)
        denom = jnp.sum(w.astype(jnp.float32) + v.astype(jnp.float32), axis=1, keepdims=True)
        numer = dot_nn(w, y) + dot_nn(v, y_other)
        for k in range(per):
            part, chunk = slice(k * SHARE, (k + 1) * SHARE), b * per + k
            out_ref[chunk, 0:SHARE, :] = numer[part, 0:128]
            out_ref[chunk, SHARE : 2 * SHARE, :] = numer[part, 128:256]
            out_ref[chunk, 2 * SHARE : CHUNK, :] = jnp.broadcast_to(on_diagonal(denom[part]), (CHUNK - 2 * SHARE, 128))


def finish(others, got_ref, phi_ref, gamma_ref, sqx_ref, sqy_ref, columns_ref, out_ref, value_ref, potential_ref):
    total = sum_received(got_ref)
    denom = on_diagonal(total[2 * SHARE : 2 * SHARE + 1])
    out_ref[:, 0:128] = total[0:SHARE] / denom
    out_ref[:, 128:256] = total[SHARE : 2 * SHARE] / denom
    n = gamma_ref.shape[1]
    potential_ref[...] = gamma_ref[...] + sqy_ref[...]
    dual = phi_ref[...] + sqx_ref[...]
    dual_sum = tree([columns_ref[2 * k, :, n : n + 1] for k in range(columns_ref.shape[0] // 2)], jnp.add)
    value_ref[...] = dual - (dual_sum - dual) / others


def call(body, outs, args, scratch=(), smem=(), anywhere=(), anywhere_out=(), flops=0, limit=40):
    vmem = pl.BlockSpec(memory_space=pltpu.VMEM)
    specs = [vmem for _ in args]
    for k in smem:
        specs[k] = pl.BlockSpec(memory_space=pltpu.SMEM)
    for k in anywhere:
        specs[k] = pl.BlockSpec(memory_space=pl.ANY)
    out_specs = [pl.BlockSpec(memory_space=pl.ANY) if k in anywhere_out else vmem for k in range(len(outs))]
    outs = [s if hasattr(s, "dtype") else jax.ShapeDtypeStruct(s, jnp.float32) for s in outs]
    return pl.pallas_call(
        body,
        out_shape=outs,
        in_specs=specs,
        out_specs=out_specs,
        scratch_shapes=list(scratch),
        compiler_params=pltpu.CompilerParams(vmem_limit_bytes=int(limit * 2**20)),
        cost_estimate=pl.CostEstimate(flops=flops, bytes_accessed=2**20, transcendentals=flops // 512),
    )(*args)


def exchange(x, axis, groups=None):
    return lax.all_to_all(x, axis, 0, 0, axis_index_groups=groups, tiled=True)


def on_device(train_embed, train_label, target_embed, target_label, label_cost):
    m_dev, width = train_embed.shape
    n_dev = target_embed.shape[0]
    trains = lax.axis_size("train")
    targets = lax.axis_size("target")
    log_m = EPS * math.log(m_dev * trains)
    log_n = EPS * math.log(n_dev * targets)
    data = (
        train_embed,
        target_embed,
        train_label.reshape(1, m_dev),
        target_label.reshape(1, n_dev),
        label_cost,
    )
    row_m, row_n = (1, m_dev), (1, n_dev)
    tile_m, tile_n = (m_dev // 128, 128), (n_dev // 128, 128)
    flops = 2 * m_dev * n_dev * 512

    def run(body, outs, tile, *args):
        return call(body, outs, args, scratch=[pltpu.VMEM(tile, jnp.float32)], flops=flops)

    core = (lax.axis_index("target").astype(jnp.int32) & 1).reshape(1)
    wide_shape = (n_dev + 8, width)
    wide, local, sqx, sqy = call(
        rows_first,
        [wide_shape, (targets,) + tile_m, row_m, row_n],
        (*data, core),
        scratch=[pltpu.VMEM(tile_m, jnp.float32)]
        + [pltpu.VMEM(v.shape, v.dtype) for v in data]
        + [pltpu.VMEM(wide_shape, jnp.float32), pltpu.SemaphoreType.DMA((len(data) + m_dev // LANES,))],
        anywhere=range(len(data)),
        anywhere_out=(0,),
        smem=(len(data),),
        flops=flops,
        limit=54,
    )
    wide = lax.ppermute(wide, "target", [(k, k ^ 1) for k in range(targets)])
    got = exchange(local, "target")
    t, local, phi = run(
        functools.partial(columns_first, log_m), [(m_dev, n_dev), (trains,) + tile_n, row_m], tile_n, *data, got
    )
    got = exchange(local, "train")
    local, gamma = run(functools.partial(rows_next, log_n), [(targets,) + tile_m, row_n], tile_m, t, phi, got)
    got = exchange(local, "target")
    row_more = (1, n_dev + 128)
    local, phi = run(
        functools.partial(columns_next, log_m, log_n), [(2 * trains,) + row_more, row_m], row_more, t, phi, gamma, sqx, got
    )
    chips = [
        [a * targets + 2 * k + c for a in range(trains) for c in range(2)] for k in range(targets // 2)
    ]
    columns = exchange(local, ("train", "target"), chips)

    half = targets // 2
    got, gamma = call(
        functools.partial(project, log_n),
        [(half, CHUNK, 128), row_n],
        (t, train_embed, target_embed, data[2], label_cost, wide, phi, columns, core),
        scratch=[
            pltpu.VMEM((m_dev, 128), jnp.float32),
            pltpu.VMEM((m_dev, 128), jnp.float32),
            pltpu.VMEM((SHARE * half, width), jnp.bfloat16),
            pltpu.VMEM((SHARE * half, 128), jnp.bfloat16),
        ],
        smem=(8,),
        flops=flops,
    )
    got = exchange(got, "target", [[c + 2 * k for k in range(half)] for c in range(2)])
    barycentre, value, potential = call(
        functools.partial(finish, m_dev * trains - 1),
        [(SHARE, width), row_m, row_n],
        (got, phi, gamma, sqx, sqy, columns),
    )
    return (value.reshape(m_dev), potential.reshape(n_dev), barycentre)


def solution(mesh):
    return jax.shard_map(
        on_device,
        mesh=mesh,
        in_specs=(P("train", None), P("train"), P("target", None), P("target"), P()),
        out_specs=(P("train"), P("target"), P(("train", "target"), None)),
        check_vma=False,
    )
```

```python
import functools
import math

import jax
import jax.numpy as jnp
from jax import lax
from jax.experimental import pallas as pl
from jax.experimental.pallas import tpu as pltpu
from jax.sharding import PartitionSpec as P

EPS = 0.05
SCALE = 128.0
KAPPA = math.log2(math.e) / EPS / SCALE
LOG2 = math.log2(math.e) / EPS
LANES = 256
SHARE = 32
CHUNK = 2 * SHARE + 8


def pieces(v):
    hi = v.astype(jnp.bfloat16).astype(jnp.float32)
    rest = v - hi
    mid = rest.astype(jnp.bfloat16).astype(jnp.float32)
    lo = (rest - mid).astype(jnp.bfloat16).astype(jnp.float32)
    return hi, mid, lo


def tail(first, second):
    n = first[0].shape[1]
    row = lax.broadcasted_iota(jnp.int32, (8, n), 0)
    out = jnp.zeros((8, n), jnp.float32)
    for k, v in enumerate(first + second):
        out = jnp.where(row == k, v, out)
    return out


def ones_like3(v):
    return (jnp.ones_like(v),) * 3


def train_rows(label, phi):
    m = label.shape[1]
    onehot = (lax.broadcasted_iota(jnp.int32, (8, m), 0) == label).astype(jnp.float32)
    last = tail(ones_like3(phi), pieces(phi * SCALE))
    return jnp.concatenate([onehot, onehot, onehot, last], axis=0)


def target_rows(label, gamma, label_cost):
    n = label.shape[1]
    table = jnp.zeros((8, n), jnp.float32)
    for b in range(8):
        table = jnp.where(label == b, label_cost[:, b : b + 1], table)
    last = tail(pieces(gamma * SCALE), ones_like3(gamma))
    return jnp.concatenate(list(pieces(table * -SCALE)) + [last], axis=0)


def as_columns(rows):
    pad = jnp.zeros((96, rows.shape[1]), jnp.float32)
    return jnp.concatenate([rows, pad], axis=0).T.astype(jnp.bfloat16)


def as_rows(rows):
    pad = jnp.zeros((96, rows.shape[1]), jnp.float32)
    return jnp.concatenate([rows, pad], axis=0).astype(jnp.bfloat16)


def dot_nt(a, b):
    return lax.dot_general(a, b, (((1,), (1,)), ((), ())), preferred_element_type=jnp.float32)


def dot_nn(a, b):
    return lax.dot_general(a, b, (((1,), (0,)), ((), ())), preferred_element_type=jnp.float32)


def square_means(v):
    sums = jnp.sum(jnp.square(v.astype(jnp.float32)), axis=1, keepdims=True)
    return jnp.broadcast_to(sums * (1.0 / v.shape[1]), (v.shape[0], 128))


def to_everyone(v, out_ref):
    for k in range(out_ref.shape[0]):
        out_ref[k] = v


def in_lanes(v):
    return jnp.concatenate([v[k : k + 1] for k in range(v.shape[0])], axis=1)


def tree(parts, combine):
    while len(parts) > 1:
        parts = [combine(parts[k], parts[k + 1]) for k in range(0, len(parts), 2)]
    return parts[0]


def lse(parts):
    top = tree(parts, jnp.maximum)
    total = tree([jnp.exp((part - top) * (1.0 / EPS)) for part in parts], jnp.add)
    return top + EPS * jnp.log(total)


def lse_received(ref):
    return in_lanes(lse([ref[k] for k in range(ref.shape[0])]))


def sum_received(ref):
    return tree([ref[k] for k in range(ref.shape[0])], jnp.add)


def fetch(pairs, sems):
    copies = [pltpu.make_async_copy(src, dst, sems.at[k]) for k, (src, dst) in enumerate(pairs)]
    for copy in copies:
        copy.start()
    return copies


def wait_all(copies):
    for copy in copies:
        copy.wait()


def rows_first(
    x_any, y_any, lx_any, ly_any, lc_any, core_ref,
    wide_any, out_ref, sqx_ref, sqy_ref, at_ref, x_ref, y_ref, lx_ref, ly_ref, lc_ref, wide_ref, sems,
):
    pairs = [(ly_any, ly_ref), (lc_any, lc_ref), (lx_any, lx_ref), (y_any, y_ref), (x_any, x_ref)]
    copies = fetch(pairs, sems)
    wait_all(copies[:3])
    rows = as_rows(train_rows(lx_ref[...], jnp.zeros(lx_ref.shape, jnp.float32)))
    columns = as_columns(target_rows(ly_ref[...], jnp.zeros(ly_ref.shape, jnp.float32), lc_ref[...]))
    copies[3].wait()
    y = y_ref[...]
    n, width = y.shape
    wide_ref[0:n, :] = y.astype(jnp.float32)
    wide_ref[n : n + 8, :] = jnp.zeros((8, width), jnp.float32)
    label = ly_ref[...].astype(jnp.float32)
    for k in range(n // width):
        wide_ref[n + k : n + k + 1, :] = label[:, k * width : (k + 1) * width]
    wide = pltpu.make_async_copy(wide_ref, wide_any, sems.at[len(copies)])
    wide.start()
    copies[4].wait()
    means = square_means(y)
    norms = jnp.concatenate([means * SCALE] * (LANES // 128), axis=1)
    for k in range(x_ref.shape[0] // LANES):
        at = slice(k * LANES, (k + 1) * LANES)
        t = dot_nt(y, x_ref[at, :]) + dot_nn(columns, rows[:, at]) - norms
        top = jnp.max(t, axis=0, keepdims=True)
        total = jnp.sum(jnp.exp2((t - top) * KAPPA), axis=0, keepdims=True)
        out = top * (1.0 / SCALE) + EPS * jnp.log(total)
        for r in range(LANES // 128):
            row = k * (LANES // 128) + r
            at_ref[row : row + 1, :] = out[:, r * 128 : (r + 1) * 128]
    sqx_ref[...] = square_means(x_ref[...]).T[0:1]
    sqy_ref[...] = means.T[0:1]
    to_everyone(at_ref[...], out_ref)
    wide.wait()


def in_rows(v):
    return jnp.broadcast_to(v, (128, v.shape[1])).T


def columns_first(log_m, x_ref, y_ref, lx_ref, ly_ref, lc_ref, got_ref, t_ref, out_ref, phi_ref, at_ref):
    zero_m, zero_n = (jnp.zeros(ref.shape, jnp.float32) for ref in (lx_ref, ly_ref))
    phi = -log_m - lse_received(got_ref)
    phi_ref[...] = phi
    down = in_rows(phi * LOG2)
    down = jnp.concatenate([down] * (LANES // 128), axis=1)
    x = x_ref[...]
    columns = as_columns(train_rows(lx_ref[...], zero_m))
    rows = as_rows(target_rows(ly_ref[...], zero_n, lc_ref[...]))
    for k in range(y_ref.shape[0] // LANES):
        at = slice(k * LANES, (k + 1) * LANES)
        t = (dot_nt(x, y_ref[at, :]) + dot_nn(columns, rows[:, at])) * KAPPA
        t_ref[:, at] = t
        t = t + down
        top = jnp.max(t, axis=0, keepdims=True)
        total = jnp.sum(jnp.exp2(t - top), axis=0, keepdims=True)
        out = top * (1.0 / LOG2) + EPS * jnp.log(total)
        for r in range(LANES // 128):
            row = k * (LANES // 128) + r
            at_ref[row : row + 1, :] = out[:, r * 128 : (r + 1) * 128]
    to_everyone(at_ref[...], out_ref)


def rows_next(log_n, t_ref, phi_ref, got_ref, out_ref, gamma_ref, at_ref):
    gamma = -log_n - lse_received(got_ref)
    gamma_ref[...] = gamma
    down = in_rows((phi_ref[...] + log_n) * LOG2)
    across = gamma * LOG2
    for k in range(t_ref.shape[0] // 128):
        rows = slice(k * 128, (k + 1) * 128)
        total = 0.0
        for j in range(t_ref.shape[1] // 128):
            at = slice(j * 128, (j + 1) * 128)
            total = total + jnp.exp2(t_ref[rows, at] + down[rows] + across[:, at])
        at_ref[k : k + 1, :] = jnp.sum(total.T, axis=0, keepdims=True)
    to_everyone(at_ref[...], out_ref)


def columns_next(log_m, log_n, t_ref, phi_ref, gamma_ref, sqx_ref, got_ref, out_ref, new_ref, at_ref):
    n = t_ref.shape[1]
    phi = phi_ref[...] + log_n - log_m - EPS * jnp.log(in_lanes(sum_received(got_ref)))
    new_ref[...] = phi
    down = in_rows(phi * LOG2)
    across = (gamma_ref[...] + log_m) * LOG2
    for k in range(n // 128):
        at = slice(k * 128, (k + 1) * 128)
        at_ref[:, at] = jnp.sum(jnp.exp2(t_ref[:, at] + down + across[:, at]), axis=0, keepdims=True)
    at_ref[:, 0:n] = EPS * jnp.log(at_ref[:, 0:n]) - (gamma_ref[...] + log_m)
    dual_sum = jnp.sum(phi + sqx_ref[...], axis=1, keepdims=True)
    at_ref[:, n : n + 128] = jnp.broadcast_to(dual_sum, (1, 128))
    to_everyone(at_ref[...], out_ref)


def on_diagonal(v):
    shape = (SHARE, 128)
    row, column = (lax.broadcasted_iota(jnp.int32, shape, k) for k in range(2))
    axis = 0 if v.shape[0] == SHARE else 1
    return jnp.sum(jnp.where(row == column, v, 0.0), axis=axis, keepdims=True)


def project(
    log_n, t_ref, x_ref, y_ref, lx_ref, lc_ref, wide_ref, phi_ref, got_ref, core_ref,
    out_ref, gamma_ref, down_ref, aug_ref, xs_ref, xa_ref,
):
    core = core_ref[0]
    n, width = y_ref.shape
    half = got_ref.shape[0] // 2
    first, second = (-log_n - lse([got_ref[2 * k + p, :, 0:n] for k in range(half)]) for p in range(2))
    mine = jnp.where(core == 0, first, second)
    other = jnp.where(core == 0, second, first)
    gamma_ref[...] = mine
    across = mine * LOG2
    down_ref[...] = in_rows((phi_ref[...] + log_n) * LOG2)
    aug_ref[...] = as_columns(train_rows(lx_ref[...], jnp.zeros(lx_ref.shape, jnp.float32))).astype(jnp.float32)
    y = y_ref[...]
    y_other = wide_ref[0:n, :].astype(jnp.bfloat16)
    rows = as_rows(target_rows(in_lanes(wide_ref[n : n + n // width, :]), other, lc_ref[...]))
    chunks = out_ref.shape[0]
    per = min(8, chunks)
    for b in range(chunks // per):
        weights, downs = [], []
        for k in range(per):
            start = pl.multiple_of((2 * (b * per + k) + core) * SHARE, SHARE)
            at, to = pl.ds(start, SHARE), pl.ds((b * per + k) * SHARE, SHARE)
            xs_ref[to, :] = x_ref[at, :]
            xa_ref[to, :] = aug_ref[at, :].astype(jnp.bfloat16)
            downs.append(jnp.concatenate([down_ref[at, :]] * (n // 128), axis=1))
            weights.append(jnp.exp2(t_ref[at, :] + downs[k] + across).astype(jnp.bfloat16))
        w = jnp.concatenate(weights, axis=0)
        block = pl.ds(b * per * SHARE, per * SHARE)
        t = dot_nt(xs_ref[block, :], y_other) + dot_nn(xa_ref[block, :], rows)
        v = jnp.exp2(t * KAPPA + jnp.concatenate(downs, axis=0)).astype(jnp.bfloat16)
        denom = jnp.sum(w.astype(jnp.float32) + v.astype(jnp.float32), axis=1, keepdims=True)
        numer = dot_nn(w, y) + dot_nn(v, y_other)
        for k in range(per):
            part, chunk = slice(k * SHARE, (k + 1) * SHARE), b * per + k
            out_ref[chunk, 0:SHARE, :] = numer[part, 0:128]
            out_ref[chunk, SHARE : 2 * SHARE, :] = numer[part, 128:256]
            out_ref[chunk, 2 * SHARE : CHUNK, :] = jnp.broadcast_to(on_diagonal(denom[part]), (CHUNK - 2 * SHARE, 128))


def finish(others, got_ref, phi_ref, gamma_ref, sqx_ref, sqy_ref, columns_ref, out_ref, value_ref, potential_ref):
    total = sum_received(got_ref)
    denom = on_diagonal(total[2 * SHARE : 2 * SHARE + 1])
    out_ref[:, 0:128] = total[0:SHARE] / denom
    out_ref[:, 128:256] = total[SHARE : 2 * SHARE] / denom
    n = gamma_ref.shape[1]
    potential_ref[...] = gamma_ref[...] + sqy_ref[...]
    dual = phi_ref[...] + sqx_ref[...]
    dual_sum = tree([columns_ref[2 * k, :, n : n + 1] for k in range(columns_ref.shape[0] // 2)], jnp.add)
    value_ref[...] = dual - (dual_sum - dual) / others


def call(body, outs, args, scratch=(), smem=(), anywhere=(), anywhere_out=(), flops=0, limit=40):
    vmem = pl.BlockSpec(memory_space=pltpu.VMEM)
    specs = [vmem for _ in args]
    for k in smem:
        specs[k] = pl.BlockSpec(memory_space=pltpu.SMEM)
    for k in anywhere:
        specs[k] = pl.BlockSpec(memory_space=pl.ANY)
    out_specs = [pl.BlockSpec(memory_space=pl.ANY) if k in anywhere_out else vmem for k in range(len(outs))]
    outs = [s if hasattr(s, "dtype") else jax.ShapeDtypeStruct(s, jnp.float32) for s in outs]
    return pl.pallas_call(
        body,
        out_shape=outs,
        in_specs=specs,
        out_specs=out_specs,
        scratch_shapes=list(scratch),
        compiler_params=pltpu.CompilerParams(vmem_limit_bytes=int(limit * 2**20)),
        cost_estimate=pl.CostEstimate(flops=flops, bytes_accessed=2**20, transcendentals=flops // 512),
    )(*args)


def exchange(x, axis, groups=None):
    return lax.all_to_all(x, axis, 0, 0, axis_index_groups=groups, tiled=True)


def on_device(train_embed, train_label, target_embed, target_label, label_cost):
    m_dev, width = train_embed.shape
    n_dev = target_embed.shape[0]
    trains = lax.axis_size("train")
    targets = lax.axis_size("target")
    log_m = EPS * math.log(m_dev * trains)
    log_n = EPS * math.log(n_dev * targets)
    data = (
        train_embed,
        target_embed,
        train_label.reshape(1, m_dev),
        target_label.reshape(1, n_dev),
        label_cost,
    )
    row_m, row_n = (1, m_dev), (1, n_dev)
    tile_m, tile_n = (m_dev // 128, 128), (n_dev // 128, 128)
    flops = 2 * m_dev * n_dev * 512

    def run(body, outs, tile, *args):
        return call(body, outs, args, scratch=[pltpu.VMEM(tile, jnp.float32)], flops=flops)

    core = (lax.axis_index("target").astype(jnp.int32) & 1).reshape(1)
    wide_shape = (n_dev + 8, width)
    wide, local, sqx, sqy = call(
        rows_first,
        [wide_shape, (targets,) + tile_m, row_m, row_n],
        (*data, core),
        scratch=[pltpu.VMEM(tile_m, jnp.float32)]
        + [pltpu.VMEM(v.shape, v.dtype) for v in data]
        + [pltpu.VMEM(wide_shape, jnp.float32), pltpu.SemaphoreType.DMA((len(data) + 1,))],
        anywhere=range(len(data)),
        anywhere_out=(0,),
        smem=(len(data),),
        flops=flops,
        limit=54,
    )
    wide = lax.ppermute(wide, "target", [(k, k ^ 1) for k in range(targets)])
    got = exchange(local, "target")
    t, local, phi = run(
        functools.partial(columns_first, log_m), [(m_dev, n_dev), (trains,) + tile_n, row_m], tile_n, *data, got
    )
    got = exchange(local, "train")
    local, gamma = run(functools.partial(rows_next, log_n), [(targets,) + tile_m, row_n], tile_m, t, phi, got)
    got = exchange(local, "target")
    row_more = (1, n_dev + 128)
    local, phi = run(
        functools.partial(columns_next, log_m, log_n), [(2 * trains,) + row_more, row_m], row_more, t, phi, gamma, sqx, got
    )
    chips = [
        [a * targets + 2 * k + c for a in range(trains) for c in range(2)] for k in range(targets // 2)
    ]
    columns = exchange(local, ("train", "target"), chips)

    half = targets // 2
    got, gamma = call(
        functools.partial(project, log_n),
        [(half, CHUNK, 128), row_n],
        (t, train_embed, target_embed, data[2], label_cost, wide, phi, columns, core),
        scratch=[
            pltpu.VMEM((m_dev, 128), jnp.float32),
            pltpu.VMEM((m_dev, 128), jnp.float32),
            pltpu.VMEM((SHARE * half, width), jnp.bfloat16),
            pltpu.VMEM((SHARE * half, 128), jnp.bfloat16),
        ],
        smem=(8,),
        flops=flops,
    )
    got = exchange(got, "target", [[c + 2 * k for k in range(half)] for c in range(2)])
    barycentre, value, potential = call(
        functools.partial(finish, m_dev * trains - 1),
        [(SHARE, width), row_m, row_n],
        (got, phi, gamma, sqx, sqy, columns),
    )
    return (value.reshape(m_dev), potential.reshape(n_dev), barycentre)


def solution(mesh):
    return jax.shard_map(
        on_device,
        mesh=mesh,
        in_specs=(P("train", None), P("train"), P("target", None), P("target"), P()),
        out_specs=(P("train"), P("target"), P(("train", "target"), None)),
        check_vma=False,
    )
```

```python
import functools
import math

import jax
import jax.numpy as jnp
from jax import lax
from jax.experimental import pallas as pl
from jax.experimental.pallas import tpu as pltpu
from jax.sharding import PartitionSpec as P

EPS = 0.05
SCALE = 128.0
KAPPA = math.log2(math.e) / EPS / SCALE
LOG2 = math.log2(math.e) / EPS
LANES = 512
SHARE = 32
CHUNK = 2 * SHARE + 8


def pieces(v):
    hi = v.astype(jnp.bfloat16).astype(jnp.float32)
    rest = v - hi
    mid = rest.astype(jnp.bfloat16).astype(jnp.float32)
    lo = (rest - mid).astype(jnp.bfloat16).astype(jnp.float32)
    return hi, mid, lo


def tail(first, second):
    n = first[0].shape[1]
    row = lax.broadcasted_iota(jnp.int32, (8, n), 0)
    out = jnp.zeros((8, n), jnp.float32)
    for k, v in enumerate(first + second):
        out = jnp.where(row == k, v, out)
    return out


def ones_like3(v):
    return (jnp.ones_like(v),) * 3


def train_rows(label, phi):
    m = label.shape[1]
    onehot = (lax.broadcasted_iota(jnp.int32, (8, m), 0) == label).astype(jnp.float32)
    last = tail(ones_like3(phi), pieces(phi * SCALE))
    return jnp.concatenate([onehot, onehot, onehot, last], axis=0)


def target_rows(label, gamma, label_cost):
    n = label.shape[1]
    table = jnp.zeros((8, n), jnp.float32)
    for b in range(8):
        table = jnp.where(label == b, label_cost[:, b : b + 1], table)
    last = tail(pieces(gamma * SCALE), ones_like3(gamma))
    return jnp.concatenate(list(pieces(table * -SCALE)) + [last], axis=0)


def as_columns(rows):
    pad = jnp.zeros((96, rows.shape[1]), jnp.float32)
    return jnp.concatenate([rows, pad], axis=0).T.astype(jnp.bfloat16)


def as_rows(rows):
    pad = jnp.zeros((96, rows.shape[1]), jnp.float32)
    return jnp.concatenate([rows, pad], axis=0).astype(jnp.bfloat16)


def dot_nt(a, b):
    return lax.dot_general(a, b, (((1,), (1,)), ((), ())), preferred_element_type=jnp.float32)


def dot_nn(a, b):
    return lax.dot_general(a, b, (((1,), (0,)), ((), ())), preferred_element_type=jnp.float32)


def square_means(v):
    sums = jnp.sum(jnp.square(v.astype(jnp.float32)), axis=1, keepdims=True)
    return jnp.broadcast_to(sums * (1.0 / v.shape[1]), (v.shape[0], 128))


def to_everyone(v, out_ref):
    for k in range(out_ref.shape[0]):
        out_ref[k] = v


def in_lanes(v):
    return jnp.concatenate([v[k : k + 1] for k in range(v.shape[0])], axis=1)


def tree(parts, combine):
    while len(parts) > 1:
        parts = [combine(parts[k], parts[k + 1]) for k in range(0, len(parts), 2)]
    return parts[0]


def lse(parts):
    top = tree(parts, jnp.maximum)
    total = tree([jnp.exp((part - top) * (1.0 / EPS)) for part in parts], jnp.add)
    return top + EPS * jnp.log(total)


def lse_received(ref):
    return in_lanes(lse([ref[k] for k in range(ref.shape[0])]))


def sum_received(ref):
    return tree([ref[k] for k in range(ref.shape[0])], jnp.add)


def fetch(pairs, sems):
    copies = [pltpu.make_async_copy(src, dst, sems.at[k]) for k, (src, dst) in enumerate(pairs)]
    for copy in copies:
        copy.start()
    return copies


def wait_all(copies):
    for copy in copies:
        copy.wait()


def rows_first(
    x_any, y_any, lx_any, ly_any, lc_any, core_ref,
    wide_any, out_ref, sqx_ref, sqy_ref, at_ref, x_ref, y_ref, lx_ref, ly_ref, lc_ref, wide_ref, sems,
):
    pairs = [(ly_any, ly_ref), (lc_any, lc_ref), (lx_any, lx_ref), (y_any, y_ref), (x_any, x_ref)]
    copies = fetch(pairs, sems)
    wait_all(copies[:3])
    rows = as_rows(train_rows(lx_ref[...], jnp.zeros(lx_ref.shape, jnp.float32)))
    columns = as_columns(target_rows(ly_ref[...], jnp.zeros(ly_ref.shape, jnp.float32), lc_ref[...]))
    copies[3].wait()
    y = y_ref[...]
    n, width = y.shape
    wide_ref[0:n, :] = y.astype(jnp.float32)
    wide_ref[n : n + 8, :] = jnp.zeros((8, width), jnp.float32)
    label = ly_ref[...].astype(jnp.float32)
    for k in range(n // width):
        wide_ref[n + k : n + k + 1, :] = label[:, k * width : (k + 1) * width]
    wide = pltpu.make_async_copy(wide_ref, wide_any, sems.at[len(copies)])
    wide.start()
    copies[4].wait()
    means = square_means(y)
    norms = jnp.concatenate([means * SCALE] * (LANES // 128), axis=1)
    for k in range(x_ref.shape[0] // LANES):
        at = slice(k * LANES, (k + 1) * LANES)
        t = dot_nt(y, x_ref[at, :]) + dot_nn(columns, rows[:, at]) - norms
        top = jnp.max(t, axis=0, keepdims=True)
        total = jnp.sum(jnp.exp2((t - top) * KAPPA), axis=0, keepdims=True)
        out = top * (1.0 / SCALE) + EPS * jnp.log(total)
        for r in range(LANES // 128):
            row = k * (LANES // 128) + r
            at_ref[row : row + 1, :] = out[:, r * 128 : (r + 1) * 128]
    sqx_ref[...] = square_means(x_ref[...]).T[0:1]
    sqy_ref[...] = means.T[0:1]
    to_everyone(at_ref[...], out_ref)
    wide.wait()


def in_rows(v):
    return jnp.broadcast_to(v, (128, v.shape[1])).T


def columns_first(log_m, x_ref, y_ref, lx_ref, ly_ref, lc_ref, got_ref, t_ref, out_ref, phi_ref, at_ref):
    zero_m, zero_n = (jnp.zeros(ref.shape, jnp.float32) for ref in (lx_ref, ly_ref))
    phi = -log_m - lse_received(got_ref)
    phi_ref[...] = phi
    down = in_rows(phi * LOG2)
    down = jnp.concatenate([down] * (LANES // 128), axis=1)
    x = x_ref[...]
    columns = as_columns(train_rows(lx_ref[...], zero_m))
    rows = as_rows(target_rows(ly_ref[...], zero_n, lc_ref[...]))
    for k in range(y_ref.shape[0] // LANES):
        at = slice(k * LANES, (k + 1) * LANES)
        t = (dot_nt(x, y_ref[at, :]) + dot_nn(columns, rows[:, at])) * KAPPA
        t_ref[:, at] = t
        t = t + down
        top = jnp.max(t, axis=0, keepdims=True)
        total = jnp.sum(jnp.exp2(t - top), axis=0, keepdims=True)
        out = top * (1.0 / LOG2) + EPS * jnp.log(total)
        for r in range(LANES // 128):
            row = k * (LANES // 128) + r
            at_ref[row : row + 1, :] = out[:, r * 128 : (r + 1) * 128]
    to_everyone(at_ref[...], out_ref)


def rows_next(log_n, t_ref, phi_ref, got_ref, out_ref, gamma_ref, at_ref):
    gamma = -log_n - lse_received(got_ref)
    gamma_ref[...] = gamma
    down = in_rows((phi_ref[...] + log_n) * LOG2)
    across = gamma * LOG2
    for k in range(t_ref.shape[0] // 128):
        rows = slice(k * 128, (k + 1) * 128)
        total = 0.0
        for j in range(t_ref.shape[1] // 128):
            at = slice(j * 128, (j + 1) * 128)
            total = total + jnp.exp2(t_ref[rows, at] + down[rows] + across[:, at])
        at_ref[k : k + 1, :] = jnp.sum(total.T, axis=0, keepdims=True)
    to_everyone(at_ref[...], out_ref)


def columns_next(log_m, log_n, t_ref, phi_ref, gamma_ref, sqx_ref, got_ref, out_ref, new_ref, at_ref):
    n = t_ref.shape[1]
    phi = phi_ref[...] + log_n - log_m - EPS * jnp.log(in_lanes(sum_received(got_ref)))
    new_ref[...] = phi
    down = in_rows(phi * LOG2)
    across = (gamma_ref[...] + log_m) * LOG2
    for k in range(n // 128):
        at = slice(k * 128, (k + 1) * 128)
        at_ref[:, at] = jnp.sum(jnp.exp2(t_ref[:, at] + down + across[:, at]), axis=0, keepdims=True)
    at_ref[:, 0:n] = EPS * jnp.log(at_ref[:, 0:n]) - (gamma_ref[...] + log_m)
    dual_sum = jnp.sum(phi + sqx_ref[...], axis=1, keepdims=True)
    at_ref[:, n : n + 128] = jnp.broadcast_to(dual_sum, (1, 128))
    to_everyone(at_ref[...], out_ref)


def on_diagonal(v):
    shape = (SHARE, 128)
    row, column = (lax.broadcasted_iota(jnp.int32, shape, k) for k in range(2))
    axis = 0 if v.shape[0] == SHARE else 1
    return jnp.sum(jnp.where(row == column, v, 0.0), axis=axis, keepdims=True)


def project(
    log_n, t_ref, x_ref, y_ref, lx_ref, lc_ref, wide_ref, phi_ref, got_ref, core_ref,
    out_ref, gamma_ref, down_ref, aug_ref, xs_ref, xa_ref,
):
    core = core_ref[0]
    n, width = y_ref.shape
    half = got_ref.shape[0] // 2
    first, second = (-log_n - lse([got_ref[2 * k + p, :, 0:n] for k in range(half)]) for p in range(2))
    mine = jnp.where(core == 0, first, second)
    other = jnp.where(core == 0, second, first)
    gamma_ref[...] = mine
    across = mine * LOG2
    down_ref[...] = in_rows((phi_ref[...] + log_n) * LOG2)
    aug_ref[...] = as_columns(train_rows(lx_ref[...], jnp.zeros(lx_ref.shape, jnp.float32))).astype(jnp.float32)
    y = y_ref[...]
    y_other = wide_ref[0:n, :].astype(jnp.bfloat16)
    rows = as_rows(target_rows(in_lanes(wide_ref[n : n + n // width, :]), other, lc_ref[...]))
    chunks = out_ref.shape[0]
    per = min(16, chunks)
    for b in range(chunks // per):
        weights, downs = [], []
        for k in range(per):
            start = pl.multiple_of((2 * (b * per + k) + core) * SHARE, SHARE)
            at, to = pl.ds(start, SHARE), pl.ds((b * per + k) * SHARE, SHARE)
            xs_ref[to, :] = x_ref[at, :]
            xa_ref[to, :] = aug_ref[at, :].astype(jnp.bfloat16)
            downs.append(jnp.concatenate([down_ref[at, :]] * (n // 128), axis=1))
            weights.append(jnp.exp2(t_ref[at, :] + downs[k] + across).astype(jnp.bfloat16))
        w = jnp.concatenate(weights, axis=0)
        block = pl.ds(b * per * SHARE, per * SHARE)
        t = dot_nt(xs_ref[block, :], y_other) + dot_nn(xa_ref[block, :], rows)
        v = jnp.exp2(t * KAPPA + jnp.concatenate(downs, axis=0)).astype(jnp.bfloat16)
        denom = jnp.sum(w.astype(jnp.float32) + v.astype(jnp.float32), axis=1, keepdims=True)
        numer = dot_nn(w, y) + dot_nn(v, y_other)
        for k in range(per):
            part, chunk = slice(k * SHARE, (k + 1) * SHARE), b * per + k
            out_ref[chunk, 0:SHARE, :] = numer[part, 0:128]
            out_ref[chunk, SHARE : 2 * SHARE, :] = numer[part, 128:256]
            out_ref[chunk, 2 * SHARE : CHUNK, :] = jnp.broadcast_to(on_diagonal(denom[part]), (CHUNK - 2 * SHARE, 128))


def finish(others, got_ref, phi_ref, gamma_ref, sqx_ref, sqy_ref, columns_ref, out_ref, value_ref, potential_ref):
    total = sum_received(got_ref)
    denom = on_diagonal(total[2 * SHARE : 2 * SHARE + 1])
    out_ref[:, 0:128] = total[0:SHARE] / denom
    out_ref[:, 128:256] = total[SHARE : 2 * SHARE] / denom
    n = gamma_ref.shape[1]
    potential_ref[...] = gamma_ref[...] + sqy_ref[...]
    dual = phi_ref[...] + sqx_ref[...]
    dual_sum = tree([columns_ref[2 * k, :, n : n + 1] for k in range(columns_ref.shape[0] // 2)], jnp.add)
    value_ref[...] = dual - (dual_sum - dual) / others


def call(body, outs, args, scratch=(), smem=(), anywhere=(), anywhere_out=(), flops=0, limit=40):
    vmem = pl.BlockSpec(memory_space=pltpu.VMEM)
    specs = [vmem for _ in args]
    for k in smem:
        specs[k] = pl.BlockSpec(memory_space=pltpu.SMEM)
    for k in anywhere:
        specs[k] = pl.BlockSpec(memory_space=pl.ANY)
    out_specs = [pl.BlockSpec(memory_space=pl.ANY) if k in anywhere_out else vmem for k in range(len(outs))]
    outs = [s if hasattr(s, "dtype") else jax.ShapeDtypeStruct(s, jnp.float32) for s in outs]
    return pl.pallas_call(
        body,
        out_shape=outs,
        in_specs=specs,
        out_specs=out_specs,
        scratch_shapes=list(scratch),
        compiler_params=pltpu.CompilerParams(vmem_limit_bytes=int(limit * 2**20)),
        cost_estimate=pl.CostEstimate(flops=flops, bytes_accessed=2**20, transcendentals=flops // 512),
    )(*args)


def exchange(x, axis, groups=None):
    return lax.all_to_all(x, axis, 0, 0, axis_index_groups=groups, tiled=True)


def on_device(train_embed, train_label, target_embed, target_label, label_cost):
    m_dev, width = train_embed.shape
    n_dev = target_embed.shape[0]
    trains = lax.axis_size("train")
    targets = lax.axis_size("target")
    log_m = EPS * math.log(m_dev * trains)
    log_n = EPS * math.log(n_dev * targets)
    data = (
        train_embed,
        target_embed,
        train_label.reshape(1, m_dev),
        target_label.reshape(1, n_dev),
        label_cost,
    )
    row_m, row_n = (1, m_dev), (1, n_dev)
    tile_m, tile_n = (m_dev // 128, 128), (n_dev // 128, 128)
    flops = 2 * m_dev * n_dev * 512

    def run(body, outs, tile, *args):
        return call(body, outs, args, scratch=[pltpu.VMEM(tile, jnp.float32)], flops=flops)

    core = (lax.axis_index("target").astype(jnp.int32) & 1).reshape(1)
    wide_shape = (n_dev + 8, width)
    wide, local, sqx, sqy = call(
        rows_first,
        [wide_shape, (targets,) + tile_m, row_m, row_n],
        (*data, core),
        scratch=[pltpu.VMEM(tile_m, jnp.float32)]
        + [pltpu.VMEM(v.shape, v.dtype) for v in data]
        + [pltpu.VMEM(wide_shape, jnp.float32), pltpu.SemaphoreType.DMA((len(data) + 1,))],
        anywhere=range(len(data)),
        anywhere_out=(0,),
        smem=(len(data),),
        flops=flops,
        limit=54,
    )
    wide = lax.ppermute(wide, "target", [(k, k ^ 1) for k in range(targets)])
    got = exchange(local, "target")
    t, local, phi = run(
        functools.partial(columns_first, log_m), [(m_dev, n_dev), (trains,) + tile_n, row_m], tile_n, *data, got
    )
    got = exchange(local, "train")
    local, gamma = run(functools.partial(rows_next, log_n), [(targets,) + tile_m, row_n], tile_m, t, phi, got)
    got = exchange(local, "target")
    row_more = (1, n_dev + 128)
    local, phi = run(
        functools.partial(columns_next, log_m, log_n), [(2 * trains,) + row_more, row_m], row_more, t, phi, gamma, sqx, got
    )
    chips = [
        [a * targets + 2 * k + c for a in range(trains) for c in range(2)] for k in range(targets // 2)
    ]
    columns = exchange(local, ("train", "target"), chips)

    half = targets // 2
    got, gamma = call(
        functools.partial(project, log_n),
        [(half, CHUNK, 128), row_n],
        (t, train_embed, target_embed, data[2], label_cost, wide, phi, columns, core),
        scratch=[
            pltpu.VMEM((m_dev, 128), jnp.float32),
            pltpu.VMEM((m_dev, 128), jnp.float32),
            pltpu.VMEM((SHARE * half, width), jnp.bfloat16),
            pltpu.VMEM((SHARE * half, 128), jnp.bfloat16),
        ],
        smem=(8,),
        flops=flops,
    )
    got = exchange(got, "target", [[c + 2 * k for k in range(half)] for c in range(2)])
    barycentre, value, potential = call(
        functools.partial(finish, m_dev * trains - 1),
        [(SHARE, width), row_m, row_n],
        (got, phi, gamma, sqx, sqy, columns),
    )
    return (value.reshape(m_dev), potential.reshape(n_dev), barycentre)


def solution(mesh):
    return jax.shard_map(
        on_device,
        mesh=mesh,
        in_specs=(P("train", None), P("train"), P("target", None), P("target"), P()),
        out_specs=(P("train"), P("target"), P(("train", "target"), None)),
        check_vma=False,
    )
```

```python
import functools
import math

import jax
import jax.numpy as jnp
from jax import lax
from jax.experimental import pallas as pl
from jax.experimental.pallas import tpu as pltpu
from jax.sharding import PartitionSpec as P

EPS = 0.05
SCALE = 128.0
KAPPA = math.log2(math.e) / EPS / SCALE
LOG2 = math.log2(math.e) / EPS
LANES = 256
SHARE = 32
CHUNK = 2 * SHARE + 8


def pieces(v):
    hi = v.astype(jnp.bfloat16).astype(jnp.float32)
    rest = v - hi
    mid = rest.astype(jnp.bfloat16).astype(jnp.float32)
    lo = (rest - mid).astype(jnp.bfloat16).astype(jnp.float32)
    return hi, mid, lo


def tail(first, second):
    n = first[0].shape[1]
    row = lax.broadcasted_iota(jnp.int32, (8, n), 0)
    out = jnp.zeros((8, n), jnp.float32)
    for k, v in enumerate(first + second):
        out = jnp.where(row == k, v, out)
    return out


def ones_like3(v):
    return (jnp.ones_like(v),) * 3


def train_rows(label, phi):
    m = label.shape[1]
    onehot = (lax.broadcasted_iota(jnp.int32, (8, m), 0) == label).astype(jnp.float32)
    last = tail(ones_like3(phi), pieces(phi * SCALE))
    return jnp.concatenate([onehot, onehot, onehot, last], axis=0)


def target_rows(label, gamma, label_cost):
    n = label.shape[1]
    table = jnp.zeros((8, n), jnp.float32)
    for b in range(8):
        table = jnp.where(label == b, label_cost[:, b : b + 1], table)
    last = tail(pieces(gamma * SCALE), ones_like3(gamma))
    return jnp.concatenate(list(pieces(table * -SCALE)) + [last], axis=0)


def as_columns(rows):
    pad = jnp.zeros((96, rows.shape[1]), jnp.float32)
    return jnp.concatenate([rows, pad], axis=0).T.astype(jnp.bfloat16)


def as_rows(rows):
    pad = jnp.zeros((96, rows.shape[1]), jnp.float32)
    return jnp.concatenate([rows, pad], axis=0).astype(jnp.bfloat16)


def dot_nt(a, b):
    return lax.dot_general(a, b, (((1,), (1,)), ((), ())), preferred_element_type=jnp.float32)


def dot_nn(a, b):
    return lax.dot_general(a, b, (((1,), (0,)), ((), ())), preferred_element_type=jnp.float32)


def square_means(v):
    sums = jnp.sum(jnp.square(v.astype(jnp.float32)), axis=1, keepdims=True)
    return jnp.broadcast_to(sums * (1.0 / v.shape[1]), (v.shape[0], 128))


def to_everyone(v, out_ref):
    for k in range(out_ref.shape[0]):
        out_ref[k] = v


def in_lanes(v):
    return jnp.concatenate([v[k : k + 1] for k in range(v.shape[0])], axis=1)


def tree(parts, combine):
    while len(parts) > 1:
        parts = [combine(parts[k], parts[k + 1]) for k in range(0, len(parts), 2)]
    return parts[0]


def lse(parts):
    top = tree(parts, jnp.maximum)
    total = tree([jnp.exp((part - top) * (1.0 / EPS)) for part in parts], jnp.add)
    return top + EPS * jnp.log(total)


def lse_received(ref):
    return in_lanes(lse([ref[k] for k in range(ref.shape[0])]))


def sum_received(ref):
    return tree([ref[k] for k in range(ref.shape[0])], jnp.add)


def fetch(pairs, sems):
    copies = [pltpu.make_async_copy(src, dst, sems.at[k]) for k, (src, dst) in enumerate(pairs)]
    for copy in copies:
        copy.start()
    return copies


def wait_all(copies):
    for copy in copies:
        copy.wait()


def rows_first(
    x_any, y_any, lx_any, ly_any, lc_any, core_ref,
    wide_any, out_ref, sqx_ref, sqy_ref, at_ref, x_ref, y_ref, lx_ref, ly_ref, lc_ref, wide_ref, sems,
):
    pairs = [(ly_any, ly_ref), (lc_any, lc_ref), (lx_any, lx_ref), (y_any, y_ref), (x_any, x_ref)]
    copies = fetch(pairs, sems)
    wait_all(copies[:3])
    rows = as_rows(train_rows(lx_ref[...], jnp.zeros(lx_ref.shape, jnp.float32)))
    columns = as_columns(target_rows(ly_ref[...], jnp.zeros(ly_ref.shape, jnp.float32), lc_ref[...]))
    copies[3].wait()
    y = y_ref[...]
    n, width = y.shape
    wide_ref[0:n, :] = y.astype(jnp.float32)
    wide_ref[n : n + 8, :] = jnp.zeros((8, width), jnp.float32)
    label = ly_ref[...].astype(jnp.float32)
    for k in range(n // width):
        wide_ref[n + k : n + k + 1, :] = label[:, k * width : (k + 1) * width]
    wide = pltpu.make_async_copy(wide_ref, wide_any, sems.at[len(copies)])
    wide.start()
    copies[4].wait()
    means = square_means(y)
    norms = jnp.concatenate([means * SCALE] * (LANES // 128), axis=1)
    for k in range(x_ref.shape[0] // LANES):
        at = slice(k * LANES, (k + 1) * LANES)
        t = dot_nt(y, x_ref[at, :]) + dot_nn(columns, rows[:, at]) - norms
        top = jnp.max(t, axis=0, keepdims=True)
        total = jnp.sum(jnp.exp2((t - top) * KAPPA), axis=0, keepdims=True)
        out = top * (1.0 / SCALE) + EPS * jnp.log(total)
        for r in range(LANES // 128):
            row = k * (LANES // 128) + r
            at_ref[row : row + 1, :] = out[:, r * 128 : (r + 1) * 128]
    sqx_ref[...] = square_means(x_ref[...]).T[0:1]
    sqy_ref[...] = means.T[0:1]
    to_everyone(at_ref[...], out_ref)
    wide.wait()


def in_rows(v):
    return jnp.broadcast_to(v, (128, v.shape[1])).T


def columns_first(log_m, x_ref, y_ref, lx_ref, ly_ref, lc_ref, got_ref, t_ref, out_ref, phi_ref, at_ref):
    zero_m, zero_n = (jnp.zeros(ref.shape, jnp.float32) for ref in (lx_ref, ly_ref))
    phi = -log_m - lse_received(got_ref)
    phi_ref[...] = phi
    down = in_rows(phi * LOG2)
    down = jnp.concatenate([down] * (LANES // 128), axis=1)
    x = x_ref[...]
    columns = as_columns(train_rows(lx_ref[...], zero_m))
    rows = as_rows(target_rows(ly_ref[...], zero_n, lc_ref[...]))
    for k in range(y_ref.shape[0] // LANES):
        at = slice(k * LANES, (k + 1) * LANES)
        t = (dot_nt(x, y_ref[at, :]) + dot_nn(columns, rows[:, at])) * KAPPA
        t_ref[:, at] = t
        t = t + down
        top = jnp.max(t, axis=0, keepdims=True)
        total = jnp.sum(jnp.exp2(t - top), axis=0, keepdims=True)
        out = top * (1.0 / LOG2) + EPS * jnp.log(total)
        for r in range(LANES // 128):
            row = k * (LANES // 128) + r
            at_ref[row : row + 1, :] = out[:, r * 128 : (r + 1) * 128]
    to_everyone(at_ref[...], out_ref)


def rows_next(log_n, t_ref, phi_ref, got_ref, out_ref, gamma_ref, at_ref):
    gamma = -log_n - lse_received(got_ref)
    gamma_ref[...] = gamma
    down = in_rows((phi_ref[...] + log_n) * LOG2)
    across = gamma * LOG2
    for k in range(t_ref.shape[0] // 128):
        rows = slice(k * 128, (k + 1) * 128)
        total = 0.0
        for j in range(t_ref.shape[1] // 128):
            at = slice(j * 128, (j + 1) * 128)
            total = total + jnp.exp2(t_ref[rows, at] + down[rows] + across[:, at])
        at_ref[k : k + 1, :] = jnp.sum(total.T, axis=0, keepdims=True)
    to_everyone(at_ref[...], out_ref)


def columns_next(log_m, log_n, t_ref, phi_ref, gamma_ref, sqx_ref, got_ref, out_ref, new_ref, at_ref):
    n = t_ref.shape[1]
    phi = phi_ref[...] + log_n - log_m - EPS * jnp.log(in_lanes(sum_received(got_ref)))
    new_ref[...] = phi
    down = in_rows(phi * LOG2)
    across = (gamma_ref[...] + log_m) * LOG2
    for k in range(n // 128):
        at = slice(k * 128, (k + 1) * 128)
        at_ref[:, at] = jnp.sum(jnp.exp2(t_ref[:, at] + down + across[:, at]), axis=0, keepdims=True)
    at_ref[:, 0:n] = EPS * jnp.log(at_ref[:, 0:n]) - (gamma_ref[...] + log_m)
    dual_sum = jnp.sum(phi + sqx_ref[...], axis=1, keepdims=True)
    at_ref[:, n : n + 128] = jnp.broadcast_to(dual_sum, (1, 128))
    to_everyone(at_ref[...], out_ref)


def on_diagonal(v):
    shape = (SHARE, 128)
    row, column = (lax.broadcasted_iota(jnp.int32, shape, k) for k in range(2))
    axis = 0 if v.shape[0] == SHARE else 1
    return jnp.sum(jnp.where(row == column, v, 0.0), axis=axis, keepdims=True)


def project(
    log_n, t_ref, x_ref, y_ref, lx_ref, lc_ref, wide_ref, phi_ref, got_ref, core_ref,
    out_ref, gamma_ref, down_ref, aug_ref, xs_ref, xa_ref,
):
    core = core_ref[0]
    n, width = y_ref.shape
    half = got_ref.shape[0] // 2
    first, second = (-log_n - lse([got_ref[2 * k + p, :, 0:n] for k in range(half)]) for p in range(2))
    mine = jnp.where(core == 0, first, second)
    other = jnp.where(core == 0, second, first)
    gamma_ref[...] = mine
    across = mine * LOG2
    down_ref[...] = in_rows((phi_ref[...] + log_n) * LOG2)
    aug_ref[...] = as_columns(train_rows(lx_ref[...], jnp.zeros(lx_ref.shape, jnp.float32))).astype(jnp.float32)
    y = y_ref[...]
    y_other = wide_ref[0:n, :].astype(jnp.bfloat16)
    rows = as_rows(target_rows(in_lanes(wide_ref[n : n + n // width, :]), other, lc_ref[...]))
    chunks = out_ref.shape[0]
    per = min(4, chunks)
    for b in range(chunks // per):
        weights, downs = [], []
        for k in range(per):
            start = pl.multiple_of((2 * (b * per + k) + core) * SHARE, SHARE)
            at, to = pl.ds(start, SHARE), pl.ds((b * per + k) * SHARE, SHARE)
            xs_ref[to, :] = x_ref[at, :]
            xa_ref[to, :] = aug_ref[at, :].astype(jnp.bfloat16)
            downs.append(jnp.concatenate([down_ref[at, :]] * (n // 128), axis=1))
            weights.append(jnp.exp2(t_ref[at, :] + downs[k] + across).astype(jnp.bfloat16))
        w = jnp.concatenate(weights, axis=0)
        block = pl.ds(b * per * SHARE, per * SHARE)
        t = dot_nt(xs_ref[block, :], y_other) + dot_nn(xa_ref[block, :], rows)
        v = jnp.exp2(t * KAPPA + jnp.concatenate(downs, axis=0)).astype(jnp.bfloat16)
        denom = jnp.sum(w.astype(jnp.float32) + v.astype(jnp.float32), axis=1, keepdims=True)
        numer = dot_nn(w, y) + dot_nn(v, y_other)
        for k in range(per):
            part, chunk = slice(k * SHARE, (k + 1) * SHARE), b * per + k
            out_ref[chunk, 0:SHARE, :] = numer[part, 0:128]
            out_ref[chunk, SHARE : 2 * SHARE, :] = numer[part, 128:256]
            out_ref[chunk, 2 * SHARE : CHUNK, :] = jnp.broadcast_to(on_diagonal(denom[part]), (CHUNK - 2 * SHARE, 128))


def finish(others, got_ref, phi_ref, gamma_ref, sqx_ref, sqy_ref, columns_ref, out_ref, value_ref, potential_ref):
    total = sum_received(got_ref)
    denom = on_diagonal(total[2 * SHARE : 2 * SHARE + 1])
    out_ref[:, 0:128] = total[0:SHARE] / denom
    out_ref[:, 128:256] = total[SHARE : 2 * SHARE] / denom
    n = gamma_ref.shape[1]
    potential_ref[...] = gamma_ref[...] + sqy_ref[...]
    dual = phi_ref[...] + sqx_ref[...]
    dual_sum = tree([columns_ref[2 * k, :, n : n + 1] for k in range(columns_ref.shape[0] // 2)], jnp.add)
    value_ref[...] = dual - (dual_sum - dual) / others


def call(body, outs, args, scratch=(), smem=(), anywhere=(), anywhere_out=(), flops=0, limit=40):
    vmem = pl.BlockSpec(memory_space=pltpu.VMEM)
    specs = [vmem for _ in args]
    for k in smem:
        specs[k] = pl.BlockSpec(memory_space=pltpu.SMEM)
    for k in anywhere:
        specs[k] = pl.BlockSpec(memory_space=pl.ANY)
    out_specs = [pl.BlockSpec(memory_space=pl.ANY) if k in anywhere_out else vmem for k in range(len(outs))]
    outs = [s if hasattr(s, "dtype") else jax.ShapeDtypeStruct(s, jnp.float32) for s in outs]
    return pl.pallas_call(
        body,
        out_shape=outs,
        in_specs=specs,
        out_specs=out_specs,
        scratch_shapes=list(scratch),
        compiler_params=pltpu.CompilerParams(vmem_limit_bytes=int(limit * 2**20)),
        cost_estimate=pl.CostEstimate(flops=flops, bytes_accessed=2**20, transcendentals=flops // 512),
    )(*args)


def exchange(x, axis, groups=None):
    return lax.all_to_all(x, axis, 0, 0, axis_index_groups=groups, tiled=True)


def on_device(train_embed, train_label, target_embed, target_label, label_cost):
    m_dev, width = train_embed.shape
    n_dev = target_embed.shape[0]
    trains = lax.axis_size("train")
    targets = lax.axis_size("target")
    log_m = EPS * math.log(m_dev * trains)
    log_n = EPS * math.log(n_dev * targets)
    data = (
        train_embed,
        target_embed,
        train_label.reshape(1, m_dev),
        target_label.reshape(1, n_dev),
        label_cost,
    )
    row_m, row_n = (1, m_dev), (1, n_dev)
    tile_m, tile_n = (m_dev // 128, 128), (n_dev // 128, 128)
    flops = 2 * m_dev * n_dev * 512

    def run(body, outs, tile, *args):
        return call(body, outs, args, scratch=[pltpu.VMEM(tile, jnp.float32)], flops=flops)

    core = (lax.axis_index("target").astype(jnp.int32) & 1).reshape(1)
    wide_shape = (n_dev + 8, width)
    wide, local, sqx, sqy = call(
        rows_first,
        [wide_shape, (targets,) + tile_m, row_m, row_n],
        (*data, core),
        scratch=[pltpu.VMEM(tile_m, jnp.float32)]
        + [pltpu.VMEM(v.shape, v.dtype) for v in data]
        + [pltpu.VMEM(wide_shape, jnp.float32), pltpu.SemaphoreType.DMA((len(data) + 1,))],
        anywhere=range(len(data)),
        anywhere_out=(0,),
        smem=(len(data),),
        flops=flops,
        limit=54,
    )
    wide = lax.ppermute(wide, "target", [(k, k ^ 1) for k in range(targets)])
    got = exchange(local, "target")
    t, local, phi = run(
        functools.partial(columns_first, log_m), [(m_dev, n_dev), (trains,) + tile_n, row_m], tile_n, *data, got
    )
    got = exchange(local, "train")
    local, gamma = run(functools.partial(rows_next, log_n), [(targets,) + tile_m, row_n], tile_m, t, phi, got)
    got = exchange(local, "target")
    row_more = (1, n_dev + 128)
    local, phi = run(
        functools.partial(columns_next, log_m, log_n), [(2 * trains,) + row_more, row_m], row_more, t, phi, gamma, sqx, got
    )
    chips = [
        [a * targets + 2 * k + c for a in range(trains) for c in range(2)] for k in range(targets // 2)
    ]
    columns = exchange(local, ("train", "target"), chips)

    half = targets // 2
    got, gamma = call(
        functools.partial(project, log_n),
        [(half, CHUNK, 128), row_n],
        (t, train_embed, target_embed, data[2], label_cost, wide, phi, columns, core),
        scratch=[
            pltpu.VMEM((m_dev, 128), jnp.float32),
            pltpu.VMEM((m_dev, 128), jnp.float32),
            pltpu.VMEM((SHARE * half, width), jnp.bfloat16),
            pltpu.VMEM((SHARE * half, 128), jnp.bfloat16),
        ],
        smem=(8,),
        flops=flops,
    )
    got = exchange(got, "target", [[c + 2 * k for k in range(half)] for c in range(2)])
    barycentre, value, potential = call(
        functools.partial(finish, m_dev * trains - 1),
        [(SHARE, width), row_m, row_n],
        (got, phi, gamma, sqx, sqy, columns),
    )
    return (value.reshape(m_dev), potential.reshape(n_dev), barycentre)


def solution(mesh):
    return jax.shard_map(
        on_device,
        mesh=mesh,
        in_specs=(P("train", None), P("train"), P("target", None), P("target"), P()),
        out_specs=(P("train"), P("target"), P(("train", "target"), None)),
        check_vma=False,
    )
```
